32 devices in a mesh: copies: 2 (over y), nodes: 4 (over z), samples: 4 (over x, core).
Axes of the slice: x: 2, y: 2, z: 4, core: 2. Of those that a mesh axis runs over, the one named last changes fastest.
Arguments:
- vector: float32 [128, 16384], P('samples', ('copies', 'nodes')), parts along dimension 1, may hold values from -1500 to 1500
- operating: float32 [128, 16384], P('samples', ('copies', 'nodes')), parts along dimension 1, may hold values from -3.5 to 3.5
- table: float32 [16], replicated, may hold values from 0.2 to 2
- linear: float32 [8192], P('nodes'), may hold values from 0.5 to 2
- capacity: float32 [8192], P('nodes'), may hold values from 0.5 to 4
- weights: float32 [8, 8192], P(None, 'nodes'), may hold values from -2 to 2
- degree: int32 [8192], P('nodes'), may hold values from 1 to 8
- neighbours: int32 [8, 8192], P(None, 'nodes'), may hold values from 0 to 2111, as said below
- boundary: int32 [1024], P('nodes'), may hold values from 0 to 2047, as said below
- send_list: int32 [256], P('nodes'), may hold values from 0 to 255, as said below
Outputs:
- basis_two: float32 [128, 16384], P('samples', ('copies', 'nodes')), parts along dimension 1
- next_residue: float32 [128, 16384], P('samples', ('copies', 'nodes')), parts along dimension 1
The draws below stay inside these ranges and needn't reach their ends.
There are 2 independent parts, one for each index of `copies`. The reference program is written for one: setup_inputs(seed, part) draws one part's arguments, and reference() takes and returns one part's arrays. A program takes and returns all parts, laid end to end along the dimension named above; an argument that names none is the same for every part. Nothing has to cross between parts.
Inputs may be any that keep to these rules, and one draw needn't show every extreme that they name: `neighbours`: columns of node part r are nodes r * 2048 onward. An entry e below 2048 names local node e of the same part; otherwise e - 2048 = q * 16 + c names the c-th cut row that part q sends to part r, with q different from r and c below that pair's count of cut rows, a count of 1 to 16 that is 16 for some pair in every draw. Every cut row below its pair's count is named by slot 0 of some node. `boundary`: entries q * 256 to q * 256 + 255 are 256 different local node numbers of node part q. `send_list`: entry q * 4 * 16 + r * 16 + c is the position, in part q's boundary list, of the node that part q sends to part r as its c-th cut row.
All inputs are finite; a program needn't handle non-finite values.
Results may differ from the reference program's by a relative error of at most 0.0003.
Values sent between devices are 32-bit elements; how exact they have to be, the bound alone decides.
No kernel may reach another device: no remote copies, remote signals or barrier semaphores. Data moves between devices by JAX's collectives and lax.ppermute only.
A program may use at most 64 MiB of HBM per device.

```python
import math
import jax
import jax.numpy as jnp
from jax import lax

K = 128
M = 16
P_SIZE = 8
CAP = 16
NODE_DEV = 2048
BND = 256
NODES = 8192
N_NODES = 4


def cut_counts(key):
    key = jax.random.fold_in(key, 17)
    baseline_key, busy_key = jax.random.split(key)
    baseline = jax.random.randint(baseline_key, (N_NODES, N_NODES), CAP // 4 + 1, CAP + 1)
    busy_sender = jax.random.randint(busy_key, (N_NODES, 1), 0, 4) == 0
    counts = jnp.where(busy_sender, CAP, baseline)
    sender = jnp.arange(N_NODES, dtype=jnp.int32)[:, None]
    receiver = jnp.arange(N_NODES, dtype=jnp.int32)[None, :]
    counts = jnp.where(sender == (receiver + 1) % N_NODES, CAP, counts)
    return jnp.where(sender == receiver, 0, counts).astype(jnp.int32)


def draw_neighbours(key, part):
    key = jax.random.fold_in(key, 3)
    count_key, row_key = jax.random.split(key)
    counts = cut_counts(count_key)

    def one_part(receiver_part, part_key):
        local_key, far_key, peer_key, pick_key, order_key = jax.random.split(part_key, 5)
        local_entry = jax.random.randint(local_key, (P_SIZE, NODE_DEV), 0, NODE_DEV)
        far_entry = jax.random.randint(far_key, (P_SIZE, NODE_DEV), 0, 4) == 0
        peer_part = (receiver_part + jax.random.randint(peer_key, (P_SIZE, NODE_DEV), 1, N_NODES)) % N_NODES
        limit = counts[peer_part, receiver_part]
        cut_row = jax.random.randint(pick_key, (P_SIZE, NODE_DEV), 0, limit)
        entries = jnp.where(far_entry, NODE_DEV + peer_part * CAP + cut_row, local_entry)
        slot_ids = jnp.arange(N_NODES * CAP, dtype=jnp.int32)
        used = slot_ids % CAP < counts[slot_ids // CAP, receiver_part]
        ordering = jax.random.permutation(order_key, NODE_DEV)[:N_NODES * CAP]
        leading = entries[0]
        leading = leading.at[ordering].set(jnp.where(used, NODE_DEV + slot_ids, leading[ordering]))
        return entries.at[0].set(leading)
    part_keys = jax.random.split(row_key, N_NODES)
    per_part = jax.vmap(one_part)(jnp.arange(N_NODES, dtype=jnp.int32), part_keys)
    return jnp.transpose(per_part, (1, 0, 2)).reshape(P_SIZE, N_NODES * NODE_DEV).astype(jnp.int32)


def draw_boundary(key, part):
    key = jax.random.fold_in(key, 5)
    part_keys = jax.random.split(key, N_NODES)

    def pick_set(set_key):
        return jax.random.permutation(set_key, NODE_DEV)[:BND]
    chosen = jax.vmap(pick_set)(part_keys)
    parts = jnp.arange(N_NODES, dtype=jnp.int32)
    wanted = jnp.where(parts == 0, NODE_DEV - 1, jnp.where(parts == 1, 0, chosen[:, 0]))
    chosen = (chosen + (wanted - chosen[:, 0])[:, None]) % NODE_DEV
    return chosen.reshape(N_NODES * BND).astype(jnp.int32)


def draw_send_list(key, part):
    key = jax.random.fold_in(key, 7)
    return jax.random.randint(key, (N_NODES * N_NODES * CAP,), 0, BND).astype(jnp.int32)


def draw_vector(key, part):
    key = jax.random.fold_in(key, 9)
    base_key, node_key, harmonic_key = jax.random.split(key, 3)
    position = jnp.arange(NODES, dtype=jnp.float32)
    rising = jnp.exp(math.log(3.0) * position / NODES)
    node_scale = rising * jnp.exp(math.log(10.0) * jax.random.uniform(node_key, (NODES,)))
    harmonic_scale = jnp.exp(math.log(10.0) * jax.random.uniform(harmonic_key, (K, 1)))
    baseline = jnp.clip(jax.random.normal(base_key, (K, NODES)), -4.5, 4.5)
    values = harmonic_scale * node_scale[None, :] * baseline
    return values.astype(jnp.float32)


def touch_ends(drawn, own_key, low, largest):
    dims = drawn.shape
    spot = [jax.random.randint(jax.random.fold_in(own_key, axis), (), 0, dims[axis]) for axis in range(len(dims))]
    drawn = drawn.at[tuple(spot)].set(low)
    longest = dims.index(max(dims))
    spot[longest] = (spot[longest] + 1) % dims[longest]
    return drawn.at[tuple(spot)].set(largest)


def level_of(own_key, shape, pieces, low, top_value):
    def one(axis_at, blocks):
        draws = jax.random.uniform(jax.random.fold_in(jax.random.fold_in(own_key, 6), axis_at), (blocks,), jnp.float32, low / len(pieces), top_value / len(pieces))
        return jnp.repeat(jnp.exp(draws), shape[axis_at] // blocks).reshape((-1,) + (1,) * (len(shape) - axis_at - 1))

    gain = one(*pieces[0])
    for cut in pieces[1:]:
        gain = gain * one(*cut)
    return gain


def scatter_about(stream_key, extent, spread, bound, cuts=(), kind=jnp.bfloat16):
    values = jax.random.normal(stream_key, extent, jnp.float32) * spread
    if len(cuts) > 0:
        values = level_of(stream_key, extent, cuts, -0.22, 0.18) * values
    return jnp.clip(values, min=-bound, max=bound).astype(kind)


def setup_inputs(seed: int = 0, part: int = 0) -> dict:
    key_of = jax.random.split(jax.random.key(seed), 11)
    part_splits = jax.random.split(jax.random.fold_in(key_of[10], part), 11)
    vector = draw_vector(jax.random.fold_in(jax.random.fold_in(key_of[10], part), 71), part)
    operating = jnp.clip(jax.random.uniform(part_splits[1], (K, NODES), jnp.float32, -3.5, 3.5) * level_of(part_splits[1], (K, NODES), ((0, 4), (1, 4)), -0.4, 0.0), -3.5, 3.5)
    table = jnp.clip(jnp.exp(jax.random.uniform(key_of[2], (M,), jnp.float32, math.log(0.2), math.log(2.0))), 0.2, 2.0)
    linear = jnp.clip(jnp.exp(math.log(2.0) - 1.3862944 * jax.random.uniform(key_of[3], (NODES,), jnp.float32) ** level_of(key_of[3], (NODES,), ((0, 4),), -0.2, 0.2)), 0.5, 2.0)
    capacity = jnp.clip(jnp.exp(math.log(4.0) - 2.0794415 * jax.random.uniform(key_of[4], (NODES,), jnp.float32) ** level_of(key_of[4], (NODES,), ((0, 4),), -0.2, 0.2)), 0.5, 4.0)
    weights = scatter_about(key_of[5], (P_SIZE, NODES), P_SIZE ** -0.5, 2.0, ((1, 4),), jnp.float32)
    degree = touch_ends(jax.random.randint(key_of[6], (NODES,), 1, P_SIZE + 1), jax.random.fold_in(key_of[6], 1), 1, P_SIZE).astype(jnp.int32)
    neighbours = draw_neighbours(jax.random.fold_in(key_of[10], 71), part)
    boundary = draw_boundary(jax.random.fold_in(key_of[10], 71), part)
    send_list = draw_send_list(jax.random.fold_in(key_of[10], 71), part)
    return {"vector": vector, "operating": operating, "table": table, "linear": linear, "capacity": capacity, "weights": weights, "degree": degree, "neighbours": neighbours, "boundary": boundary, "send_list": send_list}


EPSILON = 1e-06

def spectral_tables(length):
    indices = jnp.arange(length, dtype=jnp.int32)
    frequency = jnp.where(indices == 1, length // 2, indices // 2)
    angles = (indices[:, None] * frequency[None, :] % length).astype(jnp.float32) * (2.0 * math.pi / length)
    cosine_column = (indices % 2 == 0) | (indices == 1)
    synthesis = jnp.where(cosine_column[None, :], jnp.cos(angles), jnp.sin(angles))
    factor = jnp.where(indices < 2, 1.0 / length, 2.0 / length).astype(jnp.float32)
    analysis = jnp.transpose(synthesis) * factor[:, None]
    return (synthesis, analysis)

def conductance(operating, table):
    points = table.shape[0]
    spacing = 8.0 / (points - 1)
    summed = jnp.zeros_like(operating)
    for knot_index in range(points):
        centre = -4.0 + spacing * knot_index
        summed = summed + table[knot_index] * jnp.maximum(0.0, 1.0 - jnp.abs(operating - centre) / spacing)
    return summed

def derivative(field_in, first_pair, half_order):
    rows_total = field_in.shape[0]
    paired = field_in.reshape(rows_total // 2, 2, field_in.shape[1])
    scaling = ((first_pair + jnp.arange(rows_total // 2, dtype=jnp.int32)).astype(jnp.float32) / half_order)[:, None]
    turned = jnp.stack([scaling * paired[:, 1], -scaling * paired[:, 0]], axis=1)
    return turned.reshape(field_in.shape)

def matmul_exact(first_array, second_array):
    return jnp.dot(first_array, second_array, precision=lax.Precision.HIGHEST, preferred_element_type=jnp.float32)

def source_nodes(neighbours, boundary, send_list):
    column = jnp.arange(NODES, dtype=jnp.int32)
    owner_part = (column // NODE_DEV)[None, :]
    remote = jnp.maximum(neighbours - NODE_DEV, 0)
    sender = remote // CAP
    cut_row = remote % CAP
    position = send_list[sender * (N_NODES * CAP) + owner_part * CAP + cut_row]
    target = sender * NODE_DEV + boundary[sender * BND + position]
    return jnp.where(neighbours < NODE_DEV, owner_part * NODE_DEV + neighbours, target).astype(jnp.int32)

def jacobian(field_in, conductances, linear, capacity, masked, sources, synthesis, analysis):
    waveform = matmul_exact(synthesis, field_in)
    current = conductances * waveform
    node_load = linear[None, :] * waveform + current
    for slot_index in range(P_SIZE):
        node_load = node_load + masked[slot_index][None, :] * current[:, sources[slot_index]]
    spectrum = matmul_exact(analysis, node_load)
    return spectrum + capacity[None, :] * derivative(field_in, 0, K // 2)

def reference(vector, operating, table, linear, capacity, weights, degree, neighbours, boundary, send_list):
    synthesis, analysis = spectral_tables(K)
    conductances = conductance(operating, table)
    sources = source_nodes(neighbours, boundary, send_list)
    masked = jnp.where(jnp.arange(P_SIZE, dtype=jnp.int32)[:, None] < degree[None, :], weights, 0.0)
    entries = float(K * NODES)

    def mean_product(first_array, second_array):
        return jnp.sum(first_array * second_array) / entries

    def apply_matvec(field_in):
        return jacobian(field_in, conductances, linear, capacity, masked, sources, synthesis, analysis)
    scale_norm = jnp.sqrt(mean_product(vector, vector) + EPSILON)
    basis_one = vector / scale_norm
    image_one = apply_matvec(basis_one)
    first_coeff = mean_product(basis_one, image_one)
    residue = image_one - first_coeff * basis_one
    second_norm = jnp.sqrt(mean_product(residue, residue) + EPSILON)
    basis_two = residue / second_norm
    image_two = apply_matvec(basis_two)
    along_one = mean_product(basis_one, image_two)
    along_two = mean_product(basis_two, image_two)
    return (basis_two, image_two - along_one * basis_one - along_two * basis_two)
```

```python
import functools
import math

import jax
import jax.numpy as jnp
import numpy as np
from jax import lax
from jax.experimental import pallas as pl
from jax.experimental.pallas import tpu as pltpu
from jax.sharding import PartitionSpec as P

CAP = 16
EPSILON = 1e-06
LANES = 128
BF16 = jnp.bfloat16
F32 = jnp.float32
I32 = jnp.int32


def spectral_tables(length):
    indices = np.arange(length)
    frequency = np.where(indices == 1, length // 2, indices // 2)
    angles = (indices[:, None] * frequency[None, :] % length) * (2.0 * math.pi / length)
    cosine_column = (indices % 2 == 0) | (indices == 1)
    synthesis = np.where(cosine_column[None, :], np.cos(angles), np.sin(angles))
    factor = np.where(indices < 2, 1.0 / length, 2.0 / length)
    analysis = synthesis.T * factor[:, None]
    turn = np.zeros((length, length))
    for pair in range(length // 2):
        turn[2 * pair, 2 * pair + 1] = pair / (length // 2)
        turn[2 * pair + 1, 2 * pair] = -pair / (length // 2)
    return synthesis, analysis, synthesis @ turn


def halves(table):
    high = table.astype(np.float32).astype(BF16)
    low = (table - high.astype(np.float64)).astype(np.float32).astype(BF16)
    return np.stack([high, low])


def piece_order(count):
    masks, bit = [0], count // 2
    while bit:
        masks = masks + [mask ^ bit for mask in masks]
        bit //= 2
    return masks


def transform_tables(length, parts):
    synthesis, analysis, slope = spectral_tables(length)
    rows = length // parts
    forward, back = [], []
    for place in range(parts):
        times = np.arange(place // 2 * 2 * rows, (place // 2 + 1) * 2 * rows)
        block = lambda owner: np.arange(owner * rows, (owner + 1) * rows)
        coefs = np.concatenate([block(place ^ mask) for mask in piece_order(parts)])
        forward.append(
            np.concatenate(
                [
                    synthesis[np.ix_(times, coefs)],
                    slope[np.ix_(times, coefs)],
                    analysis[np.ix_(coefs, times)].T,
                ]
            )
        )
        sent = np.concatenate(
            [block(place ^ (2 * group) ^ side) for group in range(parts // 2) for side in (0, 1)]
        )
        back.append(analysis[np.ix_(sent, times)])
    return (
        np.moveaxis(halves(np.stack(forward)), 0, 1),
        np.moveaxis(halves(np.stack(back)), 0, 1),
    )


def split(values):
    high = values.astype(BF16)
    return high, (values - high.astype(F32)).astype(BF16)


def dot(first, second):
    return jnp.dot(first, second, preferred_element_type=F32)


def dot_split(first, second):
    (first_high, first_low), (second_high, second_low) = first, second
    rows = first_high.shape[0]
    both = dot(jnp.concatenate([first_high, first_low], axis=0), second_high)
    return both[:rows] + both[rows:] + dot(first_high, second_low)


def lane_sums(values):
    blocks = values.shape[1] // LANES
    total = values[:, :LANES]
    for block in range(1, blocks):
        total = total + values[:, block * LANES : (block + 1) * LANES]
    return jnp.sum(total, axis=0, keepdims=True)


def half_of(side, half):
    return pl.ds(pl.multiple_of(side * half, LANES), half)


def gather_kernel(place, send_list, boundary, vector, operating, picked, cut):
    node_groups = send_list.shape[0] // CAP
    nodes, lanes = picked.shape
    part = place[1]
    lane = lax.broadcasted_iota(I32, (8, lanes), 1)

    def name(slot, found):
        target = lax.rem(part + slot // CAP + 1, node_groups)
        node = boundary[send_list[target * CAP + slot % CAP]]
        return jnp.where(lane == slot, node, found)

    cut_nodes = lax.fori_loop(
        0, (node_groups - 1) * CAP, name, jnp.full((8, lanes), -1, I32), unroll=8
    )
    hit = lax.broadcasted_iota(I32, (nodes, lanes), 0) == cut_nodes[:1]
    picked[...] = jnp.where(hit, 1.0, 0.0).astype(BF16)
    both = jnp.concatenate([vector[...], operating[...]], axis=0)
    high, rest = split(both)
    middle, low = split(both - high.astype(F32))
    rows = both.shape[0]
    found = dot(jnp.concatenate([high, middle, low], axis=0), picked[...])
    cut[...] = found[:rows] + (found[rows : 2 * rows] + found[2 * rows :])


def conductance(operating, table):
    points = table.shape[1]
    spread = jnp.concatenate([table, jnp.zeros((1, LANES - points), F32)], axis=1)
    spread = jnp.broadcast_to(spread, (operating.shape[0], LANES))
    pieces = []
    for block in range(operating.shape[1] // LANES):
        scaled = (operating[:, block * LANES : (block + 1) * LANES] + 4.0) * ((points - 1) / 8.0)
        knot = jnp.clip(jnp.floor(scaled), 0.0, points - 2.0)
        weight = scaled - knot
        place = knot.astype(I32)
        left = jnp.take_along_axis(spread, place, axis=1, mode="promise_in_bounds")
        right = jnp.take_along_axis(spread, place + 1, axis=1, mode="promise_in_bounds")
        pieces.append(left + weight * (right - left))
    return jnp.concatenate(pieces, axis=1)


def prepare_kernel(
    place,
    neighbours,
    weights,
    degree,
    own_operating,
    near_operating,
    table,
    coupling_high,
    coupling_low,
    conductances,
    entry_rows,
    weight_rows,
):
    slots, nodes = neighbours.shape
    half = coupling_high.shape[1]
    sources = coupling_high.shape[0]
    node_groups = place[2]
    side, part = place[0] % 2, place[1]
    rows = own_operating.shape[0]
    conductances[pl.ds(pl.multiple_of(side * rows, 8), rows), :] = conductance(
        own_operating[...], table[...]
    )
    conductances[pl.ds(pl.multiple_of((1 - side) * rows, 8), rows), :] = conductance(
        near_operating[...], table[...]
    )

    mine = half_of(side, half)
    entry = neighbours[:, mine]
    remote = entry - nodes
    distance = part - (remote >> 4)
    distance = jnp.where(distance < 0, distance + node_groups, distance)
    entry = jnp.where(remote < 0, entry, nodes + (distance - 1) * CAP + (remote & 15))
    live = lax.broadcasted_iota(I32, (slots, half), 0) < degree[:, mine]
    masked = jnp.where(live, weights[:, mine], 0.0)
    entries = [entry[slot : slot + 1] for slot in range(slots)]
    gains = [masked[slot : slot + 1] for slot in range(slots)]
    for slot in range(slots):
        for later in range(slot + 1, slots):
            same = entries[slot] == entries[later]
            gains[slot] = gains[slot] + jnp.where(same, gains[later], 0.0)
            entries[later] = jnp.where(same, -1, entries[later])
    for slot in range(slots):
        entry_rows[slot : slot + 1, :] = entries[slot]
        weight_rows[slot : slot + 1, :] = gains[slot]

    unroll = 4

    def columns(block, carry):
        lanes = pl.ds(pl.multiple_of(block * LANES, LANES), LANES)
        wide = (CAP, LANES)
        names = [
            jnp.broadcast_to(entry_rows[slot : slot + 1, lanes], wide).astype(jnp.int16)
            for slot in range(slots)
        ]
        parts = [
            split(jnp.broadcast_to(weight_rows[slot : slot + 1, lanes], wide))
            for slot in range(slots)
        ]

        def source_rows(step, row):
            for inner in range(unroll):
                high = jnp.zeros(wide, BF16)
                low = jnp.zeros(wide, BF16)
                for slot in range(slots):
                    hit = names[slot] == row
                    high = jnp.where(hit, parts[slot][0], high)
                    low = jnp.where(hit, parts[slot][1], low)
                at = pl.ds(pl.multiple_of((step * unroll + inner) * 16, 16), 16)
                coupling_high[at, lanes] = high
                coupling_low[at, lanes] = low
                row = row + jnp.int16(16)
            return row

        lax.fori_loop(
            0,
            sources // 16 // unroll,
            source_rows,
            lax.broadcasted_iota(I32, wide, 0).astype(jnp.int16),
        )
        return carry

    lax.fori_loop(0, half // LANES, columns, 0)


def couple(load, current, halo_current, coupling_high, coupling_low):
    nodes = current.shape[1]
    high, low = split(current)
    halo_high, halo_low = split(halo_current)
    rows = high.shape[0]
    stacked = jnp.concatenate([high, low], axis=0)
    halo_stacked = jnp.concatenate([halo_high, halo_low], axis=0)
    width = 256
    for block in range(load.shape[1] // width):
        lanes = slice(block * width, (block + 1) * width)
        both = dot(stacked, coupling_high[:nodes, lanes]) + dot(
            halo_stacked, coupling_high[nodes:, lanes]
        )
        third = dot(high, coupling_low[:nodes, lanes]) + dot(
            halo_high, coupling_low[nodes:, lanes]
        )
        load[:, lanes] = load[:, lanes] + (both[:rows] + both[rows:] + third)


def signed_sums(values):
    even = lax.broadcasted_iota(I32, values.shape, 0) % 2 == 0
    return (
        jnp.sum(values, axis=0, keepdims=True),
        jnp.sum(jnp.where(even, values, -values), axis=0, keepdims=True),
    )


def first_kernel(*refs, pieces):
    place = refs[0]
    vectors = refs[1 : 1 + pieces]
    halos = refs[1 + pieces : 1 + 2 * pieces]
    (
        forward,
        back,
        conductances,
        coupling_high,
        coupling_low,
        linear,
        capacity,
        table,
        picked,
        image,
        load,
        wave,
        dual,
        halo_conductances,
        kept,
        sent,
        cut,
        sums,
        scalars,
        field_high,
        field_low,
    ) = refs[1 + 2 * pieces :]
    rows, nodes = vectors[0].shape
    half = load.shape[1]
    times = load.shape[0]
    side = place[0] % 2
    mine = half_of(side, half)
    for index in range(pieces):
        at = slice(index * rows, (index + 1) * rows)
        field_high[at, :nodes], field_low[at, :nodes] = split(vectors[index][...])
        field_high[at, nodes:], field_low[at, nodes:] = split(halos[index][:rows])
    near = piece_order(pieces).index(1)
    halo_conductances[pl.ds(pl.multiple_of(side * rows, 8), rows), :] = conductance(
        halos[0][rows:], table[...]
    )
    halo_conductances[pl.ds(pl.multiple_of((1 - side) * rows, 8), rows), :] = conductance(
        halos[near][rows:], table[...]
    )
    waveform = dot_split(
        (forward[0, :times], forward[1, :times]), (field_high[...], field_low[...])
    )
    others = dot_split(
        (forward[0, times:], forward[1, times:]), (field_high[:, mine], field_low[:, mine])
    )
    current = conductances[...] * waveform[:, :nodes]
    halo_current = halo_conductances[...] * waveform[:, nodes:]
    wave[...] = jnp.where(side == 0, waveform[:, :half], waveform[:, half:nodes])
    dual[...] = others[times:]
    load[...] = wave[...] * (linear[:, mine] + conductances[:, mine])
    couple(load, current, halo_current, coupling_high, coupling_low)
    answer = load[...] + capacity[:, mine] * others[:times]
    image[...] = answer
    halves_of_answer = split(answer)
    spectrum = dot_split((back[0], back[1]), halves_of_answer)
    kept[...] = spectrum[:times]
    sent[...] = spectrum[times:]
    cut[...] = pick(answer, picked[mine, :])
    lines = [*signed_sums(answer), *signed_sums(wave[...])]
    sums[...] = jnp.concatenate(lines + [jnp.zeros((4, half), F32)], axis=0)
    own = vectors[0][...]
    products = [lane_sums(own * own), lane_sums(dual[...] * answer)]
    scalars[...] = jnp.concatenate(products + [jnp.zeros((6, LANES), F32)], axis=0)


def pick(values, picked):
    high, rest = split(values)
    middle, low = split(values - high.astype(F32))
    rows = values.shape[0]
    found = dot(jnp.concatenate([high, middle, low], axis=0), picked)
    return found[:rows] + (found[rows : 2 * rows] + found[2 * rows :])


def second_kernel(
    place,
    image,
    near_image,
    halo,
    back,
    conductances,
    halo_conductances,
    coupling_high,
    coupling_low,
    linear,
    load,
    kept,
    sent,
    current,
):
    half = image.shape[1]
    times = image.shape[0]
    side = place[0] % 2
    mine, other = half_of(side, half), half_of(1 - side, half)
    current[:, mine] = conductances[:, mine] * image[...]
    current[:, other] = conductances[:, other] * near_image[...]
    load[...] = image[...] * (linear[:, mine] + conductances[:, mine])
    couple(load, current[...], halo_conductances[...] * halo[...], coupling_high, coupling_low)
    spectrum = dot_split((back[0], back[1]), split(load[...]))
    kept[...] = spectrum[:times]
    sent[...] = spectrum[times:]


def turned(field, first_pair, half_order):
    count = field.shape[0]
    row = lax.broadcasted_iota(I32, field.shape, 0)
    scaling = (first_pair + row // 2).astype(F32) * (1.0 / half_order)
    above = pltpu.roll(field, count - 1, 0)
    below = pltpu.roll(field, 1, 0)
    return scaling * jnp.where(row % 2 == 0, above, -below)


def norms(first_sums, entries):
    squares = jnp.sum(first_sums[0:1, :], axis=1, keepdims=True)
    cross = jnp.sum(first_sums[1:2, :], axis=1, keepdims=True)
    scale_square = squares / entries + EPSILON
    return scale_square, cross / entries / scale_square


def join(target, side, own, near):
    half = own.shape[1]
    target[:, half_of(side, half)] = own
    target[:, half_of(1 - side, half)] = near


def products_kernel(
    place,
    totals,
    vector,
    own_image,
    near_image,
    capacity,
    load,
    second_load,
    image,
    wave,
    dual,
    sums,
    residue,
    base,
    scalars,
    *,
    length,
    entries,
):
    side = place[0] % 2
    rows = vector.shape[0]
    first_pair = place[0] * (rows // 2)
    _, coeff = norms(totals[...], entries)
    join(residue, side, own_image[...], near_image[...])
    field = residue[...]
    base[...] = capacity[...] * turned(field, first_pair, length // 2) - coeff * field
    field = field - coeff * vector[...]
    residue[...] = field
    slope = capacity[...] * turned(field, first_pair, length // 2)
    change = second_load[...] - coeff * load[...]
    rest = image[...] - coeff * wave[...]
    changes = signed_sums(change)
    rests = [sums[line : line + 1] - coeff * sums[2 + line : 3 + line] for line in (0, 1)]
    ends = rests[0] * changes[0] + rests[1] * changes[1]
    products = [
        lane_sums(field * field),
        lane_sums(dual[...] * change) + lane_sums(vector[...] * slope),
        lane_sums(rest * change) * (2.0 / length)
        - lane_sums(ends) * (1.0 / length / length)
        + lane_sums(field * slope),
    ]
    scalars[...] = jnp.concatenate(products + [jnp.zeros((5, LANES), F32)], axis=0)


def last_kernel(
    place,
    first_totals,
    last_totals,
    vector,
    residue,
    base,
    own_part,
    near_part,
    basis_two,
    next_residue,
    *,
    entries,
):
    side = place[0] % 2
    scale_square, _ = norms(first_totals[...], entries)
    sums = [jnp.sum(last_totals[line : line + 1, :], axis=1, keepdims=True) for line in range(3)]
    second_norm = jnp.sqrt(sums[0] / entries / scale_square + EPSILON)
    scale = jnp.sqrt(scale_square)
    inverse = 1.0 / (second_norm * scale)
    along_one = sums[1] / entries * inverse / scale
    along_two = sums[2] / entries * inverse * inverse
    join(next_residue, side, own_part[...], near_part[...])
    second = residue[...] * inverse
    basis_two[...] = second
    next_residue[...] = (
        (next_residue[...] + base[...]) * inverse
        - (along_one / scale) * vector[...]
        - along_two * second
    )


VMEM = pl.BlockSpec(memory_space=pltpu.VMEM)
SMEM = pl.BlockSpec(memory_space=pltpu.SMEM)


def run(kernel, name, operands, outs, scratch=(), scalars=1, flops=0, moved=0):
    pinned = [pltpu.VMEM(shape, dtype) for shape, dtype in outs]
    return pl.pallas_call(
        kernel,
        out_shape=pinned,
        in_specs=[SMEM] * scalars + [VMEM] * (len(operands) - scalars),
        out_specs=[VMEM] * len(outs),
        scratch_shapes=[pltpu.VMEM(shape, dtype) for shape, dtype in scratch],
        compiler_params=pltpu.CompilerParams(vmem_limit_bytes=40 * 2**20),
        cost_estimate=pl.CostEstimate(flops=flops, bytes_accessed=moved, transcendentals=0),
        name=name,
    )(*operands)


def swap(value, mask):
    count = lax.axis_size("samples")
    return lax.ppermute(value, "samples", [(at, at ^ mask) for at in range(count)])


def total(value):
    for axis in ("samples", "nodes"):
        count, stride = lax.axis_size(axis), 1
        while stride < count:
            radix = 4 if count // stride % 4 == 0 else 2
            others = [
                lax.ppermute(value, axis, [(at, at ^ (step * stride)) for at in range(count)])
                for step in range(1, radix)
            ]
            value = value + functools.reduce(jnp.add, others)
            stride *= radix
    return value


def reduce_groups(kept, sent):
    times = kept.shape[0]
    count = lax.axis_size("samples") // 2
    blocks = {0: kept}
    for group in range(1, count):
        blocks[group] = sent[(group - 1) * times : group * times]
    bit = count // 2
    while bit:
        for group in [name for name in blocks if name & bit]:
            blocks[group ^ bit] = blocks[group ^ bit] + swap(blocks.pop(group), 2 * bit)
        bit //= 2
    return blocks[0]


def shards(
    vector, operating, table, linear, capacity, weights, degree, neighbours, boundary, send_list
):
    rows, nodes = vector.shape
    parts, node_groups = lax.axis_size("samples"), lax.axis_size("nodes")
    length, half, times = rows * parts, nodes // 2, 2 * rows
    entries = float(length * nodes * node_groups)
    lanes = -(-(node_groups - 1) * CAP // LANES) * LANES
    sources = nodes + lanes
    order = piece_order(parts)
    own_place = lax.axis_index("samples")
    place = jnp.stack([own_place, lax.axis_index("nodes"), jnp.int32(node_groups)]).astype(I32)
    forward, back = (
        lax.dynamic_index_in_dim(jnp.asarray(stack), own_place, keepdims=False)
        for stack in transform_tables(length, parts)
    )
    linear, capacity, degree, table = (
        value.reshape(1, -1) for value in (linear, capacity, degree, table)
    )
    distance = (jnp.arange(lanes, dtype=I32) // CAP + 1)[None, :]

    def from_parts(value, sides):
        found = jnp.zeros_like(value)
        for step in range(1, node_groups):
            arrived = [
                lax.ppermute(
                    value,
                    ("nodes", "samples"),
                    [
                        (at * parts + which, (at + step) % node_groups * parts + (which ^ side))
                        for at in range(node_groups)
                        for which in range(parts)
                    ],
                )
                for side in range(sides)
            ]
            found = jnp.where(distance == step, functools.reduce(jnp.add, arrived), found)
        return found

    vectors, bit = [vector], parts // 2
    while bit:
        vectors = vectors + [swap(piece, bit) for piece in vectors]
        bit //= 2
    near_operating = swap(operating, 1)

    picked, cut = run(
        gather_kernel,
        "gather",
        (place, send_list, boundary, vector, operating),
        [((nodes, lanes), BF16), ((times, lanes), F32)],
        scalars=3,
    )
    halo = from_parts(cut, 1)
    halos = [halo if mask == 0 else swap(halo, mask) for mask in order]

    coupling_high, coupling_low, conductances = run(
        prepare_kernel,
        "prepare",
        (place, neighbours, weights, degree, operating, near_operating, table),
        [((sources, half), BF16), ((sources, half), BF16), ((times, nodes), F32)],
        scratch=[((weights.shape[0], half), I32), ((weights.shape[0], half), F32)],
    )

    wide = ((times, half), F32)
    rest = max(length - times, 8)
    image, load, wave, dual, halo_conductances, kept, sent, cut, sums, scalars = run(
        functools.partial(first_kernel, pieces=parts),
        "first",
        (place, *vectors, *halos, forward, back, conductances, coupling_high, coupling_low)
        + (linear, capacity, table, picked),
        [wide, wide, wide, wide, ((times, lanes), F32), wide, ((rest, half), F32)]
        + [((times, lanes), F32), ((8, half), F32), ((8, LANES), F32)],
        scratch=[((length, sources), BF16)] * 2,
    )
    near_image = swap(image, 1)
    halo = from_parts(cut, 2)
    first_totals = total(scalars)
    bit = 2
    while bit < parts:
        sums = sums + swap(sums, bit)
        bit *= 2
    spectrum = reduce_groups(kept, sent)
    own_coefs, near_coefs = spectrum[:rows], swap(spectrum[rows:], 1)

    second_load, kept, sent = run(
        second_kernel,
        "second",
        (place, image, near_image, halo, back, conductances, halo_conductances)
        + (coupling_high, coupling_low, linear),
        [wide, wide, ((rest, half), F32)],
        scratch=[((times, nodes), F32)],
    )
    residue, base, scalars = run(
        functools.partial(products_kernel, length=length, entries=entries),
        "products",
        (place, first_totals, vector, own_coefs, near_coefs, capacity)
        + (load, second_load, image, wave, dual, sums),
        [((rows, nodes), F32), ((rows, nodes), F32), ((8, LANES), F32)],
    )
    last_totals = total(scalars)
    spectrum = reduce_groups(kept, sent)
    own_part, near_part = spectrum[:rows], swap(spectrum[rows:], 1)
    field = jax.ShapeDtypeStruct((rows, nodes), F32)
    return tuple(
        pl.pallas_call(
            functools.partial(last_kernel, entries=entries),
            out_shape=[field, field],
            in_specs=[SMEM] + [VMEM] * 7,
            out_specs=[VMEM] * 2,
            name="last",
        )(place, first_totals, last_totals, vector, residue, base, own_part, near_part)
    )


def solution(mesh):
    return jax.shard_map(
        shards,
        mesh=mesh,
        in_specs=(
            P("samples", ("copies", "nodes")),
            P("samples", ("copies", "nodes")),
            P(),
            P("nodes"),
            P("nodes"),
            P(None, "nodes"),
            P("nodes"),
            P(None, "nodes"),
            P("nodes"),
            P("nodes"),
        ),
        out_specs=(P("samples", ("copies", "nodes")), P("samples", ("copies", "nodes"))),
        check_vma=False,
    )
```

```python
import functools
import math

import jax
import jax.numpy as jnp
import numpy as np
from jax import lax
from jax.experimental import pallas as pl
from jax.experimental.pallas import tpu as pltpu
from jax.sharding import PartitionSpec as P

CAP = 16
EPSILON = 1e-06
LANES = 128
BF16 = jnp.bfloat16
F32 = jnp.float32
I32 = jnp.int32


def spectral_tables(length):
    indices = np.arange(length)
    frequency = np.where(indices == 1, length // 2, indices // 2)
    angles = (indices[:, None] * frequency[None, :] % length) * (2.0 * math.pi / length)
    cosine_column = (indices % 2 == 0) | (indices == 1)
    synthesis = np.where(cosine_column[None, :], np.cos(angles), np.sin(angles))
    factor = np.where(indices < 2, 1.0 / length, 2.0 / length)
    analysis = synthesis.T * factor[:, None]
    turn = np.zeros((length, length))
    for pair in range(length // 2):
        turn[2 * pair, 2 * pair + 1] = pair / (length // 2)
        turn[2 * pair + 1, 2 * pair] = -pair / (length // 2)
    return synthesis, analysis, synthesis @ turn


def halves(table):
    high = table.astype(np.float32).astype(BF16)
    low = (table - high.astype(np.float64)).astype(np.float32).astype(BF16)
    return np.stack([high, low])


def piece_order(count):
    masks, bit = [0], count // 2
    while bit:
        masks = masks + [mask ^ bit for mask in masks]
        bit //= 2
    return masks


def transform_tables(length, parts):
    synthesis, analysis, slope = spectral_tables(length)
    rows = length // parts
    forward, back = [], []
    for place in range(parts):
        times = np.arange(place // 2 * 2 * rows, (place // 2 + 1) * 2 * rows)
        block = lambda owner: np.arange(owner * rows, (owner + 1) * rows)
        coefs = np.concatenate([block(place ^ mask) for mask in piece_order(parts)])
        forward.append(
            np.concatenate(
                [
                    synthesis[np.ix_(times, coefs)],
                    slope[np.ix_(times, coefs)],
                    analysis[np.ix_(coefs, times)].T,
                ]
            )
        )
        sent = np.concatenate(
            [block(place ^ (2 * group) ^ side) for group in range(parts // 2) for side in (0, 1)]
        )
        back.append(analysis[np.ix_(sent, times)])
    return (
        np.moveaxis(halves(np.stack(forward)), 0, 1),
        np.moveaxis(halves(np.stack(back)), 0, 1),
    )


def split(values):
    high = values.astype(BF16)
    return high, (values - high.astype(F32)).astype(BF16)


def dot(first, second):
    return jnp.dot(first, second, preferred_element_type=F32)


def dot_split(first, second):
    (first_high, first_low), (second_high, second_low) = first, second
    rows = first_high.shape[0]
    both = dot(jnp.concatenate([first_high, first_low], axis=0), second_high)
    return both[:rows] + both[rows:] + dot(first_high, second_low)


def lane_sums(values):
    blocks = values.shape[1] // LANES
    total = values[:, :LANES]
    for block in range(1, blocks):
        total = total + values[:, block * LANES : (block + 1) * LANES]
    return jnp.sum(total, axis=0, keepdims=True)


def half_of(side, half):
    return pl.ds(pl.multiple_of(side * half, LANES), half)


def scalar_sum(values):
    return jnp.sum(lane_sums(values), axis=1, keepdims=True)


def pick(values, picked):
    high, _ = split(values)
    middle, low = split(values - high.astype(F32))
    rows = values.shape[0]
    found = dot(jnp.concatenate([high, middle, low], axis=0), picked)
    return found[:rows] + (found[rows : 2 * rows] + found[2 * rows :])


def conductance(operating, table):
    points = table.shape[1]
    spread = jnp.concatenate([table, jnp.zeros((1, LANES - points), F32)], axis=1)
    spread = jnp.broadcast_to(spread, (operating.shape[0], LANES))
    pieces = []
    for block in range(operating.shape[1] // LANES):
        scaled = (operating[:, block * LANES : (block + 1) * LANES] + 4.0) * ((points - 1) / 8.0)
        knot = jnp.clip(jnp.floor(scaled), 0.0, points - 2.0)
        weight = scaled - knot
        place = knot.astype(I32)
        left = jnp.take_along_axis(spread, place, axis=1, mode="promise_in_bounds")
        right = jnp.take_along_axis(spread, place + 1, axis=1, mode="promise_in_bounds")
        pieces.append(left + weight * (right - left))
    return jnp.concatenate(pieces, axis=1)


def prepare_kernel(
    place,
    send_list,
    boundary,
    near_operating_in,
    operating_in,
    neighbours_in,
    weights_in,
    degree_in,
    linear_in,
    capacity_in,
    table_in,
    vector_in,
    forward_in,
    back_in,
    coupling_high,
    coupling_low,
    conductances,
    picked,
    linear,
    capacity,
    capacity_all,
    cut_halo,
    vector,
    forward,
    back,
    near_operating,
    operating,
    neighbours,
    weights,
    degree,
    linear_all,
    table,
    entry_rows,
    weight_rows,
    copied,
):
    slots, nodes = neighbours.shape
    sources, width = coupling_high.shape
    lanes = picked.shape[1]
    half = width - lanes
    node_groups = send_list.shape[0] // CAP
    side, part = place[0] % 2, place[1]
    rows = operating.shape[0]
    copies = [
        pltpu.make_async_copy(source, target, copied.at[index])
        for index, (source, target) in enumerate(
            [
                (neighbours_in, neighbours),
                (weights_in, weights),
                (degree_in, degree),
                (linear_in, linear_all),
                (capacity_in, capacity_all),
                (table_in, table),
                (operating_in, operating),
                (near_operating_in, near_operating),
                (vector_in, vector),
                (forward_in.at[place[0]], forward),
                (back_in.at[place[0]], back),
            ]
        )
    ]
    for copy in copies:
        copy.start()

    lane = lax.broadcasted_iota(I32, (8, lanes), 1)

    def name(slot, found):
        target = lax.rem(part + slot // CAP + 1, node_groups)
        node = boundary[send_list[target * CAP + slot % CAP]]
        return jnp.where(lane == slot, node, found)

    cut_nodes = lax.fori_loop(
        0, (node_groups - 1) * CAP, name, jnp.full((8, lanes), -1, I32), unroll=8
    )
    hit = lax.broadcasted_iota(I32, (nodes, lanes), 0) == cut_nodes[:1]
    picked[...] = jnp.where(hit, 1.0, 0.0).astype(BF16)

    for copy in copies[:6]:
        copy.wait()
    mine = half_of(side, half)
    entry = neighbours[...]
    remote = entry - nodes
    distance = part - (remote >> 4)
    distance = jnp.where(distance < 0, distance + node_groups, distance)
    entry = jnp.where(remote < 0, entry, nodes + (distance - 1) * CAP + (remote & 15))
    live = lax.broadcasted_iota(I32, (slots, nodes), 0) < degree[...]
    neighbours[...] = entry
    weights[...] = jnp.where(live, weights[...], 0.0)
    columns = jnp.concatenate(
        [
            entry.astype(F32),
            weights[...],
            linear_all[...],
            capacity_all[...],
            jnp.zeros((6, nodes), F32),
        ],
        axis=0,
    )
    at_cut = pick(columns, picked[...])
    linear[:, :half] = linear_all[:, mine]
    linear[:, half:] = at_cut[2 * slots : 2 * slots + 1]
    capacity[:, :half] = capacity_all[:, mine]
    capacity[:, half:] = at_cut[2 * slots + 1 : 2 * slots + 2]
    entry_rows[:, :half] = neighbours[:, mine]
    entry_rows[:, half:] = at_cut[:slots].astype(I32)
    weight_rows[:, :half] = weights[:, mine]
    weight_rows[:, half:] = at_cut[slots : 2 * slots]
    entries = [entry_rows[slot : slot + 1, :] for slot in range(slots)]
    gains = [weight_rows[slot : slot + 1, :] for slot in range(slots)]
    for slot in range(slots):
        for later in range(slot + 1, slots):
            same = entries[slot] == entries[later]
            gains[slot] = gains[slot] + jnp.where(same, gains[later], 0.0)
            entries[later] = jnp.where(same, -1, entries[later])
    for slot in range(slots):
        entry_rows[slot : slot + 1, :] = entries[slot]
        weight_rows[slot : slot + 1, :] = gains[slot]

    unroll = 4

    def column_block(block, carry):
        at_lanes = pl.ds(pl.multiple_of(block * LANES, LANES), LANES)
        wide = (CAP, LANES)
        names = [
            jnp.broadcast_to(entry_rows[slot : slot + 1, at_lanes], wide).astype(jnp.int16)
            for slot in range(slots)
        ]
        parts = [
            split(jnp.broadcast_to(weight_rows[slot : slot + 1, at_lanes], wide))
            for slot in range(slots)
        ]

        def source_rows(step, row):
            for inner in range(unroll):
                high = jnp.zeros(wide, BF16)
                low = jnp.zeros(wide, BF16)
                for slot in range(slots):
                    hit = names[slot] == row
                    high = jnp.where(hit, parts[slot][0], high)
                    low = jnp.where(hit, parts[slot][1], low)
                at = pl.ds(pl.multiple_of((step * unroll + inner) * 16, 16), 16)
                coupling_high[at, at_lanes] = high
                coupling_low[at, at_lanes] = low
                row = row + jnp.int16(16)
            return row

        lax.fori_loop(
            0,
            sources // 16 // unroll,
            source_rows,
            lax.broadcasted_iota(I32, wide, 0).astype(jnp.int16),
        )
        return carry

    lax.fori_loop(0, width // LANES, column_block, 0)
    cut_halo[...] = jnp.transpose(
        coupling_high[nodes:, half:].astype(F32) + coupling_low[nodes:, half:].astype(F32)
    )

    for copy in copies[6:]:
        copy.wait()
    conductances[pl.ds(pl.multiple_of(side * rows, 8), rows), :nodes] = conductance(
        operating[...], table[...]
    )
    conductances[pl.ds(pl.multiple_of((1 - side) * rows, 8), rows), :nodes] = conductance(
        near_operating[...], table[...]
    )
    conductances[:, nodes:] = pick(conductances[:, :nodes], picked[...])


def coupled(high, stacked, coupling_high, coupling_low, sources, lanes):
    rows = high.shape[0]
    both = dot(stacked, coupling_high[sources, lanes])
    return both[:rows] + both[rows:] + dot(high, coupling_low[sources, lanes])


def packet_layout(steps, times):
    shared = steps * CAP <= LANES
    return shared, times if shared else 0


def wave_kernel(*refs, pieces):
    vectors = refs[:pieces]
    (
        forward,
        conductances,
        picked,
        coupling_high,
        coupling_low,
        linear,
        capacity,
        cut_halo,
        field_high,
        field_low,
        wave,
        current,
        cut_current,
    ) = refs[pieces : pieces + 13]
    sent = refs[pieces + 13 :]
    rows, nodes = vectors[0].shape
    lanes = picked.shape[1]
    times = wave.shape[0]
    half = linear.shape[1] - lanes
    for index in range(pieces):
        at = slice(index * rows, (index + 1) * rows)
        field_high[at, :nodes], field_low[at, :nodes] = split(vectors[index][...])
    field_high[:, nodes:] = dot(field_high[:, :nodes], picked[...]).astype(BF16)
    field_low[:, nodes:] = dot(field_low[:, :nodes], picked[...]).astype(BF16)
    wave[...] = dot_split(
        (forward[0, :times], forward[1, :times]), (field_high[...], field_low[...])
    )
    slope = dot_split(
        (forward[0, times : 2 * times], forward[1, times : 2 * times]),
        (field_high[:, nodes:], field_low[:, nodes:]),
    )
    high, low = split(conductances[:, :nodes] * wave[:, :nodes])
    current[:times] = high
    current[times:] = low
    at_cut = conductances[:, nodes:] * wave[:, nodes:]
    cut_current[...] = jnp.transpose(at_cut)
    image = (
        linear[:, half:] * wave[:, nodes:]
        + at_cut
        + capacity[:, half:] * slope
        + coupled(
            high, current[...], coupling_high, coupling_low, slice(0, nodes), slice(half, None)
        )
    )
    image = jnp.transpose(image)
    at_cut = jnp.transpose(conductances[:, nodes:])
    slots = len(sent) * CAP
    shared, start = packet_layout(len(sent), times)
    for step, target in enumerate(sent):
        at = slice(step * CAP, (step + 1) * CAP)
        target[...] = jnp.zeros(target.shape, F32)
        if shared:
            target[:slots, :times] = cut_current[:slots]
        target[:CAP, start : start + slots] = cut_halo[at, :slots]
        target[CAP : 2 * CAP, start : start + times] = image[at]
        target[2 * CAP : 3 * CAP, start : start + times] = at_cut[at]


def local_kernel(
    field_high,
    field_low,
    forward,
    wave,
    current,
    conductances,
    coupling_high,
    coupling_low,
    linear,
    capacity,
    place,
    load,
    slope,
    own_wave,
    dual,
):
    times, half = load.shape
    sources = slice(0, current.shape[1])
    mine = half_of(place[0] % 2, half)
    others = dot_split(
        (forward[0, times:], forward[1, times:]), (field_high[:, mine], field_low[:, mine])
    )
    slope[...] = capacity[:, :half] * others[:times]
    dual[...] = others[times:]
    own_wave[...] = wave[:, mine]
    load[...] = own_wave[...] * (linear[:, :half] + conductances[:, mine])
    high = current[:times]
    step = 256
    for block in range(half // step):
        lanes = slice(block * step, (block + 1) * step)
        load[:, lanes] += coupled(
            high, current[...], coupling_high, coupling_low, sources, lanes
        )


def signed_sums(values):
    even = lax.broadcasted_iota(I32, values.shape, 0) % 2 == 0
    return (
        jnp.sum(values, axis=0, keepdims=True),
        jnp.sum(jnp.where(even, values, -values), axis=0, keepdims=True),
    )


def first_kernel(*refs, steps, apart):
    arrived, others = refs[:steps], refs[steps : steps + apart]
    (
        cut_current,
        local_load,
        slope,
        own_wave,
        back,
        coupling_high,
        coupling_low,
        image,
        load,
        kept,
        sent,
        halo,
    ) = refs[steps + apart :]
    times, half = local_load.shape
    lanes = halo.shape[1]
    nodes = coupling_high.shape[0] - lanes
    slots = steps * CAP
    start = packet_layout(steps, times)[1]
    blank = jnp.zeros((lanes - slots, times), F32)

    def stack(blocks):
        return jnp.transpose(jnp.concatenate([*blocks, blank], axis=0))

    def sender(step, block):
        at = slice((block - 1) * CAP, block * CAP)
        if step == 0:
            return cut_current[at]
        return others[0][step, at] if apart else arrived[step - 1][at, :times]

    current = stack([sender(step, step) for step in range(1, steps + 1)])
    high, low = split(current)
    share = coupled(
        high,
        jnp.concatenate([high, low], axis=0),
        coupling_high,
        coupling_low,
        slice(nodes, None),
        slice(0, half),
    )
    load[...] = local_load[...] + share
    answer = load[...] + slope[...]
    image[...] = answer
    spectrum = dot_split((back[0], back[1]), split(answer))
    kept[...] = spectrum[:times]
    rest = spectrum.shape[0] - times
    if rest:
        sent[:rest] = spectrum[times:]
    lines = [*signed_sums(answer), *signed_sums(own_wave[...])]
    sent[rest:] = jnp.concatenate(lines + [jnp.zeros((4, half), F32)], axis=0)

    blocks = []
    for step in range(1, steps + 1):
        theirs = jnp.concatenate(
            [sender((step + block) % (steps + 1), block) for block in range(1, steps + 1)], axis=0
        )
        gains = arrived[step - 1][:CAP, start : start + slots]
        image_part = arrived[step - 1][CAP : 2 * CAP, start : start + times]
        there = arrived[step - 1][2 * CAP : 3 * CAP, start : start + times]
        blocks.append(there * (image_part + dot_split(split(gains), split(theirs))))
    halo[...] = stack(blocks)


def second_kernel(
    place,
    halo,
    near_image,
    image,
    back,
    conductances,
    coupling_high,
    coupling_low,
    linear,
    load,
    kept,
    sent,
    current,
):
    times, half = image.shape
    nodes = current.shape[1]
    side = place[0] % 2
    mine, other = half_of(side, half), half_of(1 - side, half)
    for at, field in ((mine, image), (other, near_image)):
        current[:times, at], current[times:, at] = split(conductances[:, at] * field[...])
    load[...] = image[...] * (linear[:, :half] + conductances[:, mine])
    high, low = split(halo[...])
    halo_stacked = jnp.concatenate([high, low], axis=0)
    step = 256
    for block in range(half // step):
        lanes = slice(block * step, (block + 1) * step)
        load[:, lanes] += coupled(
            current[:times], current[...], coupling_high, coupling_low, slice(0, nodes), lanes
        ) + coupled(high, halo_stacked, coupling_high, coupling_low, slice(nodes, None), lanes)
    spectrum = dot_split((back[0], back[1]), split(load[...]))
    kept[...] = spectrum[:times]
    if spectrum.shape[0] > times:
        sent[...] = spectrum[times:]


def turned(field, first_pair, half_order):
    count = field.shape[0]
    row = lax.broadcasted_iota(I32, field.shape, 0)
    scaling = (first_pair + row // 2).astype(F32) * (1.0 / half_order)
    above = pltpu.roll(field, count - 1, 0)
    below = pltpu.roll(field, 1, 0)
    return scaling * jnp.where(row % 2 == 0, above, -below)


def join(target, side, own, near):
    half = own.shape[1]
    target[:, half_of(side, half)] = own
    target[:, half_of(1 - side, half)] = near


def guess(cross, squares):
    ratio = cross / jnp.where(squares > 0.0, squares, 1.0)
    return jnp.clip(jnp.where(squares > 0.0, ratio, 0.0), -40.0, 40.0)


def products_kernel(
    place,
    vector,
    own_image,
    near_image,
    capacity,
    load,
    second_load,
    image,
    wave,
    dual,
    own_sums,
    far_sums,
    answer,
    slope,
    scalars,
    *,
    length,
):
    side = place[0] % 2
    rows = vector.shape[0]
    first_pair = place[0] * (rows // 2)
    join(answer, side, own_image[...], near_image[...])
    field, start = answer[...], vector[...]
    squares = scalar_sum(start * start)
    coeff = guess(scalar_sum(start * field), squares)
    slope[...] = capacity[...] * turned(field, first_pair, length // 2)
    start_slope = capacity[...] * turned(start, first_pair, length // 2)
    rest = field - coeff * start
    rest_slope = slope[...] - coeff * start_slope
    found = [
        coeff,
        squares,
        scalar_sum(start * rest),
        scalar_sum(rest * rest),
        scalar_sum(start * rest_slope),
        scalar_sum(start * start_slope),
        scalar_sum(rest * rest_slope),
        scalar_sum(rest * start_slope),
    ]

    sums = own_sums[...] + far_sums[...]
    base = wave[...]
    coeff = guess(scalar_sum(base * image[...]), scalar_sum(base * base))
    rest = image[...] - coeff * base
    rest_sums = [sums[line : line + 1] - coeff * sums[line + 2 : line + 3] for line in (0, 1)]
    base_sums = [sums[line + 2 : line + 3] for line in (0, 1)]
    first = load[...]
    change = second_load[...] - coeff * first
    first_ends, change_ends = signed_sums(first), signed_sums(change)

    def mixed(values, value_sums, others, other_ends):
        ends = value_sums[0] * other_ends[0] + value_sums[1] * other_ends[1]
        return scalar_sum(values * others) * (2.0 / length) - scalar_sum(ends) * (
            1.0 / length / length
        )

    found += [
        coeff,
        scalar_sum(dual[...] * change),
        scalar_sum(dual[...] * first),
        mixed(rest, rest_sums, change, change_ends),
        mixed(rest, rest_sums, first, first_ends) + mixed(base, base_sums, change, change_ends),
        mixed(base, base_sums, first, first_ends),
    ]
    device = place[1] * place[3] + place[0]
    lane = lax.broadcasted_iota(I32, scalars.shape, 1)
    column = jnp.concatenate(found + [jnp.zeros((2, 1), F32)], axis=0)
    scalars[...] = jnp.where(lane == device, column, 0.0)


def last_kernel(
    gathered,
    vector,
    answer,
    slope,
    place,
    own_part,
    near_part,
    basis_two,
    next_residue,
    *,
    entries,
):
    side = place[0] % 2
    own = [gathered[line : line + 1, :] for line in range(14)]

    def everywhere(values):
        return jnp.sum(values, axis=1, keepdims=True) / entries

    scale_square = everywhere(own[1]) + EPSILON
    coeff = everywhere(own[2] + own[0] * own[1]) / scale_square
    near = own[0] - coeff
    rest_square = everywhere(own[3] + near * (2.0 * own[2] + near * own[1]))
    along_one = own[4] + near * own[5]
    along_two = own[6] + near * (own[4] + own[7] + near * own[5])
    near = own[8] - coeff
    along_one = everywhere(along_one + own[9] + near * own[10])
    along_two = everywhere(along_two + own[11] + near * (own[12] + near * own[13]))
    scale = jnp.sqrt(scale_square)
    second_norm = jnp.sqrt(jnp.maximum(rest_square, 0.0) / scale_square + EPSILON)
    inverse = 1.0 / (second_norm * scale)
    along_one = along_one * inverse / scale_square
    along_two = along_two * inverse * inverse
    join(next_residue, side, own_part[...], near_part[...])
    second = (answer[...] - coeff * vector[...]) * inverse
    basis_two[...] = second
    next_residue[...] = (
        (next_residue[...] + slope[...] - coeff * answer[...]) * inverse
        - along_one * vector[...]
        - along_two * second
    )


VMEM = pl.BlockSpec(memory_space=pltpu.VMEM)
SMEM = pl.BlockSpec(memory_space=pltpu.SMEM)
ANY = pl.BlockSpec(memory_space=pl.ANY)


def run(kernel, name, specs, operands, outs, scratch=(), micros=1):
    return pl.pallas_call(
        kernel,
        out_shape=[pltpu.VMEM(shape, dtype) for shape, dtype in outs],
        in_specs=specs,
        out_specs=[VMEM] * len(outs),
        scratch_shapes=list(scratch),
        compiler_params=pltpu.CompilerParams(vmem_limit_bytes=40 * 2**20),
        cost_estimate=pl.CostEstimate(
            flops=0, bytes_accessed=int(micros * 3e6), transcendentals=0
        ),
        name=name,
    )(*operands)


def swap(value, mask):
    count = lax.axis_size("samples")
    return lax.ppermute(value, "samples", [(at, at ^ mask) for at in range(count)])


def ahead(value, step):
    count = lax.axis_size("nodes")
    return lax.ppermute(value, "nodes", [(at, (at + step) % count) for at in range(count)])


def total(value):
    for axis in ("samples", "nodes"):
        count, stride = lax.axis_size(axis), 1
        while stride < count:
            radix = 4 if count // stride % 4 == 0 else 2
            others = [
                lax.ppermute(value, axis, [(at, at ^ (step * stride)) for at in range(count)])
                for step in range(1, radix)
            ]
            value = value + functools.reduce(jnp.add, others)
            stride *= radix
    return value


def reduce_groups(kept, sent):
    times = kept.shape[0]
    count = lax.axis_size("samples") // 2
    extra = sent[(count - 1) * times :]
    if count == 2:
        arrived = swap(sent, 2)
        return kept + arrived[:times], arrived[times:]
    blocks = {0: kept}
    for group in range(1, count):
        blocks[group] = sent[(group - 1) * times : group * times]
    bit = count // 2
    while bit:
        for group in [name for name in blocks if name & bit]:
            blocks[group ^ bit] = blocks[group ^ bit] + swap(blocks.pop(group), 2 * bit)
        bit //= 2
    others, bit = extra, 1
    while bit < count:
        others = others + swap(others, 2 * bit)
        bit *= 2
    return blocks[0], others - extra


def shards(
    vector, operating, table, linear, capacity, weights, degree, neighbours, boundary, send_list
):
    rows, nodes = vector.shape
    parts, node_groups = lax.axis_size("samples"), lax.axis_size("nodes")
    length, half, times = rows * parts, nodes // 2, 2 * rows
    entries = float(length * nodes * node_groups)
    steps = node_groups - 1
    slots = steps * CAP
    lanes = -(-slots // LANES) * LANES
    sources, width = nodes + lanes, half + lanes
    place = jnp.stack(
        [
            lax.axis_index("samples"),
            lax.axis_index("nodes"),
            jnp.int32(node_groups),
            jnp.int32(parts),
        ]
    ).astype(I32)
    forward, back = (jnp.asarray(table) for table in transform_tables(length, parts))
    linear, capacity, degree, table = (
        value.reshape(1, -1) for value in (linear, capacity, degree, table)
    )

    near_operating = swap(operating, 1)
    vectors, bit = [vector], parts // 2
    while bit:
        vectors = vectors + [swap(piece, bit) for piece in vectors]
        bit //= 2

    slot_count = weights.shape[0]
    (
        coupling_high,
        coupling_low,
        conductances,
        picked,
        linear_wide,
        capacity_wide,
        capacity,
        cut_halo,
        own_vector,
        forward,
        back,
    ) = run(
        prepare_kernel,
        "prepare",
        [SMEM] * 3 + [ANY] * 11,
        (place, send_list, boundary, near_operating, operating, neighbours, weights, degree)
        + (linear, capacity, table, vector, forward, back),
        [
            ((sources, width), BF16),
            ((sources, width), BF16),
            ((times, sources), F32),
            ((nodes, lanes), BF16),
            ((1, width), F32),
            ((1, width), F32),
            ((1, nodes), F32),
            ((lanes, lanes), F32),
            ((rows, nodes), F32),
            (forward.shape[1:], BF16),
            (back.shape[1:], BF16),
        ],
        scratch=[
            pltpu.VMEM((rows, nodes), F32),
            pltpu.VMEM((rows, nodes), F32),
            pltpu.VMEM((slot_count, nodes), I32),
            pltpu.VMEM((slot_count, nodes), F32),
            pltpu.VMEM((1, nodes), I32),
            pltpu.VMEM((1, nodes), F32),
            pltpu.VMEM(table.shape, F32),
            pltpu.VMEM((slot_count, width), I32),
            pltpu.VMEM((slot_count, width), F32),
            pltpu.SemaphoreType.DMA((11,)),
        ],
        micros=8,
    )
    vectors[0] = own_vector

    wide = ((times, half), F32)
    shared, start = packet_layout(steps, times)
    packet = (
        max(slots if shared else 0, 3 * CAP),
        -(-(start + max(times, slots)) // LANES) * LANES,
    )
    field_high, field_low, wave, current, cut_current, *sent = run(
        functools.partial(wave_kernel, pieces=parts),
        "wave",
        [VMEM] * (parts + 8),
        (*vectors, forward, conductances, picked, coupling_high, coupling_low)
        + (linear_wide, capacity_wide, cut_halo),
        [
            ((length, sources), BF16),
            ((length, sources), BF16),
            ((times, sources), F32),
            ((2 * times, nodes), BF16),
            ((lanes, times), F32),
        ]
        + [(packet, F32)] * steps,
        micros=2,
    )
    arrived = [ahead(packet, step + 1) for step, packet in enumerate(sent)]
    others = []
    if not shared:
        gathered = lax.all_gather(cut_current, "nodes")
        distance = jnp.arange(node_groups, dtype=I32)
        others = [gathered[(lax.axis_index("nodes") - distance) % node_groups]]
    local_load, slope, own_wave, dual = run(
        local_kernel,
        "local",
        [VMEM] * 10 + [SMEM],
        (field_high, field_low, forward, wave, current, conductances)
        + (coupling_high, coupling_low, linear_wide, capacity_wide, place),
        [wide] * 4,
        micros=3,
    )
    rest = length - times
    image, load, kept, sent, halo = run(
        functools.partial(first_kernel, steps=steps, apart=len(others)),
        "first",
        [VMEM] * (steps + len(others) + 7),
        (*arrived, *others, cut_current, local_load, slope, own_wave, back, coupling_high, coupling_low),
        [wide, wide, wide, ((rest + 8, half), F32), ((times, lanes), F32)],
        micros=1,
    )
    own_sums = sent[rest:]
    near_image = swap(image, 1)
    spectrum, far_sums = reduce_groups(kept, sent)
    own_coefs, near_coefs = spectrum[:rows], swap(spectrum[rows:], 1)

    second_load, kept, sent = run(
        second_kernel,
        "second",
        [SMEM] + [VMEM] * 8,
        (place, halo, near_image, image, back, conductances)
        + (coupling_high, coupling_low, linear_wide),
        [wide, wide, ((max(rest, 8), half), F32)],
        scratch=[pltpu.VMEM((2 * times, nodes), BF16)],
        micros=3,
    )
    gathered = -(-node_groups * parts // LANES) * LANES
    answer, slope, scalars = run(
        functools.partial(products_kernel, length=length),
        "products",
        [SMEM] + [VMEM] * 11,
        (place, own_vector, own_coefs, near_coefs, capacity, load, second_load)
        + (image, own_wave, dual, own_sums, far_sums),
        [((rows, nodes), F32), ((rows, nodes), F32), ((16, gathered), F32)],
        micros=1,
    )
    scalars = total(scalars)
    spectrum, _ = reduce_groups(kept, sent)
    own_part, near_part = spectrum[:rows], swap(spectrum[rows:], 1)
    field = jax.ShapeDtypeStruct((rows, nodes), F32)
    return tuple(
        pl.pallas_call(
            functools.partial(last_kernel, entries=entries),
            out_shape=[field, field],
            in_specs=[VMEM] * 4 + [SMEM] + [VMEM] * 2,
            out_specs=[VMEM] * 2,
            name="last",
        )(scalars, own_vector, answer, slope, place, own_part, near_part)
    )


def solution(mesh):
    return jax.shard_map(
        shards,
        mesh=mesh,
        in_specs=(
            P("samples", ("copies", "nodes")),
            P("samples", ("copies", "nodes")),
            P(),
            P("nodes"),
            P("nodes"),
            P(None, "nodes"),
            P("nodes"),
            P(None, "nodes"),
            P("nodes"),
            P("nodes"),
        ),
        out_specs=(P("samples", ("copies", "nodes")), P("samples", ("copies", "nodes"))),
        check_vma=False,
    )
```

```python
import functools
import math

import jax
import jax.numpy as jnp
import numpy as np
from jax import lax
from jax.experimental import pallas as pl
from jax.experimental.pallas import tpu as pltpu
from jax.sharding import PartitionSpec as P

CAP = 16
EPSILON = 1e-06
LANES = 128
BF16 = jnp.bfloat16
F32 = jnp.float32
I32 = jnp.int32


def spectral_tables(length):
    indices = np.arange(length)
    frequency = np.where(indices == 1, length // 2, indices // 2)
    angles = (indices[:, None] * frequency[None, :] % length) * (2.0 * math.pi / length)
    cosine_column = (indices % 2 == 0) | (indices == 1)
    synthesis = np.where(cosine_column[None, :], np.cos(angles), np.sin(angles))
    factor = np.where(indices < 2, 1.0 / length, 2.0 / length)
    analysis = synthesis.T * factor[:, None]
    turn = np.zeros((length, length))
    for pair in range(length // 2):
        turn[2 * pair, 2 * pair + 1] = pair / (length // 2)
        turn[2 * pair + 1, 2 * pair] = -pair / (length // 2)
    return synthesis, analysis, synthesis @ turn


def halves(table):
    high = table.astype(np.float32).astype(BF16)
    low = (table - high.astype(np.float64)).astype(np.float32).astype(BF16)
    return np.stack([high, low])


def piece_order(count):
    masks, bit = [0], count // 2
    while bit:
        masks = masks + [mask ^ bit for mask in masks]
        bit //= 2
    return masks


def transform_tables(length, parts):
    synthesis, analysis, slope = spectral_tables(length)
    rows = length // parts
    forward, back = [], []
    for place in range(parts):
        times = np.arange(place // 2 * 2 * rows, (place // 2 + 1) * 2 * rows)
        block = lambda owner: np.arange(owner * rows, (owner + 1) * rows)
        coefs = np.concatenate([block(place ^ mask) for mask in piece_order(parts)])
        forward.append(
            np.concatenate(
                [
                    synthesis[np.ix_(times, coefs)],
                    slope[np.ix_(times, coefs)],
                    analysis[np.ix_(coefs, times)].T,
                ]
            )
        )
        sent = np.concatenate(
            [block(place ^ (2 * group) ^ side) for group in range(parts // 2) for side in (0, 1)]
        )
        back.append(analysis[np.ix_(sent, times)])
    return (
        np.moveaxis(halves(np.stack(forward)), 0, 1),
        np.moveaxis(halves(np.stack(back)), 0, 1),
    )


def split(values):
    high = values.astype(BF16)
    return high, (values - high.astype(F32)).astype(BF16)


def dot(first, second):
    return jnp.dot(first, second, preferred_element_type=F32)


def dot_split(first, second):
    (first_high, first_low), (second_high, second_low) = first, second
    rows = first_high.shape[0]
    both = dot(jnp.concatenate([first_high, first_low], axis=0), second_high)
    return both[:rows] + both[rows:] + dot(first_high, second_low)


def lane_sums(values):
    blocks = values.shape[1] // LANES
    total = values[:, :LANES]
    for block in range(1, blocks):
        total = total + values[:, block * LANES : (block + 1) * LANES]
    return jnp.sum(total, axis=0, keepdims=True)


def half_of(side, half):
    return pl.ds(pl.multiple_of(side * half, LANES), half)


def scalar_sum(values):
    return jnp.sum(lane_sums(values), axis=1, keepdims=True)


def pick(values, picked):
    high, _ = split(values)
    middle, low = split(values - high.astype(F32))
    rows = values.shape[0]
    found = dot(jnp.concatenate([high, middle, low], axis=0), picked)
    return found[:rows] + (found[rows : 2 * rows] + found[2 * rows :])


def conductance(operating, table):
    points = table.shape[1]
    spread = jnp.concatenate([table, jnp.zeros((1, LANES - points), F32)], axis=1)
    spread = jnp.broadcast_to(spread, (operating.shape[0], LANES))
    pieces = []
    for block in range(operating.shape[1] // LANES):
        scaled = (operating[:, block * LANES : (block + 1) * LANES] + 4.0) * ((points - 1) / 8.0)
        knot = jnp.clip(jnp.floor(scaled), 0.0, points - 2.0)
        weight = scaled - knot
        place = knot.astype(I32)
        left = jnp.take_along_axis(spread, place, axis=1, mode="promise_in_bounds")
        right = jnp.take_along_axis(spread, place + 1, axis=1, mode="promise_in_bounds")
        pieces.append(left + weight * (right - left))
    return jnp.concatenate(pieces, axis=1)


def prepare_kernel(
    place,
    neighbours_in,
    weights_in,
    degree_in,
    linear_in,
    capacity_in,
    send_list_in,
    boundary_in,
    table_in,
    operating_in,
    vector_in,
    forward_in,
    back_in,
    coupling_high,
    coupling_low,
    picked,
    linear,
    capacity,
    capacity_all,
    cut_halo,
    table,
    operating,
    vector,
    forward,
    back,
    neighbours,
    weights,
    degree,
    linear_all,
    send_list,
    boundary,
    entry_rows,
    weight_rows,
    copied,
):
    slots, nodes = neighbours.shape
    sources, width = coupling_high.shape
    lanes = picked.shape[1]
    half = width - lanes
    node_groups = send_list.shape[0] // CAP
    side, part = place[0] % 2, place[1]
    copies = [
        pltpu.make_async_copy(source, target, copied.at[index])
        for index, (source, target) in enumerate(
            [
                (send_list_in, send_list),
                (boundary_in, boundary),
                (neighbours_in, neighbours),
                (weights_in, weights),
                (degree_in, degree),
                (linear_in, linear_all),
                (capacity_in, capacity_all),
                (table_in, table),
                (operating_in, operating),
                (vector_in, vector),
                (forward_in.at[place[0]], forward),
                (back_in.at[place[0]], back),
            ]
        )
    ]
    for copy in copies:
        copy.start()
    for copy in copies[:2]:
        copy.wait()

    lane = lax.broadcasted_iota(I32, (8, lanes), 1)

    def name(slot, found):
        target = part ^ (slot // CAP + 1)
        node = boundary[send_list[target * CAP + slot % CAP]]
        return jnp.where(lane == slot, node, found)

    cut_nodes = lax.fori_loop(
        0, (node_groups - 1) * CAP, name, jnp.full((8, lanes), -1, I32), unroll=8
    )
    hit = lax.broadcasted_iota(I32, (nodes, lanes), 0) == cut_nodes[:1]
    picked[...] = jnp.where(hit, 1.0, 0.0).astype(BF16)

    for copy in copies[2:7]:
        copy.wait()
    mine = half_of(side, half)
    entry = neighbours[...]
    remote = entry - nodes
    distance = part ^ (remote >> 4)
    entry = jnp.where(remote < 0, entry, nodes + (distance - 1) * CAP + (remote & 15))
    live = lax.broadcasted_iota(I32, (slots, nodes), 0) < degree[...]
    neighbours[...] = entry
    weights[...] = jnp.where(live, weights[...], 0.0)
    columns = jnp.concatenate(
        [
            entry.astype(F32),
            weights[...],
            linear_all[...],
            capacity_all[...],
            jnp.zeros((6, nodes), F32),
        ],
        axis=0,
    )
    at_cut = pick(columns, picked[...])
    linear[:, :half] = linear_all[:, mine]
    linear[:, half:] = at_cut[2 * slots : 2 * slots + 1]
    capacity[:, :half] = capacity_all[:, mine]
    capacity[:, half:] = at_cut[2 * slots + 1 : 2 * slots + 2]
    entry_rows[:, :half] = neighbours[:, mine]
    entry_rows[:, half:] = at_cut[:slots].astype(I32)
    weight_rows[:, :half] = weights[:, mine]
    weight_rows[:, half:] = at_cut[slots : 2 * slots]
    entries = [entry_rows[slot : slot + 1, :] for slot in range(slots)]
    gains = [weight_rows[slot : slot + 1, :] for slot in range(slots)]
    for slot in range(slots):
        for later in range(slot + 1, slots):
            same = entries[slot] == entries[later]
            gains[slot] = gains[slot] + jnp.where(same, gains[later], 0.0)
            entries[later] = jnp.where(same, -1, entries[later])
    for slot in range(slots):
        entry_rows[slot : slot + 1, :] = entries[slot]
        weight_rows[slot : slot + 1, :] = gains[slot]

    unroll = 4

    def column_block(block, carry):
        at_lanes = pl.ds(pl.multiple_of(block * LANES, LANES), LANES)
        wide = (CAP, LANES)
        names = [
            jnp.broadcast_to(entry_rows[slot : slot + 1, at_lanes], wide).astype(jnp.int16)
            for slot in range(slots)
        ]
        parts = [
            split(jnp.broadcast_to(weight_rows[slot : slot + 1, at_lanes], wide))
            for slot in range(slots)
        ]

        def source_rows(step, row):
            for inner in range(unroll):
                high = jnp.zeros(wide, BF16)
                low = jnp.zeros(wide, BF16)
                for slot in range(slots):
                    hit = names[slot] == row
                    high = jnp.where(hit, parts[slot][0], high)
                    low = jnp.where(hit, parts[slot][1], low)
                at = pl.ds(pl.multiple_of((step * unroll + inner) * 16, 16), 16)
                coupling_high[at, at_lanes] = high
                coupling_low[at, at_lanes] = low
                row = row + jnp.int16(16)
            return row

        lax.fori_loop(
            0,
            sources // 16 // unroll,
            source_rows,
            lax.broadcasted_iota(I32, wide, 0).astype(jnp.int16),
        )
        return carry

    lax.fori_loop(0, width // LANES, column_block, 0)
    cut_halo[...] = jnp.transpose(
        coupling_high[nodes:, half:].astype(F32) + coupling_low[nodes:, half:].astype(F32)
    )

    for copy in copies[7:]:
        copy.wait()


def relay_kernel(*refs):
    count = (len(refs) - 1) // 2
    for source, target in zip(refs[1 : 1 + count], refs[1 + count :]):
        target[...] = source[...]


def conductance_kernel(place, near_operating, operating, table, picked, conductances):
    rows, nodes = operating.shape
    side = place[0] % 2
    for at, values in ((side, operating), (1 - side, near_operating)):
        conductances[pl.ds(pl.multiple_of(at * rows, 8), rows), :nodes] = conductance(
            values[...], table[...]
        )
    conductances[:, nodes:] = pick(conductances[:, :nodes], picked[...])


def coupled(high, stacked, coupling_high, coupling_low, sources, lanes):
    rows = high.shape[0]
    both = dot(stacked, coupling_high[sources, lanes])
    return both[:rows] + both[rows:] + dot(high, coupling_low[sources, lanes])


def packet_layout(steps, times):
    shared = steps * CAP <= LANES
    return shared, times if shared else 0


def wave_kernel(*refs, pieces):
    vectors = refs[:pieces]
    (
        forward,
        conductances,
        picked,
        coupling_high,
        coupling_low,
        linear,
        capacity,
        cut_halo,
        field_high,
        field_low,
        wave,
        current,
        cut_current,
    ) = refs[pieces : pieces + 13]
    sent = refs[pieces + 13 :]
    rows, nodes = vectors[0].shape
    lanes = picked.shape[1]
    times = wave.shape[0]
    half = linear.shape[1] - lanes
    for index in range(pieces):
        at = slice(index * rows, (index + 1) * rows)
        field_high[at, :nodes], field_low[at, :nodes] = split(vectors[index][...])
    field_high[:, nodes:] = dot(field_high[:, :nodes], picked[...]).astype(BF16)
    field_low[:, nodes:] = dot(field_low[:, :nodes], picked[...]).astype(BF16)
    wave[...] = dot_split(
        (forward[0, :times], forward[1, :times]), (field_high[...], field_low[...])
    )
    slope = dot_split(
        (forward[0, times : 2 * times], forward[1, times : 2 * times]),
        (field_high[:, nodes:], field_low[:, nodes:]),
    )
    high, low = split(conductances[:, :nodes] * wave[:, :nodes])
    current[:times] = high
    current[times:] = low
    at_cut = conductances[:, nodes:] * wave[:, nodes:]
    cut_current[...] = jnp.transpose(at_cut)
    image = (
        linear[:, half:] * wave[:, nodes:]
        + at_cut
        + capacity[:, half:] * slope
        + coupled(
            high, current[...], coupling_high, coupling_low, slice(0, nodes), slice(half, None)
        )
    )
    image = jnp.transpose(image)
    at_cut = jnp.transpose(conductances[:, nodes:])
    slots = len(sent) * CAP
    shared, start = packet_layout(len(sent), times)
    for step, target in enumerate(sent):
        at = slice(step * CAP, (step + 1) * CAP)
        target[...] = jnp.zeros(target.shape, F32)
        if shared:
            target[:slots, :times] = cut_current[:slots]
        target[:CAP, start : start + slots] = cut_halo[at, :slots]
        target[CAP : 2 * CAP, start : start + times] = image[at]
        target[2 * CAP : 3 * CAP, start : start + times] = at_cut[at]


def local_kernel(
    field_high,
    field_low,
    forward,
    wave,
    current,
    conductances,
    coupling_high,
    coupling_low,
    linear,
    capacity,
    place,
    load,
    slope,
    own_wave,
    dual,
):
    times, half = load.shape
    sources = slice(0, current.shape[1])
    mine = half_of(place[0] % 2, half)
    others = dot_split(
        (forward[0, times:], forward[1, times:]), (field_high[:, mine], field_low[:, mine])
    )
    slope[...] = capacity[:, :half] * others[:times]
    dual[...] = others[times:]
    own_wave[...] = wave[:, mine]
    load[...] = own_wave[...] * (linear[:, :half] + conductances[:, mine])
    high = current[:times]
    step = 256
    for block in range(half // step):
        lanes = slice(block * step, (block + 1) * step)
        load[:, lanes] += coupled(
            high, current[...], coupling_high, coupling_low, sources, lanes
        )


def signed_sums(values):
    even = lax.broadcasted_iota(I32, values.shape, 0) % 2 == 0
    return (
        jnp.sum(values, axis=0, keepdims=True),
        jnp.sum(jnp.where(even, values, -values), axis=0, keepdims=True),
    )


def first_kernel(*refs, steps, apart):
    arrived, others = refs[:steps], refs[steps : steps + apart]
    (
        cut_current,
        local_load,
        slope,
        own_wave,
        back,
        coupling_high,
        coupling_low,
        image,
        load,
        kept,
        sent,
        halo,
    ) = refs[steps + apart :]
    times, half = local_load.shape
    lanes = halo.shape[1]
    nodes = coupling_high.shape[0] - lanes
    slots = steps * CAP
    start = packet_layout(steps, times)[1]
    blank = jnp.zeros((lanes - slots, times), F32)

    def stack(blocks):
        return jnp.transpose(jnp.concatenate([*blocks, blank], axis=0))

    def sender(step, block):
        at = slice((block - 1) * CAP, block * CAP)
        if step == 0:
            return cut_current[at]
        return others[0][step, at] if apart else arrived[step - 1][at, :times]

    current = stack([sender(step, step) for step in range(1, steps + 1)])
    high, low = split(current)
    share = coupled(
        high,
        jnp.concatenate([high, low], axis=0),
        coupling_high,
        coupling_low,
        slice(nodes, None),
        slice(0, half),
    )
    load[...] = local_load[...] + share
    answer = load[...] + slope[...]
    image[...] = answer
    spectrum = dot_split((back[0], back[1]), split(answer))
    kept[...] = spectrum[:times]
    rest = spectrum.shape[0] - times
    if rest:
        sent[:rest] = spectrum[times:]
    lines = [*signed_sums(answer), *signed_sums(own_wave[...])]
    sent[rest:] = jnp.concatenate(lines + [jnp.zeros((4, half), F32)], axis=0)

    blocks = []
    for step in range(1, steps + 1):
        theirs = jnp.concatenate(
            [sender(step ^ block, block) for block in range(1, steps + 1)], axis=0
        )
        gains = arrived[step - 1][:CAP, start : start + slots]
        image_part = arrived[step - 1][CAP : 2 * CAP, start : start + times]
        there = arrived[step - 1][2 * CAP : 3 * CAP, start : start + times]
        blocks.append(there * (image_part + dot_split(split(gains), split(theirs))))
    halo[...] = stack(blocks)


def second_kernel(
    place,
    halo,
    near_image,
    image,
    back,
    conductances,
    coupling_high,
    coupling_low,
    linear,
    load,
    kept,
    sent,
    current,
):
    times, half = image.shape
    nodes = current.shape[1]
    side = place[0] % 2
    mine, other = half_of(side, half), half_of(1 - side, half)
    for at, field in ((mine, image), (other, near_image)):
        current[:times, at], current[times:, at] = split(conductances[:, at] * field[...])
    load[...] = image[...] * (linear[:, :half] + conductances[:, mine])
    high, low = split(halo[...])
    halo_stacked = jnp.concatenate([high, low], axis=0)
    step = 256
    for block in range(half // step):
        lanes = slice(block * step, (block + 1) * step)
        load[:, lanes] += coupled(
            current[:times], current[...], coupling_high, coupling_low, slice(0, nodes), lanes
        ) + coupled(high, halo_stacked, coupling_high, coupling_low, slice(nodes, None), lanes)
    spectrum = dot_split((back[0], back[1]), split(load[...]))
    kept[...] = spectrum[:times]
    if spectrum.shape[0] > times:
        sent[...] = spectrum[times:]


def merge_kernel(after, kept, arrived, own, near, far_sums):
    rows = own.shape[0]
    own[...] = kept[:rows] + arrived[:rows]
    near[...] = kept[rows:] + arrived[rows : 2 * rows]
    if arrived.shape[0] > 2 * rows:
        far_sums[...] = arrived[2 * rows :]
    else:
        far_sums[...] = jnp.zeros(far_sums.shape, F32)


def turned(field, first_pair, half_order):
    count = field.shape[0]
    row = lax.broadcasted_iota(I32, field.shape, 0)
    scaling = (first_pair + row // 2).astype(F32) * (1.0 / half_order)
    above = pltpu.roll(field, count - 1, 0)
    below = pltpu.roll(field, 1, 0)
    return scaling * jnp.where(row % 2 == 0, above, -below)


def join(target, side, own, near):
    half = own.shape[1]
    target[:, half_of(side, half)] = own
    target[:, half_of(1 - side, half)] = near


def guess(cross, squares):
    ratio = cross / jnp.where(squares > 0.0, squares, 1.0)
    return jnp.clip(jnp.where(squares > 0.0, ratio, 0.0), -40.0, 40.0)


def products_kernel(
    place,
    vector,
    own_image,
    near_image,
    capacity,
    load,
    second_load,
    image,
    wave,
    dual,
    own_sums,
    far_sums,
    answer,
    slope,
    scalars,
    *,
    length,
):
    side = place[0] % 2
    rows = vector.shape[0]
    first_pair = place[0] * (rows // 2)
    join(answer, side, own_image[...], near_image[...])
    field, start = answer[...], vector[...]
    squares = scalar_sum(start * start)
    coeff = guess(scalar_sum(start * field), squares)
    slope[...] = capacity[...] * turned(field, first_pair, length // 2)
    start_slope = capacity[...] * turned(start, first_pair, length // 2)
    rest = field - coeff * start
    rest_slope = slope[...] - coeff * start_slope
    found = [
        coeff,
        squares,
        scalar_sum(start * rest),
        scalar_sum(rest * rest),
        scalar_sum(start * rest_slope),
        scalar_sum(start * start_slope),
        scalar_sum(rest * rest_slope),
        scalar_sum(rest * start_slope),
    ]

    sums = own_sums[...] + far_sums[...]
    base = wave[...]
    coeff = guess(scalar_sum(base * image[...]), scalar_sum(base * base))
    rest = image[...] - coeff * base
    rest_sums = [sums[line : line + 1] - coeff * sums[line + 2 : line + 3] for line in (0, 1)]
    base_sums = [sums[line + 2 : line + 3] for line in (0, 1)]
    first = load[...]
    change = second_load[...] - coeff * first
    first_ends, change_ends = signed_sums(first), signed_sums(change)

    def mixed(values, value_sums, others, other_ends):
        ends = value_sums[0] * other_ends[0] + value_sums[1] * other_ends[1]
        return scalar_sum(values * others) * (2.0 / length) - scalar_sum(ends) * (
            1.0 / length / length
        )

    found += [
        coeff,
        scalar_sum(dual[...] * change),
        scalar_sum(dual[...] * first),
        mixed(rest, rest_sums, change, change_ends),
        mixed(rest, rest_sums, first, first_ends) + mixed(base, base_sums, change, change_ends),
        mixed(base, base_sums, first, first_ends),
    ]
    device = place[1] * place[3] + place[0]
    lane = lax.broadcasted_iota(I32, scalars.shape, 1)
    column = jnp.concatenate(found + [jnp.zeros((2, 1), F32)], axis=0)
    scalars[...] = jnp.where(lane == device, column, 0.0)


def last_kernel(
    gathered,
    vector,
    answer,
    slope,
    place,
    own_part,
    near_part,
    basis_two,
    next_residue,
    *,
    entries,
):
    side = place[0] % 2
    own = [gathered[line : line + 1, :] for line in range(14)]

    def everywhere(values):
        return jnp.sum(values, axis=1, keepdims=True) / entries

    scale_square = everywhere(own[1]) + EPSILON
    coeff = everywhere(own[2] + own[0] * own[1]) / scale_square
    near = own[0] - coeff
    rest_square = everywhere(own[3] + near * (2.0 * own[2] + near * own[1]))
    along_one = own[4] + near * own[5]
    along_two = own[6] + near * (own[4] + own[7] + near * own[5])
    near = own[8] - coeff
    along_one = everywhere(along_one + own[9] + near * own[10])
    along_two = everywhere(along_two + own[11] + near * (own[12] + near * own[13]))
    scale = jnp.sqrt(scale_square)
    second_norm = jnp.sqrt(jnp.maximum(rest_square, 0.0) / scale_square + EPSILON)
    inverse = 1.0 / (second_norm * scale)
    along_one = along_one * inverse / scale_square
    along_two = along_two * inverse * inverse
    join(next_residue, side, own_part[...], near_part[...])
    second = (answer[...] - coeff * vector[...]) * inverse
    basis_two[...] = second
    next_residue[...] = (
        (next_residue[...] + slope[...] - coeff * answer[...]) * inverse
        - along_one * vector[...]
        - along_two * second
    )


VMEM = pl.BlockSpec(memory_space=pltpu.VMEM)
SMEM = pl.BlockSpec(memory_space=pltpu.SMEM)


HBM = pl.BlockSpec(memory_space=pltpu.HBM)


def run(kernel, name, specs, operands, outs, scratch=(), micros=1, room=12):
    return pl.pallas_call(
        kernel,
        out_shape=[pltpu.VMEM(shape, dtype) for shape, dtype in outs],
        in_specs=specs,
        out_specs=[VMEM] * len(outs),
        scratch_shapes=list(scratch),
        compiler_params=pltpu.CompilerParams(vmem_limit_bytes=room * 2**20),
        cost_estimate=pl.CostEstimate(
            flops=0, bytes_accessed=int(micros * 3e6), transcendentals=0
        ),
        name=name,
    )(*operands)


def swap(value, mask):
    count = lax.axis_size("samples")
    return lax.ppermute(value, "samples", [(at, at ^ mask) for at in range(count)])


def trade(value, mask):
    count = lax.axis_size("nodes")
    return lax.ppermute(value, "nodes", [(at, at ^ mask) for at in range(count)])


def total(value):
    for axis in ("nodes", "samples"):
        count, stride = lax.axis_size(axis), 1
        while stride < count:
            radix = 4 if count // stride % 4 == 0 else 2
            others = [
                lax.ppermute(value, axis, [(at, at ^ (step * stride)) for at in range(count)])
                for step in range(1, radix)
            ]
            value = value + functools.reduce(jnp.add, others)
            stride *= radix
    return value


def reduce_groups(kept, sent, after):
    times, half = kept.shape
    count = lax.axis_size("samples") // 2
    block, arrived = kept, sent
    if count > 2:
        blocks = {group: sent[(group - 1) * times : group * times] for group in range(1, count)}
        extra = sent[(count - 1) * times :]
        blocks[0], bit = kept, count // 2
        while bit > 1:
            for group in [name for name in blocks if name & bit]:
                blocks[group ^ bit] = blocks[group ^ bit] + swap(blocks.pop(group), 2 * bit)
            bit //= 2
        block = blocks[0]
        others, bit = extra, 2
        while bit < count:
            others = others + swap(others, 2 * bit)
            bit *= 2
        arrived = jnp.concatenate([blocks[1], others], axis=0)
        arrived = swap(arrived, 2)
        arrived = jnp.concatenate([arrived[:times], arrived[times:] + others - extra], axis=0)
    elif count == 2:
        arrived = swap(sent, 2)
    else:
        arrived = jnp.zeros((times + sent.shape[0], half), F32)
    own, near, extra = run(
        merge_kernel,
        "merge",
        [VMEM] * 3,
        (after, block, arrived),
        [((times // 2, half), F32), ((times // 2, half), F32), ((8, half), F32)],
    )
    return own, swap(near, 1), extra


def shards(
    vector, operating, table, linear, capacity, weights, degree, neighbours, boundary, send_list
):
    rows, nodes = vector.shape
    parts, node_groups = lax.axis_size("samples"), lax.axis_size("nodes")
    length, half, times = rows * parts, nodes // 2, 2 * rows
    entries = float(length * nodes * node_groups)
    steps = node_groups - 1
    slots = steps * CAP
    lanes = -(-slots // LANES) * LANES
    sources, width = nodes + lanes, half + lanes
    place = jnp.stack(
        [
            lax.axis_index("samples"),
            lax.axis_index("nodes"),
            jnp.int32(node_groups),
            jnp.int32(parts),
        ]
    ).astype(I32)
    forward, back = (jnp.asarray(table) for table in transform_tables(length, parts))
    linear, capacity, degree, table = (
        value.reshape(1, -1) for value in (linear, capacity, degree, table)
    )

    slot_count = weights.shape[0]
    (
        coupling_high,
        coupling_low,
        picked,
        linear_wide,
        capacity_wide,
        capacity,
        cut_halo,
        table,
        own_operating,
        own_vector,
        forward,
        back,
    ) = run(
        prepare_kernel,
        "prepare",
        [SMEM] + [HBM] * 12,
        (place,)
        + tuple(
            pltpu.with_memory_space_constraint(value, pltpu.HBM)
            for value in (neighbours, weights, degree, linear, capacity, send_list, boundary)
            + (table, operating, vector, forward, back)
        ),
        [
            ((sources, width), BF16),
            ((sources, width), BF16),
            ((nodes, lanes), BF16),
            ((1, width), F32),
            ((1, width), F32),
            ((1, nodes), F32),
            ((lanes, lanes), F32),
            (table.shape, F32),
            ((rows, nodes), F32),
            ((rows, nodes), F32),
            (forward.shape[1:], BF16),
            (back.shape[1:], BF16),
        ],
        scratch=[
            pltpu.VMEM((slot_count, nodes), I32),
            pltpu.VMEM((slot_count, nodes), F32),
            pltpu.VMEM((1, nodes), I32),
            pltpu.VMEM((1, nodes), F32),
            pltpu.SMEM(send_list.shape, I32),
            pltpu.SMEM(boundary.shape, I32),
            pltpu.VMEM((slot_count, width), I32),
            pltpu.VMEM((slot_count, width), F32),
            pltpu.SemaphoreType.DMA((12,)),
        ],
        micros=8,
    )
    near_operating = swap(operating, 1)
    vectors, bit = [vector], parts // 2
    while bit > 1:
        vectors = vectors + [swap(piece, bit) for piece in vectors]
        bit //= 2
    far = len(vectors) - 1
    if far:
        vectors[1:] = run(
            relay_kernel,
            "relay",
            [VMEM] * (far + 1),
            (cut_halo, *vectors[1:]),
            [((rows, nodes), F32)] * far,
        )
    vectors = vectors + [swap(piece, 1) for piece in vectors]
    vectors[0] = own_vector
    (conductances,) = run(
        conductance_kernel,
        "conductance",
        [SMEM] + [VMEM] * 4,
        (place, near_operating, own_operating, table, picked),
        [((times, sources), F32)],
        micros=1,
    )

    wide = ((times, half), F32)
    shared, start = packet_layout(steps, times)
    packet = (
        max(slots if shared else 0, 3 * CAP),
        -(-(start + max(times, slots)) // LANES) * LANES,
    )
    field_high, field_low, wave, current, cut_current, *sent = run(
        functools.partial(wave_kernel, pieces=parts),
        "wave",
        [VMEM] * (parts + 8),
        (*vectors, forward, conductances, picked, coupling_high, coupling_low)
        + (linear_wide, capacity_wide, cut_halo),
        [
            ((length, sources), BF16),
            ((length, sources), BF16),
            ((times, sources), F32),
            ((2 * times, nodes), BF16),
            ((lanes, times), F32),
        ]
        + [(packet, F32)] * steps,
        micros=2,
    )
    arrived = [trade(packet, step + 1) for step, packet in enumerate(sent)]
    others = []
    if not shared:
        gathered = lax.all_gather(cut_current, "nodes")
        distance = jnp.arange(node_groups, dtype=I32)
        others = [gathered[lax.axis_index("nodes") ^ distance]]
    local_load, slope, own_wave, dual = run(
        local_kernel,
        "local",
        [VMEM] * 10 + [SMEM],
        (field_high, field_low, forward, wave, current, conductances)
        + (coupling_high, coupling_low, linear_wide, capacity_wide, place),
        [wide] * 4,
        micros=3,
    )
    rest = length - times
    image, load, kept, sent, halo = run(
        functools.partial(first_kernel, steps=steps, apart=len(others)),
        "first",
        [VMEM] * (steps + len(others) + 7),
        (*arrived, *others, cut_current, local_load, slope, own_wave, back, coupling_high, coupling_low),
        [wide, wide, wide, ((rest + 8, half), F32), ((times, lanes), F32)],
        micros=1,
    )
    own_sums = sent[rest:]
    near_image = swap(image, 1)

    second_load, second_kept, second_sent = run(
        second_kernel,
        "second",
        [SMEM] + [VMEM] * 8,
        (place, halo, near_image, image, back, conductances)
        + (coupling_high, coupling_low, linear_wide),
        [wide, wide, ((max(rest, 8), half), F32)],
        scratch=[pltpu.VMEM((2 * times, nodes), BF16)],
        micros=3,
    )
    own_coefs, near_coefs, far_sums = reduce_groups(kept, sent, second_load)
    gathered = -(-node_groups * parts // LANES) * LANES
    answer, slope, scalars = run(
        functools.partial(products_kernel, length=length),
        "products",
        [SMEM] + [VMEM] * 11,
        (place, own_vector, own_coefs, near_coefs, capacity, load, second_load)
        + (image, own_wave, dual, own_sums, far_sums),
        [((rows, nodes), F32), ((rows, nodes), F32), ((16, gathered), F32)],
        micros=1,
    )
    scalars = total(scalars)
    own_part, near_part, _ = reduce_groups(second_kept, second_sent, answer)
    field = jax.ShapeDtypeStruct((rows, nodes), F32)
    return tuple(
        pl.pallas_call(
            functools.partial(last_kernel, entries=entries),
            out_shape=[field, field],
            in_specs=[VMEM] * 4 + [SMEM] + [VMEM] * 2,
            out_specs=[VMEM] * 2,
            compiler_params=pltpu.CompilerParams(vmem_limit_bytes=12 * 2**20),
            name="last",
        )(scalars, own_vector, answer, slope, place, own_part, near_part)
    )


def solution(mesh):
    return jax.shard_map(
        shards,
        mesh=mesh,
        in_specs=(
            P("samples", ("copies", "nodes")),
            P("samples", ("copies", "nodes")),
            P(),
            P("nodes"),
            P("nodes"),
            P(None, "nodes"),
            P("nodes"),
            P(None, "nodes"),
            P("nodes"),
            P("nodes"),
        ),
        out_specs=(P("samples", ("copies", "nodes")), P("samples", ("copies", "nodes"))),
        check_vma=False,
    )
```

```python
import functools
import math

import jax
import jax.numpy as jnp
import numpy as np
from jax import lax
from jax.experimental import pallas as pl
from jax.experimental.pallas import tpu as pltpu
from jax.sharding import PartitionSpec as P

CAP = 16
EPSILON = 1e-06
LANES = 128
BF16 = jnp.bfloat16
F32 = jnp.float32
I32 = jnp.int32


def spectral_tables(length):
    indices = np.arange(length)
    frequency = np.where(indices == 1, length // 2, indices // 2)
    angles = (indices[:, None] * frequency[None, :] % length) * (2.0 * math.pi / length)
    cosine_column = (indices % 2 == 0) | (indices == 1)
    synthesis = np.where(cosine_column[None, :], np.cos(angles), np.sin(angles))
    factor = np.where(indices < 2, 1.0 / length, 2.0 / length)
    analysis = synthesis.T * factor[:, None]
    turn = np.zeros((length, length))
    for pair in range(length // 2):
        turn[2 * pair, 2 * pair + 1] = pair / (length // 2)
        turn[2 * pair + 1, 2 * pair] = -pair / (length // 2)
    return synthesis, analysis, turn


def halves(table):
    high = table.astype(np.float32).astype(BF16)
    low = (table - high.astype(np.float64)).astype(np.float32).astype(BF16)
    return np.stack([high, low])


def piece_order(count):
    masks, bit = [0], count // 2
    while bit:
        masks = masks + [mask ^ bit for mask in masks]
        bit //= 2
    return masks


def transform_tables(length, parts):
    synthesis, analysis, turn = spectral_tables(length)
    slope, dual_slope = synthesis @ turn, analysis.T @ turn
    rows = length // parts
    forward, back = [], []
    for place in range(parts):
        times = np.arange(place // 2 * 2 * rows, (place // 2 + 1) * 2 * rows)
        block = lambda owner: np.arange(owner * rows, (owner + 1) * rows)
        coefs = np.concatenate([block(place ^ mask) for mask in piece_order(parts)])
        forward.append(
            np.concatenate(
                [
                    synthesis[np.ix_(times, coefs)],
                    slope[np.ix_(times, coefs)],
                    analysis[np.ix_(coefs, times)].T,
                    dual_slope[np.ix_(times, coefs)],
                ]
            )
        )
        sent = np.concatenate(
            [block(place ^ (2 * group) ^ side) for group in range(parts // 2) for side in (0, 1)]
        )
        back.append(analysis[np.ix_(sent, times)])
    return (
        np.moveaxis(halves(np.stack(forward)), 0, 1),
        np.moveaxis(halves(np.stack(back)), 0, 1),
    )


def split(values):
    high = values.astype(BF16)
    return high, (values - high.astype(F32)).astype(BF16)


def dot(first, second):
    return jnp.dot(first, second, preferred_element_type=F32)


def dot_split(first, second):
    (first_high, first_low), (second_high, second_low) = first, second
    rows = first_high.shape[0]
    both = dot(jnp.concatenate([first_high, first_low], axis=0), second_high)
    return both[:rows] + both[rows:] + dot(first_high, second_low)


def lane_sums(values):
    blocks = values.shape[1] // LANES
    total = values[:, :LANES]
    for block in range(1, blocks):
        total = total + values[:, block * LANES : (block + 1) * LANES]
    return jnp.sum(total, axis=0, keepdims=True)


def half_of(side, half):
    return pl.ds(pl.multiple_of(side * half, LANES), half)


def scalar_sum(values):
    return jnp.sum(lane_sums(values), axis=1, keepdims=True)


def pick(values, picked):
    high, _ = split(values)
    middle, low = split(values - high.astype(F32))
    rows = values.shape[0]
    found = dot(jnp.concatenate([high, middle, low], axis=0), picked)
    return found[:rows] + (found[rows : 2 * rows] + found[2 * rows :])


def conductance(operating, table):
    points = table.shape[1]
    spread = jnp.concatenate([table, jnp.zeros((1, LANES - points), F32)], axis=1)
    spread = jnp.broadcast_to(spread, (operating.shape[0], LANES))
    pieces = []
    for block in range(operating.shape[1] // LANES):
        scaled = (operating[:, block * LANES : (block + 1) * LANES] + 4.0) * ((points - 1) / 8.0)
        knot = jnp.clip(jnp.floor(scaled), 0.0, points - 2.0)
        weight = scaled - knot
        place = knot.astype(I32)
        left = jnp.take_along_axis(spread, place, axis=1, mode="promise_in_bounds")
        right = jnp.take_along_axis(spread, place + 1, axis=1, mode="promise_in_bounds")
        pieces.append(left + weight * (right - left))
    return jnp.concatenate(pieces, axis=1)


def prepare_kernel(
    place,
    neighbours_in,
    weights_in,
    degree_in,
    linear_in,
    capacity_in,
    send_list_in,
    boundary_in,
    table_in,
    operating_in,
    vector_in,
    forward_in,
    back_in,
    coupling_high,
    coupling_low,
    picked,
    linear,
    capacity,
    capacity_all,
    cut_halo,
    table,
    operating,
    vector,
    forward,
    back,
    neighbours,
    weights,
    degree,
    linear_all,
    send_list,
    boundary,
    entry_rows,
    weight_rows,
    copied,
):
    slots, nodes = neighbours.shape
    sources, width = coupling_high.shape
    lanes = picked.shape[1]
    half = width - lanes
    node_groups = send_list.shape[0] // CAP
    side, part = place[0] % 2, place[1]
    copies = [
        pltpu.make_async_copy(source, target, copied.at[index])
        for index, (source, target) in enumerate(
            [
                (send_list_in, send_list),
                (boundary_in, boundary),
                (neighbours_in, neighbours),
                (weights_in, weights),
                (degree_in, degree),
                (linear_in, linear_all),
                (capacity_in, capacity_all),
                (table_in, table),
                (operating_in, operating),
                (vector_in, vector),
                (forward_in.at[place[0]], forward),
                (back_in.at[place[0]], back),
            ]
        )
    ]
    for copy in copies:
        copy.start()
    for copy in copies[:2]:
        copy.wait()

    lane = lax.broadcasted_iota(I32, (8, lanes), 1)

    def name(slot, found):
        target = part ^ (slot // CAP + 1)
        node = boundary[send_list[target * CAP + slot % CAP]]
        return jnp.where(lane == slot, node, found)

    cut_nodes = lax.fori_loop(
        0, (node_groups - 1) * CAP, name, jnp.full((8, lanes), -1, I32), unroll=8
    )
    hit = lax.broadcasted_iota(I32, (nodes, lanes), 0) == cut_nodes[:1]
    picked[...] = jnp.where(hit, 1.0, 0.0).astype(BF16)

    for copy in copies[2:7]:
        copy.wait()
    mine = half_of(side, half)
    entry = neighbours[...]
    remote = entry - nodes
    distance = part ^ (remote >> 4)
    entry = jnp.where(remote < 0, entry, nodes + (distance - 1) * CAP + (remote & 15))
    live = lax.broadcasted_iota(I32, (slots, nodes), 0) < degree[...]
    neighbours[...] = entry
    weights[...] = jnp.where(live, weights[...], 0.0)
    columns = jnp.concatenate(
        [
            entry.astype(F32),
            weights[...],
            linear_all[...],
            capacity_all[...],
            jnp.zeros((6, nodes), F32),
        ],
        axis=0,
    )
    at_cut = pick(columns, picked[...])
    linear[:, :half] = linear_all[:, mine]
    linear[:, half:] = at_cut[2 * slots : 2 * slots + 1]
    capacity[:, :half] = capacity_all[:, mine]
    capacity[:, half:] = at_cut[2 * slots + 1 : 2 * slots + 2]
    entry_rows[:, :half] = neighbours[:, mine]
    entry_rows[:, half:] = at_cut[:slots].astype(I32)
    weight_rows[:, :half] = weights[:, mine]
    weight_rows[:, half:] = at_cut[slots : 2 * slots]
    entries = [entry_rows[slot : slot + 1, :] for slot in range(slots)]
    gains = [weight_rows[slot : slot + 1, :] for slot in range(slots)]
    for slot in range(slots):
        for later in range(slot + 1, slots):
            same = entries[slot] == entries[later]
            gains[slot] = gains[slot] + jnp.where(same, gains[later], 0.0)
            entries[later] = jnp.where(same, -1, entries[later])
    for slot in range(slots):
        entry_rows[slot : slot + 1, :] = entries[slot]
        weight_rows[slot : slot + 1, :] = gains[slot]

    unroll = 4

    def column_block(block, carry):
        at_lanes = pl.ds(pl.multiple_of(block * LANES, LANES), LANES)
        wide = (CAP, LANES)
        names = [
            jnp.broadcast_to(entry_rows[slot : slot + 1, at_lanes], wide).astype(jnp.int16)
            for slot in range(slots)
        ]
        parts = [
            split(jnp.broadcast_to(weight_rows[slot : slot + 1, at_lanes], wide))
            for slot in range(slots)
        ]

        def source_rows(step, row):
            for inner in range(unroll):
                high = jnp.zeros(wide, BF16)
                low = jnp.zeros(wide, BF16)
                for slot in range(slots):
                    hit = names[slot] == row
                    high = jnp.where(hit, parts[slot][0], high)
                    low = jnp.where(hit, parts[slot][1], low)
                at = pl.ds(pl.multiple_of((step * unroll + inner) * 16, 16), 16)
                coupling_high[at, at_lanes] = high
                coupling_low[at, at_lanes] = low
                row = row + jnp.int16(16)
            return row

        lax.fori_loop(
            0,
            sources // 16 // unroll,
            source_rows,
            lax.broadcasted_iota(I32, wide, 0).astype(jnp.int16),
        )
        return carry

    lax.fori_loop(0, width // LANES, column_block, 0)
    cut_halo[...] = jnp.transpose(
        coupling_high[nodes:, half:].astype(F32) + coupling_low[nodes:, half:].astype(F32)
    )

    for copy in copies[7:]:
        copy.wait()


def relay_kernel(*refs):
    count = (len(refs) - 1) // 2
    for source, target in zip(refs[1 : 1 + count], refs[1 + count :]):
        target[...] = source[...]


def conductance_kernel(place, near_operating, operating, table, picked, conductances):
    rows, nodes = operating.shape
    side = place[0] % 2
    for at, values in ((side, operating), (1 - side, near_operating)):
        conductances[pl.ds(pl.multiple_of(at * rows, 8), rows), :nodes] = conductance(
            values[...], table[...]
        )
    conductances[:, nodes:] = pick(conductances[:, :nodes], picked[...])


def coupled(high, stacked, coupling_high, coupling_low, sources, lanes):
    rows = high.shape[0]
    both = dot(stacked, coupling_high[sources, lanes])
    return both[:rows] + both[rows:] + dot(high, coupling_low[sources, lanes])


def packet_layout(steps, times):
    shared = steps * CAP <= LANES
    return shared, times if shared else 0


def wave_kernel(*refs, pieces):
    vectors = refs[:pieces]
    (
        forward,
        conductances,
        picked,
        coupling_high,
        coupling_low,
        linear,
        capacity,
        cut_halo,
        field_high,
        field_low,
        wave,
        current,
        cut_current,
    ) = refs[pieces : pieces + 13]
    sent = refs[pieces + 13 :]
    rows, nodes = vectors[0].shape
    lanes = picked.shape[1]
    times = wave.shape[0]
    half = linear.shape[1] - lanes
    for index in range(pieces):
        at = slice(index * rows, (index + 1) * rows)
        field_high[at, :nodes], field_low[at, :nodes] = split(vectors[index][...])
    field_high[:, nodes:] = dot(field_high[:, :nodes], picked[...]).astype(BF16)
    field_low[:, nodes:] = dot(field_low[:, :nodes], picked[...]).astype(BF16)
    wave[...] = dot_split(
        (forward[0, :times], forward[1, :times]), (field_high[...], field_low[...])
    )
    slope = dot_split(
        (forward[0, times : 2 * times], forward[1, times : 2 * times]),
        (field_high[:, nodes:], field_low[:, nodes:]),
    )
    high, low = split(conductances[:, :nodes] * wave[:, :nodes])
    current[:times] = high
    current[times:] = low
    at_cut = conductances[:, nodes:] * wave[:, nodes:]
    cut_current[...] = jnp.transpose(at_cut)
    image = (
        linear[:, half:] * wave[:, nodes:]
        + at_cut
        + capacity[:, half:] * slope
        + coupled(
            high, current[...], coupling_high, coupling_low, slice(0, nodes), slice(half, None)
        )
    )
    image = jnp.transpose(image)
    at_cut = jnp.transpose(conductances[:, nodes:])
    slots = len(sent) * CAP
    shared, start = packet_layout(len(sent), times)
    for step, target in enumerate(sent):
        at = slice(step * CAP, (step + 1) * CAP)
        target[...] = jnp.zeros(target.shape, F32)
        if shared:
            target[:slots, :times] = cut_current[:slots]
        target[:CAP, start : start + slots] = cut_halo[at, :slots]
        target[CAP : 2 * CAP, start : start + times] = image[at]
        target[2 * CAP : 3 * CAP, start : start + times] = at_cut[at]


def local_kernel(
    field_high,
    field_low,
    forward,
    wave,
    current,
    conductances,
    coupling_high,
    coupling_low,
    linear,
    capacity,
    place,
    load,
    slope,
    own_wave,
    dual,
    dual_slope,
):
    times, half = load.shape
    sources = slice(0, current.shape[1])
    mine = half_of(place[0] % 2, half)
    others = dot_split(
        (forward[0, times:], forward[1, times:]), (field_high[:, mine], field_low[:, mine])
    )
    slope[...] = capacity[:, :half] * others[:times]
    dual[...] = others[times : 2 * times]
    dual_slope[...] = capacity[:, :half] * others[2 * times :]
    own_wave[...] = wave[:, mine]
    load[...] = own_wave[...] * (linear[:, :half] + conductances[:, mine])
    high = current[:times]
    step = 256
    for block in range(half // step):
        lanes = slice(block * step, (block + 1) * step)
        load[:, lanes] += coupled(
            high, current[...], coupling_high, coupling_low, sources, lanes
        )


def signed_sums(values):
    even = lax.broadcasted_iota(I32, values.shape, 0) % 2 == 0
    return (
        jnp.sum(values, axis=0, keepdims=True),
        jnp.sum(jnp.where(even, values, -values), axis=0, keepdims=True),
    )


def first_kernel(*refs, steps, apart):
    arrived, others = refs[:steps], refs[steps : steps + apart]
    (
        cut_current,
        local_load,
        slope,
        own_wave,
        back,
        coupling_high,
        coupling_low,
        image,
        load,
        kept,
        sent,
        sums,
        halo,
    ) = refs[steps + apart :]
    times, half = local_load.shape
    lanes = halo.shape[1]
    nodes = coupling_high.shape[0] - lanes
    slots = steps * CAP
    start = packet_layout(steps, times)[1]
    blank = jnp.zeros((lanes - slots, times), F32)

    def stack(blocks):
        return jnp.transpose(jnp.concatenate([*blocks, blank], axis=0))

    def sender(step, block):
        at = slice((block - 1) * CAP, block * CAP)
        if step == 0:
            return cut_current[at]
        return others[0][step, at] if apart else arrived[step - 1][at, :times]

    current = stack([sender(step, step) for step in range(1, steps + 1)])
    high, low = split(current)
    share = coupled(
        high,
        jnp.concatenate([high, low], axis=0),
        coupling_high,
        coupling_low,
        slice(nodes, None),
        slice(0, half),
    )
    load[...] = local_load[...] + share
    answer = load[...] + slope[...]
    image[...] = answer
    spectrum = dot_split((back[0], back[1]), split(answer))
    kept[...] = spectrum[:times]
    if spectrum.shape[0] > times:
        sent[...] = spectrum[times:]
    lines = [*signed_sums(answer), *signed_sums(own_wave[...])]
    sums[...] = jnp.concatenate(lines + [jnp.zeros((4, half), F32)], axis=0)

    blocks = []
    for step in range(1, steps + 1):
        theirs = jnp.concatenate(
            [sender(step ^ block, block) for block in range(1, steps + 1)], axis=0
        )
        gains = arrived[step - 1][:CAP, start : start + slots]
        image_part = arrived[step - 1][CAP : 2 * CAP, start : start + times]
        there = arrived[step - 1][2 * CAP : 3 * CAP, start : start + times]
        blocks.append(there * (image_part + dot_split(split(gains), split(theirs))))
    halo[...] = stack(blocks)


def second_kernel(
    place,
    halo,
    near_image,
    image,
    back,
    conductances,
    coupling_high,
    coupling_low,
    linear,
    load,
    kept,
    sent,
    current,
):
    times, half = image.shape
    nodes = current.shape[1]
    side = place[0] % 2
    mine, other = half_of(side, half), half_of(1 - side, half)
    for at, field in ((mine, image), (other, near_image)):
        current[:times, at], current[times:, at] = split(conductances[:, at] * field[...])
    load[...] = image[...] * (linear[:, :half] + conductances[:, mine])
    high, low = split(halo[...])
    halo_stacked = jnp.concatenate([high, low], axis=0)
    step = 256
    for block in range(half // step):
        lanes = slice(block * step, (block + 1) * step)
        load[:, lanes] += coupled(
            current[:times], current[...], coupling_high, coupling_low, slice(0, nodes), lanes
        ) + coupled(high, halo_stacked, coupling_high, coupling_low, slice(nodes, None), lanes)
    spectrum = dot_split((back[0], back[1]), split(load[...]))
    kept[...] = spectrum[:times]
    if spectrum.shape[0] > times:
        sent[...] = spectrum[times:]


def merge_kernel(after, kept, arrived, own, near):
    rows = own.shape[0]
    own[...] = kept[:rows] + arrived[:rows]
    near[...] = kept[rows:] + arrived[rows:]


def turned(field, first_pair, half_order):
    count = field.shape[0]
    row = lax.broadcasted_iota(I32, field.shape, 0)
    scaling = (first_pair + row // 2).astype(F32) * (1.0 / half_order)
    above = pltpu.roll(field, count - 1, 0)
    below = pltpu.roll(field, 1, 0)
    return scaling * jnp.where(row % 2 == 0, above, -below)


def join(target, side, own, near):
    half = own.shape[1]
    target[:, half_of(side, half)] = own
    target[:, half_of(1 - side, half)] = near


def guess(cross, squares):
    ratio = cross / jnp.where(squares > 0.0, squares, 1.0)
    return jnp.clip(jnp.where(squares > 0.0, ratio, 0.0), -40.0, 40.0)


def products_kernel(
    place,
    vector,
    load,
    second_load,
    image,
    wave,
    dual,
    dual_slope,
    sums,
    scalars,
    *,
    length,
):
    start, first = wave[...], load[...]
    field = vector[...]
    coeff = guess(scalar_sum(start * image[...]), scalar_sum(start * start))
    rest = image[...] - coeff * start
    change = second_load[...] - coeff * first
    start_sums = [sums[line + 2 : line + 3] for line in (0, 1)]
    rest_sums = [sums[line : line + 1] - coeff * start_sums[line] for line in (0, 1)]
    start_ends, rest_ends, first_ends, change_ends = (
        signed_sums(values) for values in (start, rest, first, change)
    )

    def mixed(values, value_sums, others, other_ends):
        ends = value_sums[0] * other_ends[0] + value_sums[1] * other_ends[1]
        return scalar_sum(values * others) * (2.0 / length) - scalar_sum(ends) * (
            1.0 / length / length
        )

    found = [
        coeff,
        scalar_sum(field * field),
        scalar_sum(dual[...] * rest),
        scalar_sum(dual[...] * start),
        mixed(rest, rest_sums, rest, rest_ends),
        mixed(rest, rest_sums, start, start_ends) + mixed(start, start_sums, rest, rest_ends),
        mixed(start, start_sums, start, start_ends),
        scalar_sum(dual[...] * change - dual_slope[...] * rest),
        scalar_sum(dual[...] * first - dual_slope[...] * start),
        mixed(rest, rest_sums, change, change_ends),
        mixed(rest, rest_sums, first, first_ends) + mixed(start, start_sums, change, change_ends),
        mixed(start, start_sums, first, first_ends),
    ]
    device = place[1] * place[3] + place[0]
    lane = lax.broadcasted_iota(I32, scalars.shape, 1)
    column = jnp.concatenate(found + [jnp.zeros((4, 1), F32)], axis=0)
    scalars[...] = jnp.where(lane == device, column, 0.0)


def settle_kernel(place, own_image, near_image, vector, capacity, answer, slope, skew, *, length):
    rows = vector.shape[0]
    first_pair = place[0] * (rows // 2)
    join(answer, place[0] % 2, own_image[...], near_image[...])
    field, start = answer[...], vector[...]
    slope[...] = capacity[...] * turned(field, first_pair, length // 2)
    start_slope = capacity[...] * turned(start, first_pair, length // 2)
    products = [
        scalar_sum(field * slope[...]),
        scalar_sum(field * start_slope + start * slope[...]),
        scalar_sum(start * start_slope),
        jnp.zeros((5, 1), F32),
    ]
    skew[...] = jnp.broadcast_to(jnp.concatenate(products, axis=0), skew.shape)


def last_kernel(
    gathered,
    vector,
    answer,
    slope,
    skew,
    place,
    own_part,
    near_part,
    basis_two,
    next_residue,
    *,
    entries,
    devices,
):
    side = place[0] % 2
    own = [gathered[line : line + 1, :] for line in range(12)]

    def everywhere(values):
        return jnp.sum(values, axis=1, keepdims=True) / entries

    scale_square = everywhere(own[1]) + EPSILON
    coeff = everywhere(own[2] + own[0] * own[3]) / scale_square
    near = own[0] - coeff
    rest_square = everywhere(own[4] + near * (own[5] + near * own[6]))
    along_one = everywhere(own[7] + near * own[8])
    along_two = everywhere(own[9] + near * (own[10] + near * own[11]))
    turn = skew[0:1, :1] - coeff * (skew[1:2, :1] - coeff * skew[2:3, :1])
    along_two = along_two + turn * (devices / entries)
    scale = jnp.sqrt(scale_square)
    second_norm = jnp.sqrt(jnp.maximum(rest_square, 0.0) / scale_square + EPSILON)
    inverse = 1.0 / (second_norm * scale)
    along_one = along_one * inverse / scale_square
    along_two = along_two * inverse * inverse
    join(next_residue, side, own_part[...], near_part[...])
    second = (answer[...] - coeff * vector[...]) * inverse
    basis_two[...] = second
    next_residue[...] = (
        (next_residue[...] + slope[...] - coeff * answer[...]) * inverse
        - along_one * vector[...]
        - along_two * second
    )


VMEM = pl.BlockSpec(memory_space=pltpu.VMEM)
SMEM = pl.BlockSpec(memory_space=pltpu.SMEM)


HBM = pl.BlockSpec(memory_space=pltpu.HBM)


def run(kernel, name, specs, operands, outs, scratch=(), micros=1, room=12):
    return pl.pallas_call(
        kernel,
        out_shape=[pltpu.VMEM(shape, dtype) for shape, dtype in outs],
        in_specs=specs,
        out_specs=[VMEM] * len(outs),
        scratch_shapes=list(scratch),
        compiler_params=pltpu.CompilerParams(vmem_limit_bytes=room * 2**20),
        cost_estimate=pl.CostEstimate(
            flops=0, bytes_accessed=int(micros * 3e6), transcendentals=0
        ),
        name=name,
    )(*operands)


def swap(value, mask):
    count = lax.axis_size("samples")
    return lax.ppermute(value, "samples", [(at, at ^ mask) for at in range(count)])


def trade(value, mask):
    count = lax.axis_size("nodes")
    return lax.ppermute(value, "nodes", [(at, at ^ mask) for at in range(count)])


def total(value, axis):
    count, stride = lax.axis_size(axis), 1
    while stride < count:
        radix = 4 if count // stride % 4 == 0 else 2
        others = [
            lax.ppermute(value, axis, [(at, at ^ (step * stride)) for at in range(count)])
            for step in range(1, radix)
        ]
        value = value + functools.reduce(jnp.add, others)
        stride *= radix
    return value


def send_groups(kept, sent):
    times = kept.shape[0]
    count = lax.axis_size("samples") // 2
    blocks = {0: kept}
    for group in range(1, count):
        blocks[group] = sent[(group - 1) * times : group * times] if count > 2 else sent
    bit = count // 2
    while bit > 1:
        for group in [name for name in blocks if name & bit]:
            blocks[group ^ bit] = blocks[group ^ bit] + swap(blocks.pop(group), 2 * bit)
        bit //= 2
    return blocks[0], swap(blocks[1], 2) if count > 1 else jnp.zeros_like(kept)


def merge(after, kept, arrived):
    half_block = ((kept.shape[0] // 2, kept.shape[1]), F32)
    own, near = run(
        merge_kernel, "merge", [VMEM] * 3, (after, kept, arrived), [half_block, half_block]
    )
    return own, swap(near, 1)


def shards(
    vector, operating, table, linear, capacity, weights, degree, neighbours, boundary, send_list
):
    rows, nodes = vector.shape
    parts, node_groups = lax.axis_size("samples"), lax.axis_size("nodes")
    length, half, times = rows * parts, nodes // 2, 2 * rows
    entries = float(length * nodes * node_groups)
    steps = node_groups - 1
    slots = steps * CAP
    lanes = -(-slots // LANES) * LANES
    sources, width = nodes + lanes, half + lanes
    place = jnp.stack(
        [
            lax.axis_index("samples"),
            lax.axis_index("nodes"),
            jnp.int32(node_groups),
            jnp.int32(parts),
        ]
    ).astype(I32)
    forward, back = (jnp.asarray(table) for table in transform_tables(length, parts))
    linear, capacity, degree, table = (
        value.reshape(1, -1) for value in (linear, capacity, degree, table)
    )

    slot_count = weights.shape[0]
    (
        coupling_high,
        coupling_low,
        picked,
        linear_wide,
        capacity_wide,
        capacity,
        cut_halo,
        table,
        own_operating,
        own_vector,
        forward,
        back,
    ) = run(
        prepare_kernel,
        "prepare",
        [SMEM] + [HBM] * 12,
        (place,)
        + tuple(
            pltpu.with_memory_space_constraint(value, pltpu.HBM)
            for value in (neighbours, weights, degree, linear, capacity, send_list, boundary)
            + (table, operating, vector, forward, back)
        ),
        [
            ((sources, width), BF16),
            ((sources, width), BF16),
            ((nodes, lanes), BF16),
            ((1, width), F32),
            ((1, width), F32),
            ((1, nodes), F32),
            ((lanes, lanes), F32),
            (table.shape, F32),
            ((rows, nodes), F32),
            ((rows, nodes), F32),
            (forward.shape[1:], BF16),
            (back.shape[1:], BF16),
        ],
        scratch=[
            pltpu.VMEM((slot_count, nodes), I32),
            pltpu.VMEM((slot_count, nodes), F32),
            pltpu.VMEM((1, nodes), I32),
            pltpu.VMEM((1, nodes), F32),
            pltpu.SMEM(send_list.shape, I32),
            pltpu.SMEM(boundary.shape, I32),
            pltpu.VMEM((slot_count, width), I32),
            pltpu.VMEM((slot_count, width), F32),
            pltpu.SemaphoreType.DMA((12,)),
        ],
        micros=8,
    )
    near_operating = swap(operating, 1)
    vectors, bit = [vector], parts // 2
    while bit > 1:
        vectors = vectors + [swap(piece, bit) for piece in vectors]
        bit //= 2
    far = len(vectors) - 1
    if far:
        vectors[1:] = run(
            relay_kernel,
            "relay",
            [VMEM] * (far + 1),
            (cut_halo, *vectors[1:]),
            [((rows, nodes), F32)] * far,
        )
    vectors = vectors + [swap(piece, 1) for piece in vectors]
    vectors[0] = own_vector
    (conductances,) = run(
        conductance_kernel,
        "conductance",
        [SMEM] + [VMEM] * 4,
        (place, near_operating, own_operating, table, picked),
        [((times, sources), F32)],
        micros=1,
    )

    wide = ((times, half), F32)
    shared, start = packet_layout(steps, times)
    packet = (
        max(slots if shared else 0, 3 * CAP),
        -(-(start + max(times, slots)) // LANES) * LANES,
    )
    field_high, field_low, wave, current, cut_current, *sent = run(
        functools.partial(wave_kernel, pieces=parts),
        "wave",
        [VMEM] * (parts + 8),
        (*vectors, forward, conductances, picked, coupling_high, coupling_low)
        + (linear_wide, capacity_wide, cut_halo),
        [
            ((length, sources), BF16),
            ((length, sources), BF16),
            ((times, sources), F32),
            ((2 * times, nodes), BF16),
            ((lanes, times), F32),
        ]
        + [(packet, F32)] * steps,
        micros=2,
    )
    arrived = [trade(packet, step + 1) for step, packet in enumerate(sent)]
    others = []
    if not shared:
        gathered = lax.all_gather(cut_current, "nodes")
        distance = jnp.arange(node_groups, dtype=I32)
        others = [gathered[lax.axis_index("nodes") ^ distance]]
    local_load, slope, own_wave, dual, dual_slope = run(
        local_kernel,
        "local",
        [VMEM] * 10 + [SMEM],
        (field_high, field_low, forward, wave, current, conductances)
        + (coupling_high, coupling_low, linear_wide, capacity_wide, place),
        [wide] * 5,
        micros=3,
    )
    rest = length - times
    image, load, kept, sent, sums, halo = run(
        functools.partial(first_kernel, steps=steps, apart=len(others)),
        "first",
        [VMEM] * (steps + len(others) + 7),
        (*arrived, *others, cut_current, local_load, slope, own_wave, back, coupling_high, coupling_low),
        [wide, wide, wide, ((max(rest, 8), half), F32), ((8, half), F32), ((times, lanes), F32)],
        micros=1,
    )
    near_image = swap(image, 1)
    bit = 2
    while bit < parts:
        sums = sums + swap(sums, bit)
        bit *= 2
    kept, arrived = send_groups(kept, sent)
    second_load, second_kept, second_sent = run(
        second_kernel,
        "second",
        [SMEM] + [VMEM] * 8,
        (place, halo, near_image, image, back, conductances)
        + (coupling_high, coupling_low, linear_wide),
        [wide, wide, ((max(rest, 8), half), F32)],
        scratch=[pltpu.VMEM((2 * times, nodes), BF16)],
        micros=3,
    )
    gathered = -(-node_groups * parts // LANES) * LANES
    (scalars,) = run(
        functools.partial(products_kernel, length=length),
        "products",
        [SMEM] + [VMEM] * 8,
        (place, own_vector, load, second_load, image, own_wave, dual, dual_slope, sums),
        [((16, gathered), F32)],
        micros=1,
    )
    second_kept, second_arrived = send_groups(second_kept, second_sent)
    own_image, near_image = merge(scalars, kept, arrived)
    scalars = total(scalars, "nodes")
    answer, slope, skew = run(
        functools.partial(settle_kernel, length=length),
        "settle",
        [SMEM] + [VMEM] * 4,
        (place, own_image, near_image, own_vector, capacity),
        [((rows, nodes), F32), ((rows, nodes), F32), ((8, LANES), F32)],
        micros=1,
    )
    own_part, near_part = merge(scalars, second_kept, second_arrived)
    scalars = total(scalars, "samples")
    field = jax.ShapeDtypeStruct((rows, nodes), F32)
    return tuple(
        pl.pallas_call(
            functools.partial(
                last_kernel, entries=entries, devices=float(node_groups * parts)
            ),
            out_shape=[field, field],
            in_specs=[VMEM] * 5 + [SMEM] + [VMEM] * 2,
            out_specs=[VMEM] * 2,
            compiler_params=pltpu.CompilerParams(vmem_limit_bytes=12 * 2**20),
            name="last",
        )(scalars, own_vector, answer, slope, skew, place, own_part, near_part)
    )


def solution(mesh):
    return jax.shard_map(
        shards,
        mesh=mesh,
        in_specs=(
            P("samples", ("copies", "nodes")),
            P("samples", ("copies", "nodes")),
            P(),
            P("nodes"),
            P("nodes"),
            P(None, "nodes"),
            P("nodes"),
            P(None, "nodes"),
            P("nodes"),
            P("nodes"),
        ),
        out_specs=(P("samples", ("copies", "nodes")), P("samples", ("copies", "nodes"))),
        check_vma=False,
    )
```

```python
import functools
import math

import jax
import jax.numpy as jnp
import numpy as np
from jax import lax
from jax.experimental import pallas as pl
from jax.experimental.pallas import tpu as pltpu
from jax.sharding import PartitionSpec as P

CAP = 16
EPSILON = 1e-06
LANES = 128
BF16 = jnp.bfloat16
F32 = jnp.float32
I32 = jnp.int32


def spectral_tables(length):
    indices = np.arange(length)
    frequency = np.where(indices == 1, length // 2, indices // 2)
    angles = (indices[:, None] * frequency[None, :] % length) * (2.0 * math.pi / length)
    cosine_column = (indices % 2 == 0) | (indices == 1)
    synthesis = np.where(cosine_column[None, :], np.cos(angles), np.sin(angles))
    factor = np.where(indices < 2, 1.0 / length, 2.0 / length)
    analysis = synthesis.T * factor[:, None]
    turn = np.zeros((length, length))
    for pair in range(length // 2):
        turn[2 * pair, 2 * pair + 1] = pair / (length // 2)
        turn[2 * pair + 1, 2 * pair] = -pair / (length // 2)
    return synthesis, analysis, turn


def halves(table):
    high = table.astype(np.float32).astype(BF16)
    low = (table - high.astype(np.float64)).astype(np.float32).astype(BF16)
    return np.stack([high, low])


def piece_order(count):
    masks, bit = [0], count // 2
    while bit:
        masks = masks + [mask ^ bit for mask in masks]
        bit //= 2
    return masks


def transform_tables(length, parts):
    synthesis, analysis, turn = spectral_tables(length)
    slope, dual_slope = synthesis @ turn, analysis.T @ turn
    rows = length // parts
    forward, back = [], []
    for place in range(parts):
        times = np.arange(place // 2 * 2 * rows, (place // 2 + 1) * 2 * rows)
        block = lambda owner: np.arange(owner * rows, (owner + 1) * rows)
        coefs = np.concatenate([block(place ^ mask) for mask in piece_order(parts)])
        forward.append(
            np.concatenate(
                [
                    synthesis[np.ix_(times, coefs)],
                    slope[np.ix_(times, coefs)],
                    analysis[np.ix_(coefs, times)].T,
                    dual_slope[np.ix_(times, coefs)],
                ]
            )
        )
        sent = np.concatenate(
            [block(place ^ mask ^ side) for side in (0, 1) for mask in range(0, parts, 2)]
        )
        back.append(analysis[np.ix_(sent, times)])
    return (
        np.moveaxis(halves(np.stack(forward)), 0, 1),
        np.moveaxis(halves(np.stack(back)), 0, 1),
    )


def split(values):
    high = values.astype(BF16)
    return high, (values - high.astype(F32)).astype(BF16)


def dot(first, second):
    return jnp.dot(first, second, preferred_element_type=F32)


def dot_split(first, second):
    (first_high, first_low), (second_high, second_low) = first, second
    rows = first_high.shape[0]
    both = dot(jnp.concatenate([first_high, first_low], axis=0), second_high)
    return both[:rows] + both[rows:] + dot(first_high, second_low)


def lane_sums(values):
    rows, lanes = values.shape
    step = 8 if rows % 8 == 0 else rows
    total = functools.reduce(
        jnp.add,
        [
            values[row : row + step, lane : lane + LANES]
            for row in range(0, rows, step)
            for lane in range(0, lanes, LANES)
        ],
    )
    return jnp.sum(total, axis=0, keepdims=True)


def half_of(side, half):
    return pl.ds(pl.multiple_of(side * half, LANES), half)


def scalar_sum(values):
    return jnp.sum(lane_sums(values), axis=1, keepdims=True)


def pick(values, picked):
    high, _ = split(values)
    middle, low = split(values - high.astype(F32))
    rows = values.shape[0]
    found = dot(jnp.concatenate([high, middle, low], axis=0), picked)
    return found[:rows] + (found[rows : 2 * rows] + found[2 * rows :])


def conductance(operating, table):
    points = table.shape[1]
    spread = jnp.concatenate([table, jnp.zeros((1, LANES - points), F32)], axis=1)
    spread = jnp.broadcast_to(spread, (operating.shape[0], LANES))
    pieces = []
    for block in range(operating.shape[1] // LANES):
        scaled = (operating[:, block * LANES : (block + 1) * LANES] + 4.0) * ((points - 1) / 8.0)
        knot = jnp.clip(jnp.floor(scaled), 0.0, points - 2.0)
        weight = scaled - knot
        place = knot.astype(I32)
        left = jnp.take_along_axis(spread, place, axis=1, mode="promise_in_bounds")
        right = jnp.take_along_axis(spread, place + 1, axis=1, mode="promise_in_bounds")
        pieces.append(left + weight * (right - left))
    return jnp.concatenate(pieces, axis=1)


def fetch_kernel(
    place_in,
    vector_in,
    neighbours_in,
    weights_in,
    degree_in,
    linear_in,
    capacity_in,
    send_list_in,
    boundary_in,
    table_in,
    operating_in,
    forward_in,
    back_in,
    vector,
    picked,
    linear,
    capacity,
    capacity_all,
    table,
    operating,
    forward,
    back,
    entry_rows,
    weight_rows,
    place,
    neighbours,
    weights,
    degree,
    linear_all,
    send_list,
    boundary,
    copied,
):
    for index in range(4):
        place[index] = place_in[index]
    slots, nodes = neighbours.shape
    lanes = picked.shape[1]
    half = linear.shape[1] - lanes
    node_groups = send_list.shape[0] // CAP
    side, part = place[0] % 2, place[1]
    copies = [
        pltpu.make_async_copy(source, target, copied.at[index])
        for index, (source, target) in enumerate(
            [
                (vector_in, vector),
                (send_list_in, send_list),
                (boundary_in, boundary),
                (neighbours_in, neighbours),
                (weights_in, weights),
                (degree_in, degree),
                (linear_in, linear_all),
                (capacity_in, capacity_all),
                (table_in, table),
                (operating_in, operating),
                (forward_in.at[place[0]], forward),
                (back_in.at[place[0]], back),
            ]
        )
    ]
    for copy in copies:
        copy.start()
    for copy in copies[1:3]:
        copy.wait()

    lane = lax.broadcasted_iota(I32, (8, lanes), 1)

    def name(slot, found):
        target = part ^ (slot // CAP + 1)
        node = boundary[send_list[target * CAP + slot % CAP]]
        return jnp.where(lane == slot, node, found)

    cut_nodes = lax.fori_loop(
        0, (node_groups - 1) * CAP, name, jnp.full((8, lanes), -1, I32), unroll=8
    )
    hit = lax.broadcasted_iota(I32, (nodes, lanes), 0) == cut_nodes[:1]
    picked[...] = jnp.where(hit, 1.0, 0.0).astype(BF16)

    for copy in copies[3:8]:
        copy.wait()
    mine = half_of(side, half)
    entry = neighbours[...]
    remote = entry - nodes
    distance = part ^ (remote >> 4)
    entry = jnp.where(remote < 0, entry, nodes + (distance - 1) * CAP + (remote & 15))
    live = lax.broadcasted_iota(I32, (slots, nodes), 0) < degree[...]
    neighbours[...] = entry
    weights[...] = jnp.where(live, weights[...], 0.0)
    columns = jnp.concatenate(
        [
            entry.astype(F32),
            weights[...],
            linear_all[...],
            capacity_all[...],
            jnp.zeros((6, nodes), F32),
        ],
        axis=0,
    )
    at_cut = pick(columns, picked[...])
    linear[:, :half] = linear_all[:, mine]
    linear[:, half:] = at_cut[2 * slots : 2 * slots + 1]
    capacity[:, :half] = capacity_all[:, mine]
    capacity[:, half:] = at_cut[2 * slots + 1 : 2 * slots + 2]
    entry_rows[:, :half] = neighbours[:, mine]
    entry_rows[:, half:] = at_cut[:slots].astype(I32)
    weight_rows[:, :half] = weights[:, mine]
    weight_rows[:, half:] = at_cut[slots : 2 * slots]
    entries = [entry_rows[slot : slot + 1, :] for slot in range(slots)]
    gains = [weight_rows[slot : slot + 1, :] for slot in range(slots)]
    for slot in range(slots):
        for later in range(slot + 1, slots):
            same = entries[slot] == entries[later]
            gains[slot] = gains[slot] + jnp.where(same, gains[later], 0.0)
            entries[later] = jnp.where(same, -1, entries[later])
    for slot in range(slots):
        entry_rows[slot : slot + 1, :] = entries[slot]
        weight_rows[slot : slot + 1, :] = gains[slot]
    copies[0].wait()
    for copy in copies[8:]:
        copy.wait()


def prepare_kernel(entry_rows, weight_rows, coupling_high, coupling_low, cut_halo):
    slots, width = entry_rows.shape
    sources = coupling_high.shape[0]
    nodes = sources - cut_halo.shape[0]
    half = width - cut_halo.shape[0]
    unroll = 4

    def column_block(block, carry):
        at_lanes = pl.ds(pl.multiple_of(block * LANES, LANES), LANES)
        wide = (CAP, LANES)
        names = [
            jnp.broadcast_to(entry_rows[slot : slot + 1, at_lanes], wide).astype(jnp.int16)
            for slot in range(slots)
        ]
        parts = [
            split(jnp.broadcast_to(weight_rows[slot : slot + 1, at_lanes], wide))
            for slot in range(slots)
        ]

        def source_rows(step, row):
            for inner in range(unroll):
                high = jnp.zeros(wide, BF16)
                low = jnp.zeros(wide, BF16)
                for slot in range(slots):
                    hit = names[slot] == row
                    high = jnp.where(hit, parts[slot][0], high)
                    low = jnp.where(hit, parts[slot][1], low)
                at = pl.ds(pl.multiple_of((step * unroll + inner) * 16, 16), 16)
                coupling_high[at, at_lanes] = high
                coupling_low[at, at_lanes] = low
                row = row + jnp.int16(16)
            return row

        lax.fori_loop(
            0,
            sources // 16 // unroll,
            source_rows,
            lax.broadcasted_iota(I32, wide, 0).astype(jnp.int16),
        )
        return carry

    lax.fori_loop(0, width // LANES, column_block, 0)
    cut_halo[...] = jnp.transpose(
        coupling_high[nodes:, half:].astype(F32) + coupling_low[nodes:, half:].astype(F32)
    )


def relay_kernel(*refs):
    count = (len(refs) - 1) // 2
    for source, target in zip(refs[1 : 1 + count], refs[1 + count :]):
        target[...] = source[...]


def conductance_kernel(place, near_operating, operating, table, picked, conductances):
    rows, nodes = operating.shape
    side = place[0] % 2
    for at, values in ((side, operating), (1 - side, near_operating)):
        conductances[pl.ds(pl.multiple_of(at * rows, 8), rows), :nodes] = conductance(
            values[...], table[...]
        )
    conductances[:, nodes:] = pick(conductances[:, :nodes], picked[...])


def coupled(high, stacked, coupling_high, coupling_low, sources, lanes):
    rows = high.shape[0]
    both = dot(stacked, coupling_high[sources, lanes])
    return both[:rows] + both[rows:] + dot(high, coupling_low[sources, lanes])


def packet_layout(steps, times):
    shared = steps * CAP <= LANES
    return shared, times if shared else 0


def packet_steps(steps):
    return [(2,), (1, 3)] if steps == 3 else [(step,) for step in range(1, steps + 1)]


def wave_kernel(*refs, pieces, steps):
    vectors = refs[1 : 1 + pieces]
    (
        forward,
        conductances,
        picked,
        coupling_high,
        coupling_low,
        linear,
        capacity,
        cut_halo,
        field_high,
        field_low,
        wave,
        current,
        cut_current,
    ) = refs[1 + pieces : 1 + pieces + 13]
    sent = refs[1 + pieces + 13 :]
    side = refs[0][0] % 2
    rows, nodes = vectors[0].shape
    lanes = picked.shape[1]
    times = wave.shape[0]
    half = linear.shape[1] - lanes
    for index in range(pieces):
        at = slice(index * rows, (index + 1) * rows)
        field_high[at, :nodes], field_low[at, :nodes] = split(vectors[index][...])
    field_high[:, nodes:] = dot(field_high[:, :nodes], picked[...]).astype(BF16)
    field_low[:, nodes:] = dot(field_low[:, :nodes], picked[...]).astype(BF16)
    wave[...] = dot_split(
        (forward[0, :times], forward[1, :times]), (field_high[...], field_low[...])
    )
    slope = dot_split(
        (forward[0, times : 2 * times], forward[1, times : 2 * times]),
        (field_high[:, nodes:], field_low[:, nodes:]),
    )
    high, low = split(conductances[:, :nodes] * wave[:, :nodes])
    current[:times] = high
    current[times:] = low
    at_cut = conductances[:, nodes:] * wave[:, nodes:]
    cut_current[...] = jnp.transpose(at_cut)
    image = (
        linear[:, half:] * wave[:, nodes:]
        + at_cut
        + capacity[:, half:] * slope
        + coupled(
            high, current[...], coupling_high, coupling_low, slice(0, nodes), slice(half, None)
        )
    )
    image = jnp.transpose(image)
    at_cut = jnp.transpose(conductances[:, nodes:])
    slots = steps * CAP
    shared, start = packet_layout(steps, times)
    for target, wanted in zip(sent, packet_steps(steps)):
        target[...] = jnp.zeros(target.shape, F32)
        if shared:
            target[:slots, :times] = cut_current[:slots]
        for row, values, size in ((0, cut_halo, slots), (1, image, times), (2, at_cut, times)):
            blocks = [values[(step - 1) * CAP : step * CAP, :size] for step in wanted]
            block = blocks[0] if len(blocks) == 1 else jnp.where(side == 0, *blocks)
            target[row * CAP : (row + 1) * CAP, start : start + size] = block


def local_kernel(
    field_high,
    field_low,
    forward,
    wave,
    current,
    conductances,
    coupling_high,
    coupling_low,
    linear,
    capacity,
    place,
    load,
    slope,
    own_wave,
    dual,
    dual_slope,
):
    times, half = load.shape
    sources = slice(0, current.shape[1])
    mine = half_of(place[0] % 2, half)
    others = dot_split(
        (forward[0, times:], forward[1, times:]), (field_high[:, mine], field_low[:, mine])
    )
    slope[...] = capacity[:, :half] * others[:times]
    dual[...] = others[times : 2 * times]
    dual_slope[...] = capacity[:, :half] * others[2 * times :]
    own_wave[...] = wave[:, mine]
    load[...] = own_wave[...] * (linear[:, :half] + conductances[:, mine])
    high = current[:times]
    step = 256
    for block in range(half // step):
        lanes = slice(block * step, (block + 1) * step)
        load[:, lanes] += coupled(
            high, current[...], coupling_high, coupling_low, sources, lanes
        )


def signed_sums(values):
    rows = values.shape[0]
    folded = functools.reduce(jnp.add, [values[row : row + 8] for row in range(0, rows, 8)])
    even = lax.broadcasted_iota(I32, folded.shape, 0) % 2 == 0
    return (
        jnp.sum(folded, axis=0, keepdims=True),
        jnp.sum(jnp.where(even, folded, -folded), axis=0, keepdims=True),
    )


def analysed(back, load):
    spectrum = dot_split((back[0], back[1]), split(load))
    middle = spectrum.shape[0] // 2
    return spectrum[:middle], spectrum[middle:]


def first_kernel(*refs, steps, apart):
    side, arrived, others = refs[0][0] % 2, refs[1 : steps + 1], refs[steps + 1 : steps + 1 + apart]
    if steps == 3:
        both, own, near = (packet[...] for packet in arrived)
        arrived = [
            jnp.where(side == 0, own, near),
            both,
            jnp.where(side == 0, near, own),
        ]
    (
        cut_current,
        local_load,
        slope,
        own_wave,
        back,
        coupling_high,
        coupling_low,
        image,
        load,
        sums,
        halo,
        kept,
        sent,
    ) = refs[1 + steps + apart :]
    times, half = local_load.shape
    lanes = halo.shape[1]
    nodes = coupling_high.shape[0] - lanes
    slots = steps * CAP
    start = packet_layout(steps, times)[1]
    blank = jnp.zeros((lanes - slots, times), F32)

    def stack(blocks):
        return jnp.transpose(jnp.concatenate([*blocks, blank], axis=0))

    def sender(step, block):
        at = slice((block - 1) * CAP, block * CAP)
        if step == 0:
            return cut_current[at]
        return others[0][step, at] if apart else arrived[step - 1][at, :times]

    current = stack([sender(step, step) for step in range(1, steps + 1)])
    high, low = split(current)
    share = coupled(
        high,
        jnp.concatenate([high, low], axis=0),
        coupling_high,
        coupling_low,
        slice(nodes, None),
        slice(0, half),
    )
    load[...] = local_load[...] + share
    answer = load[...] + slope[...]
    image[...] = answer
    kept[...], sent[...] = analysed(back, answer)
    lines = [*signed_sums(answer), *signed_sums(own_wave[...])]
    sums[...] = jnp.concatenate(lines + [jnp.zeros((4, half), F32)], axis=0)

    currents = []
    for step in range(1, steps + 1):
        theirs = jnp.concatenate(
            [sender(step ^ block, block) for block in range(1, steps + 1)], axis=0
        )
        gains = arrived[step - 1][:CAP, start : start + slots]
        image_part = arrived[step - 1][CAP : 2 * CAP, start : start + times]
        there = arrived[step - 1][2 * CAP : 3 * CAP, start : start + times]
        currents.append(there * (image_part + dot_split(split(gains), split(theirs))))
    halo[...] = stack(currents)


def second_kernel(
    place,
    halo,
    near_image,
    image,
    back,
    conductances,
    coupling_high,
    coupling_low,
    linear,
    load,
    kept,
    sent,
    current,
):
    times, half = image.shape
    nodes = current.shape[1]
    side = place[0] % 2
    mine, other = half_of(side, half), half_of(1 - side, half)
    for at, field in ((mine, image), (other, near_image)):
        current[:times, at], current[times:, at] = split(conductances[:, at] * field[...])
    load[...] = image[...] * (linear[:, :half] + conductances[:, mine])
    high, low = split(halo[...])
    halo_stacked = jnp.concatenate([high, low], axis=0)
    step = 256
    for block in range(half // step):
        lanes = slice(block * step, (block + 1) * step)
        load[:, lanes] += coupled(
            current[:times], current[...], coupling_high, coupling_low, slice(0, nodes), lanes
        ) + coupled(high, halo_stacked, coupling_high, coupling_low, slice(nodes, None), lanes)
    kept[...], sent[...] = analysed(back, load[...])


def sum_kernel(after, *refs):
    total = refs[0][...]
    for value in refs[1:-1]:
        total = total + value[...]
    refs[-1][...] = total


def turned(field, first_pair, half_order):
    count = field.shape[0]
    row = lax.broadcasted_iota(I32, field.shape, 0)
    scaling = (first_pair + row // 2).astype(F32) * (1.0 / half_order)
    above = pltpu.roll(field, count - 1, 0)
    below = pltpu.roll(field, 1, 0)
    return scaling * jnp.where(row % 2 == 0, above, -below)


def combine_kernel(after, place, kept, arrived, *targets):
    half = kept.shape[1]
    rows = targets[0].shape[0]
    side = place[0] % 2
    for index, target in enumerate(targets):
        at = slice(index * rows, (index + 1) * rows)
        target[:, half_of(side, half)] = kept[at]
        target[:, half_of(1 - side, half)] = arrived[at]


def joined(parts):
    return functools.reduce(jnp.add, [part[...] for part in parts])


def guess(cross, squares):
    ratio = cross / jnp.where(squares > 0.0, squares, 1.0)
    return jnp.clip(jnp.where(squares > 0.0, ratio, 0.0), -40.0, 40.0)


def products_kernel(
    place,
    vector,
    load,
    second_load,
    image,
    wave,
    dual,
    dual_slope,
    own_sums,
    far_sums,
    scalars,
    *,
    length,
):
    start, first = wave[...], load[...]
    field, sums = vector[...], own_sums[...] + far_sums[...]
    coeff = guess(scalar_sum(start * image[...]), scalar_sum(start * start))
    rest = image[...] - coeff * start
    change = second_load[...] - coeff * first
    start_sums = [sums[line + 2 : line + 3] for line in (0, 1)]
    rest_sums = [sums[line : line + 1] - coeff * start_sums[line] for line in (0, 1)]
    start_ends, rest_ends, first_ends, change_ends = (
        signed_sums(values) for values in (start, rest, first, change)
    )

    def mixed(values, value_sums, others, other_ends):
        ends = value_sums[0] * other_ends[0] + value_sums[1] * other_ends[1]
        return lane_sums(values * others) * (2.0 / length) - lane_sums(ends) * (
            1.0 / length / length
        )

    found = [
        lane_sums(field * field),
        lane_sums(dual[...] * rest),
        lane_sums(dual[...] * start),
        mixed(rest, rest_sums, rest, rest_ends),
        mixed(rest, rest_sums, start, start_ends) + mixed(start, start_sums, rest, rest_ends),
        mixed(start, start_sums, start, start_ends),
        lane_sums(dual[...] * change - dual_slope[...] * rest),
        lane_sums(dual[...] * first - dual_slope[...] * start),
        mixed(rest, rest_sums, change, change_ends),
        mixed(rest, rest_sums, first, first_ends) + mixed(start, start_sums, change, change_ends),
        mixed(start, start_sums, first, first_ends),
    ]
    device = place[1] * place[3] + place[0]
    lane = lax.broadcasted_iota(I32, scalars.shape, 1)
    column = jnp.concatenate(found + [jnp.zeros((5, LANES), F32)], axis=0)
    column = jnp.sum(column, axis=1, keepdims=True)
    line = lax.broadcasted_iota(I32, column.shape, 0)
    column = jnp.where(line == len(found), coeff, column)
    scalars[...] = jnp.where(lane == device, column, 0.0)


def settle_kernel(place, vector, capacity, *refs, length):
    *parts, answer, slope, skew = refs
    rows = vector.shape[0]
    first_pair = place[0] * (rows // 2)
    answer[...] = joined(parts)
    field, start = answer[...], vector[...]
    slope[...] = capacity[...] * turned(field, first_pair, length // 2)
    start_slope = capacity[...] * turned(start, first_pair, length // 2)
    products = [
        scalar_sum(field * slope[...]),
        scalar_sum(field * start_slope + start * slope[...]),
        scalar_sum(start * start_slope),
        jnp.zeros((5, 1), F32),
    ]
    skew[...] = jnp.broadcast_to(jnp.concatenate(products, axis=0), skew.shape)


def last_kernel(
    gathered,
    vector,
    answer,
    slope,
    skew,
    *refs,
    entries,
    devices,
):
    *parts, basis_two, next_residue = refs
    own = [gathered[line : line + 1, :] for line in range(12)]
    local = own.pop()

    def everywhere(values):
        return jnp.sum(values, axis=1, keepdims=True) / entries

    scale_square = everywhere(own[0]) + EPSILON
    coeff = everywhere(own[1] + local * own[2]) / scale_square
    near = local - coeff
    rest_square = everywhere(own[3] + near * (own[4] + near * own[5]))
    along_one = everywhere(own[6] + near * own[7])
    along_two = everywhere(own[8] + near * (own[9] + near * own[10]))
    turn = skew[0:1, :1] - coeff * (skew[1:2, :1] - coeff * skew[2:3, :1])
    along_two = along_two + turn * (devices / entries)
    scale = jnp.sqrt(scale_square)
    second_norm = jnp.sqrt(jnp.maximum(rest_square, 0.0) / scale_square + EPSILON)
    inverse = 1.0 / (second_norm * scale)
    along_one = along_one * inverse / scale_square
    along_two = along_two * inverse * inverse
    second = (answer[...] - coeff * vector[...]) * inverse
    basis_two[...] = second
    next_residue[...] = (
        (joined(parts) + slope[...] - coeff * answer[...]) * inverse
        - along_one * vector[...]
        - along_two * second
    )


VMEM = pl.BlockSpec(memory_space=pltpu.VMEM)
SMEM = pl.BlockSpec(memory_space=pltpu.SMEM)


HBM = pl.BlockSpec(memory_space=pltpu.HBM)


def run(kernel, name, specs, operands, outs, scratch=(), micros=1, room=12, spaces=None):
    spaces = spaces or [pltpu.VMEM] * len(outs)
    return pl.pallas_call(
        kernel,
        out_shape=[space(shape, dtype) for space, (shape, dtype) in zip(spaces, outs)],
        in_specs=specs,
        out_specs=[pl.BlockSpec(memory_space=space) for space in spaces],
        scratch_shapes=list(scratch),
        compiler_params=pltpu.CompilerParams(vmem_limit_bytes=room * 2**20),
        cost_estimate=pl.CostEstimate(
            flops=0, bytes_accessed=int(micros * 3e6), transcendentals=0
        ),
        name=name,
    )(*operands)


def swap(value, mask):
    count = lax.axis_size("samples")
    return lax.ppermute(value, "samples", [(at, at ^ mask) for at in range(count)])


def trade(value, masks):
    count, parts = lax.axis_size("nodes"), lax.axis_size("samples")
    pairs = [
        (at * parts + which, (at ^ masks[which % len(masks)]) * parts + which)
        for at in range(count)
        for which in range(parts)
    ]
    return lax.ppermute(value, ("nodes", "samples"), pairs)


def add(after, terms):
    (value,) = run(
        sum_kernel,
        "sum",
        [VMEM] * (len(terms) + 1),
        (after, *terms),
        [(terms[0].shape, F32)],
    )
    return value


def exchange(value, axis, after):
    count, stride, terms = lax.axis_size(axis), 1, [value]
    while stride < count:
        if stride > 1:
            value = add(after, terms)
        radix = 4 if count // stride % 4 == 0 else 2
        terms = [value] + [
            lax.ppermute(value, axis, [(at, at ^ (step * stride)) for at in range(count)])
            for step in range(radix - 1, 0, -1)
        ]
        stride *= radix
    return terms


def hand_out(after, place, kept, arrived):
    count = lax.axis_size("samples") // 2
    field = ((kept.shape[0] // count, 2 * kept.shape[1]), F32)
    parts = run(
        combine_kernel,
        "combine",
        [VMEM, SMEM] + [VMEM] * 2,
        (after, place, kept, arrived),
        [field] * count,
    )
    return [parts[0]] + [swap(part, 2 * mask) for mask, part in enumerate(parts) if mask]


def shards(
    vector, operating, table, linear, capacity, weights, degree, neighbours, boundary, send_list
):
    rows, nodes = vector.shape
    parts, node_groups = lax.axis_size("samples"), lax.axis_size("nodes")
    length, half, times = rows * parts, nodes // 2, 2 * rows
    entries = float(length * nodes * node_groups)
    steps = node_groups - 1
    slots = steps * CAP
    lanes = -(-slots // LANES) * LANES
    sources, width = nodes + lanes, half + lanes
    place = jnp.stack(
        [
            lax.axis_index("samples"),
            lax.axis_index("nodes"),
            jnp.int32(node_groups),
            jnp.int32(parts),
        ]
    ).astype(I32)
    forward, back = (jnp.asarray(table) for table in transform_tables(length, parts))
    linear, capacity, degree, table = (
        value.reshape(1, -1) for value in (linear, capacity, degree, table)
    )

    slot_count = weights.shape[0]
    (
        own_vector,
        picked,
        linear_wide,
        capacity_wide,
        capacity,
        table,
        own_operating,
        forward,
        back,
        entry_rows,
        weight_rows,
        place,
    ) = run(
        fetch_kernel,
        "fetch",
        [SMEM] + [HBM] * 12,
        (place,)
        + tuple(
            pltpu.with_memory_space_constraint(value, pltpu.HBM)
            for value in (vector, neighbours, weights, degree, linear, capacity, send_list)
            + (boundary, table, operating, forward, back)
        ),
        [
            ((rows, nodes), F32),
            ((nodes, lanes), BF16),
            ((1, width), F32),
            ((1, width), F32),
            ((1, nodes), F32),
            (table.shape, F32),
            ((rows, nodes), F32),
            (forward.shape[1:], BF16),
            (back.shape[1:], BF16),
            ((slot_count, width), I32),
            ((slot_count, width), F32),
            ((4,), I32),
        ],
        scratch=[
            pltpu.VMEM((slot_count, nodes), I32),
            pltpu.VMEM((slot_count, nodes), F32),
            pltpu.VMEM((1, nodes), I32),
            pltpu.VMEM((1, nodes), F32),
            pltpu.SMEM(send_list.shape, I32),
            pltpu.SMEM(boundary.shape, I32),
            pltpu.SemaphoreType.DMA((12,)),
        ],
        micros=2,
        spaces=[pltpu.VMEM] * 11 + [pltpu.SMEM],
    )
    coupling_high, coupling_low, cut_halo = run(
        prepare_kernel,
        "prepare",
        [VMEM] * 2,
        (entry_rows, weight_rows),
        [((sources, width), BF16), ((sources, width), BF16), ((lanes, lanes), F32)],
        micros=7,
    )
    near_operating = swap(operating, 1)
    vectors, bit = [vector], parts // 2
    while bit > 1:
        vectors = vectors + [swap(piece, bit) for piece in vectors]
        bit //= 2
    far = len(vectors) - 1
    if far:
        vectors[1:] = run(
            relay_kernel,
            "relay",
            [VMEM] * (far + 1),
            (cut_halo, *vectors[1:]),
            [((rows, nodes), F32)] * far,
        )
    vectors = vectors + [swap(piece, 1) for piece in vectors]
    vectors[0] = own_vector
    (conductances,) = run(
        conductance_kernel,
        "conductance",
        [SMEM] + [VMEM] * 4,
        (place, near_operating, own_operating, table, picked),
        [((times, sources), F32)],
        micros=1,
    )

    wide = ((times, half), F32)
    shared, start = packet_layout(steps, times)
    packet = (
        max(slots if shared else 0, 3 * CAP),
        -(-(start + max(times, slots)) // LANES) * LANES,
    )
    field_high, field_low, wave, current, cut_current, *sent = run(
        functools.partial(wave_kernel, pieces=parts, steps=steps),
        "wave",
        [SMEM] + [VMEM] * (parts + 8),
        (place, *vectors, forward, conductances, picked, coupling_high, coupling_low)
        + (linear_wide, capacity_wide, cut_halo),
        [
            ((length, sources), BF16),
            ((length, sources), BF16),
            ((times, sources), F32),
            ((2 * times, nodes), BF16),
            ((lanes, times), F32),
        ]
        + [(packet, F32)] * len(packet_steps(steps)),
        micros=2,
    )
    arrived = [trade(packet, masks) for packet, masks in zip(sent, packet_steps(steps))]
    if steps == 3:
        arrived.append(swap(arrived[-1], 1))
    others = []
    if not shared:
        gathered = lax.all_gather(cut_current, "nodes")
        distance = jnp.arange(node_groups, dtype=I32)
        others = [gathered[lax.axis_index("nodes") ^ distance]]
    local_load, slope, own_wave, dual, dual_slope = run(
        local_kernel,
        "local",
        [VMEM] * 10 + [SMEM],
        (field_high, field_low, forward, wave, current, conductances)
        + (coupling_high, coupling_low, linear_wide, capacity_wide, place),
        [wide] * 5,
        micros=3,
    )
    block = ((length // 2, half), F32)
    image, load, own_sums, halo, kept, sent = run(
        functools.partial(first_kernel, steps=steps, apart=len(others)),
        "first",
        [SMEM] + [VMEM] * (steps + len(others) + 7),
        (place, *arrived, *others, cut_current, local_load, slope, own_wave, back, coupling_high, coupling_low),
        [wide, wide, ((8, half), F32), ((times, lanes), F32), block, block],
        micros=1,
    )
    near_image = swap(image, 1)
    bit = 2
    while 2 * bit < parts:
        own_sums = own_sums + swap(own_sums, bit)
        bit *= 2
    far_sums = swap(own_sums, bit) if bit < parts else jnp.zeros_like(own_sums)
    arrived = swap(sent, 1)

    second_load, second_kept, second_sent = run(
        second_kernel,
        "second",
        [SMEM] + [VMEM] * 8,
        (place, halo, near_image, image, back, conductances)
        + (coupling_high, coupling_low, linear_wide),
        [wide, block, block],
        scratch=[pltpu.VMEM((2 * times, nodes), BF16)],
        micros=3,
    )
    answer_parts = hand_out(second_load, place, kept, arrived)
    (second_sent,) = run(
        relay_kernel,
        "relay",
        [VMEM] * 2,
        (far_sums, second_sent),
        [(second_sent.shape, F32)],
    )
    second_arrived = swap(second_sent, 1)
    gathered = -(-node_groups * parts // LANES) * LANES
    (scalars,) = run(
        functools.partial(products_kernel, length=length),
        "products",
        [SMEM] + [VMEM] * 9,
        (place, own_vector, load, second_load, image, own_wave, dual, dual_slope)
        + (own_sums, far_sums),
        [((16, gathered), F32)],
        micros=1,
    )
    second_parts = hand_out(scalars, place, second_kept, second_arrived)
    scalars = add(cut_halo, exchange(scalars, "nodes", cut_halo))
    answer, slope, skew = run(
        functools.partial(settle_kernel, length=length),
        "settle",
        [SMEM] + [VMEM] * (len(answer_parts) + 2),
        (place, own_vector, capacity, *answer_parts),
        [((rows, nodes), F32), ((rows, nodes), F32), ((8, LANES), F32)],
        micros=1,
    )
    scalars = add(skew, exchange(scalars, "samples", cut_halo))
    field = jax.ShapeDtypeStruct((rows, nodes), F32)
    return tuple(
        pl.pallas_call(
            functools.partial(
                last_kernel, entries=entries, devices=float(node_groups * parts)
            ),
            out_shape=[field, field],
            in_specs=[VMEM] * (5 + len(second_parts)),
            out_specs=[VMEM] * 2,
            compiler_params=pltpu.CompilerParams(vmem_limit_bytes=12 * 2**20),
            name="last",
        )(scalars, own_vector, answer, slope, skew, *second_parts)
    )


def solution(mesh):
    return jax.shard_map(
        shards,
        mesh=mesh,
        in_specs=(
            P("samples", ("copies", "nodes")),
            P("samples", ("copies", "nodes")),
            P(),
            P("nodes"),
            P("nodes"),
            P(None, "nodes"),
            P("nodes"),
            P(None, "nodes"),
            P("nodes"),
            P("nodes"),
        ),
        out_specs=(P("samples", ("copies", "nodes")), P("samples", ("copies", "nodes"))),
        check_vma=False,
    )
```

```python
import functools
import math

import jax
import jax.numpy as jnp
import numpy as np
from jax import lax
from jax.experimental import pallas as pl
from jax.experimental.pallas import tpu as pltpu
from jax.sharding import PartitionSpec as P

CAP = 16
EPSILON = 1e-06
LANES = 128
BF16 = jnp.bfloat16
F32 = jnp.float32
I32 = jnp.int32


def spectral_tables(length):
    indices = np.arange(length)
    frequency = np.where(indices == 1, length // 2, indices // 2)
    angles = (indices[:, None] * frequency[None, :] % length) * (2.0 * math.pi / length)
    cosine_column = (indices % 2 == 0) | (indices == 1)
    synthesis = np.where(cosine_column[None, :], np.cos(angles), np.sin(angles))
    factor = np.where(indices < 2, 1.0 / length, 2.0 / length)
    analysis = synthesis.T * factor[:, None]
    turn = np.zeros((length, length))
    for pair in range(length // 2):
        turn[2 * pair, 2 * pair + 1] = pair / (length // 2)
        turn[2 * pair + 1, 2 * pair] = -pair / (length // 2)
    return synthesis, analysis, turn


def halves(table):
    high = table.astype(np.float32).astype(BF16)
    low = (table - high.astype(np.float64)).astype(np.float32).astype(BF16)
    return np.stack([high, low])


def piece_order(count):
    masks, bit = [0], count // 2
    while bit:
        masks = masks + [mask ^ bit for mask in masks]
        bit //= 2
    return masks


def transform_tables(length, parts):
    synthesis, analysis, turn = spectral_tables(length)
    slope, dual_slope = synthesis @ turn, analysis.T @ turn
    rows = length // parts
    forward, back = [], []
    for place in range(parts):
        times = np.arange(place // 2 * 2 * rows, (place // 2 + 1) * 2 * rows)
        block = lambda owner: np.arange(owner * rows, (owner + 1) * rows)
        coefs = np.concatenate([block(place ^ mask) for mask in piece_order(parts)])
        forward.append(
            np.concatenate(
                [
                    synthesis[np.ix_(times, coefs)],
                    slope[np.ix_(times, coefs)],
                    analysis[np.ix_(coefs, times)].T,
                    dual_slope[np.ix_(times, coefs)],
                ]
            )
        )
        sent = np.concatenate(
            [block(place ^ mask ^ side) for side in (0, 1) for mask in range(0, parts, 2)]
        )
        back.append(analysis[np.ix_(sent, times)])
    return (
        np.moveaxis(halves(np.stack(forward)), 0, 1),
        np.moveaxis(halves(np.stack(back)), 0, 1),
    )


def split(values):
    high = values.astype(BF16)
    return high, (values - high.astype(F32)).astype(BF16)


def dot(first, second):
    return jnp.dot(first, second, preferred_element_type=F32)


def dot_split(first, second):
    (first_high, first_low), (second_high, second_low) = first, second
    rows = first_high.shape[0]
    both = dot(jnp.concatenate([first_high, first_low], axis=0), second_high)
    return both[:rows] + both[rows:] + dot(first_high, second_low)


def lane_sums(values):
    rows, lanes = values.shape
    step = 8 if rows % 8 == 0 else rows
    total = functools.reduce(
        jnp.add,
        [
            values[row : row + step, lane : lane + LANES]
            for row in range(0, rows, step)
            for lane in range(0, lanes, LANES)
        ],
    )
    return jnp.sum(total, axis=0, keepdims=True)


def half_of(side, half):
    return pl.ds(pl.multiple_of(side * half, LANES), half)


def scalar_sum(values):
    return jnp.sum(lane_sums(values), axis=1, keepdims=True)


def pick(values, picked):
    high, _ = split(values)
    middle, low = split(values - high.astype(F32))
    rows = values.shape[0]
    found = dot(jnp.concatenate([high, middle, low], axis=0), picked)
    return found[:rows] + (found[rows : 2 * rows] + found[2 * rows :])


def conductance(operating, table):
    points = table.shape[1]
    spread = jnp.concatenate([table, jnp.zeros((1, LANES - points), F32)], axis=1)
    spread = jnp.broadcast_to(spread, (operating.shape[0], LANES))
    pieces = []
    for block in range(operating.shape[1] // LANES):
        scaled = (operating[:, block * LANES : (block + 1) * LANES] + 4.0) * ((points - 1) / 8.0)
        knot = jnp.clip(jnp.floor(scaled), 0.0, points - 2.0)
        weight = scaled - knot
        place = knot.astype(I32)
        left = jnp.take_along_axis(spread, place, axis=1, mode="promise_in_bounds")
        right = jnp.take_along_axis(spread, place + 1, axis=1, mode="promise_in_bounds")
        pieces.append(left + weight * (right - left))
    return jnp.concatenate(pieces, axis=1)


def fetch_kernel(
    vector_in,
    neighbours_in,
    weights_in,
    degree_in,
    linear_in,
    capacity_in,
    send_list_in,
    boundary_in,
    table_in,
    operating_in,
    forward_in,
    back_in,
    vector,
    picked,
    linear,
    capacity,
    capacity_all,
    table,
    operating,
    forward,
    back,
    entry_rows,
    weight_rows,
    place,
    neighbours,
    weights,
    degree,
    linear_all,
    send_list,
    boundary,
    copied,
):
    place[0], place[1] = lax.axis_index("samples"), lax.axis_index("nodes")
    place[2], place[3] = lax.axis_size("nodes"), lax.axis_size("samples")
    slots, nodes = neighbours.shape
    lanes = picked.shape[1]
    half = linear.shape[1] - lanes
    node_groups = send_list.shape[0] // CAP
    side, part = place[0] % 2, place[1]
    copies = [
        pltpu.make_async_copy(source, target, copied.at[index])
        for index, (source, target) in enumerate(
            [
                (vector_in, vector),
                (send_list_in, send_list),
                (boundary_in, boundary),
                (neighbours_in, neighbours),
                (weights_in, weights),
                (degree_in, degree),
                (linear_in, linear_all),
                (capacity_in, capacity_all),
                (table_in, table),
                (operating_in, operating),
                (forward_in.at[place[0]], forward),
                (back_in.at[place[0]], back),
            ]
        )
    ]
    for copy in copies:
        copy.start()
    for copy in copies[1:3]:
        copy.wait()

    lane = lax.broadcasted_iota(I32, (8, lanes), 1)

    def name(slot, found):
        target = part ^ (slot // CAP + 1)
        node = boundary[send_list[target * CAP + slot % CAP]]
        return jnp.where(lane == slot, node, found)

    cut_nodes = lax.fori_loop(
        0, (node_groups - 1) * CAP, name, jnp.full((8, lanes), -1, I32), unroll=8
    )
    hit = lax.broadcasted_iota(I32, (nodes, lanes), 0) == cut_nodes[:1]
    picked[...] = jnp.where(hit, 1.0, 0.0).astype(BF16)

    for copy in copies[3:8]:
        copy.wait()
    mine = half_of(side, half)
    entry = neighbours[...]
    remote = entry - nodes
    distance = part ^ (remote >> 4)
    entry = jnp.where(remote < 0, entry, nodes + (distance - 1) * CAP + (remote & 15))
    live = lax.broadcasted_iota(I32, (slots, nodes), 0) < degree[...]
    neighbours[...] = entry
    weights[...] = jnp.where(live, weights[...], 0.0)
    columns = jnp.concatenate(
        [
            entry.astype(F32),
            weights[...],
            linear_all[...],
            capacity_all[...],
            jnp.zeros((6, nodes), F32),
        ],
        axis=0,
    )
    at_cut = pick(columns, picked[...])
    linear[:, :half] = linear_all[:, mine]
    linear[:, half:] = at_cut[2 * slots : 2 * slots + 1]
    capacity[:, :half] = capacity_all[:, mine]
    capacity[:, half:] = at_cut[2 * slots + 1 : 2 * slots + 2]
    entry_rows[:, :half] = neighbours[:, mine]
    entry_rows[:, half:] = at_cut[:slots].astype(I32)
    weight_rows[:, :half] = weights[:, mine]
    weight_rows[:, half:] = at_cut[slots : 2 * slots]
    entries = [entry_rows[slot : slot + 1, :] for slot in range(slots)]
    gains = [weight_rows[slot : slot + 1, :] for slot in range(slots)]
    for slot in range(slots):
        for later in range(slot + 1, slots):
            same = entries[slot] == entries[later]
            gains[slot] = gains[slot] + jnp.where(same, gains[later], 0.0)
            entries[later] = jnp.where(same, -1, entries[later])
    for slot in range(slots):
        entry_rows[slot : slot + 1, :] = entries[slot]
        weight_rows[slot : slot + 1, :] = gains[slot]
    copies[0].wait()
    for copy in copies[8:]:
        copy.wait()


def build(entry_rows, weight_rows, coupling_high, coupling_low):
    slots, width = entry_rows.shape
    sources = coupling_high.shape[0]
    blocks = sources // CAP
    unroll = max(count for count in range(1, 35) if blocks % count == 0)
    wide = (CAP, LANES)

    def column_block(block, carry):
        at_lanes = pl.ds(pl.multiple_of(block * LANES, LANES), LANES)
        names = [
            jnp.broadcast_to(entry_rows[slot : slot + 1, at_lanes], wide).astype(jnp.int16)
            for slot in range(slots)
        ]
        parts = [
            split(jnp.broadcast_to(weight_rows[slot : slot + 1, at_lanes], wide))
            for slot in range(slots)
        ]

        def source_rows(step, row):
            for inner in range(unroll):
                high = jnp.zeros(wide, BF16)
                low = jnp.zeros(wide, BF16)
                for slot in range(slots):
                    hit = names[slot] == row + jnp.int16(CAP * inner)
                    high = jnp.where(hit, parts[slot][0], high)
                    low = jnp.where(hit, parts[slot][1], low)
                at = pl.ds(pl.multiple_of((step * unroll + inner) * CAP, CAP), CAP)
                coupling_high[at, at_lanes] = high
                coupling_low[at, at_lanes] = low
            return row + jnp.int16(CAP * unroll)

        lax.fori_loop(
            0,
            blocks // unroll,
            source_rows,
            lax.broadcasted_iota(I32, wide, 0).astype(jnp.int16),
        )
        return carry

    lax.fori_loop(0, width // LANES, column_block, 0)


def prepare_kernel(entry_rows, weight_rows, coupling_high, coupling_low):
    half = coupling_high.shape[1]
    build(entry_rows.at[:, :half], weight_rows.at[:, :half], coupling_high, coupling_low)


def prepare_cut_kernel(after, entry_rows, weight_rows, cut_high, cut_low, cut_halo):
    lanes = cut_high.shape[1]
    half = entry_rows.shape[1] - lanes
    build(entry_rows.at[:, half:], weight_rows.at[:, half:], cut_high, cut_low)
    nodes = cut_high.shape[0] - lanes
    cut_halo[...] = jnp.transpose(cut_high[nodes:].astype(F32) + cut_low[nodes:].astype(F32))


def relay_kernel(*refs):
    count = (len(refs) - 1) // 2
    for source, target in zip(refs[1 : 1 + count], refs[1 + count :]):
        target[...] = source[...]


def conductance_kernel(place, near_operating, operating, table, picked, conductances):
    rows, nodes = operating.shape
    side = place[0] % 2
    for at, values in ((side, operating), (1 - side, near_operating)):
        conductances[pl.ds(pl.multiple_of(at * rows, 8), rows), :nodes] = conductance(
            values[...], table[...]
        )
    conductances[:, nodes:] = pick(conductances[:, :nodes], picked[...])


def coupled(high, stacked, coupling_high, coupling_low, sources, lanes):
    rows = high.shape[0]
    both = dot(stacked, coupling_high[sources, lanes])
    return both[:rows] + both[rows:] + dot(high, coupling_low[sources, lanes])


def packet_layout(steps, times):
    shared = steps * CAP <= LANES
    return shared, times if shared else 0


def packet_steps(steps):
    return [(2,), (1, 3)] if steps == 3 else [(step,) for step in range(1, steps + 1)]


def wave_kernel(*refs, pieces, steps):
    vectors = refs[1 : 1 + pieces]
    (
        forward,
        conductances,
        picked,
        coupling_high,
        coupling_low,
        linear,
        capacity,
        cut_halo,
        field_high,
        field_low,
        wave,
        current,
        cut_current,
    ) = refs[1 + pieces : 1 + pieces + 13]
    sent = refs[1 + pieces + 13 :]
    side = refs[0][0] % 2
    rows, nodes = vectors[0].shape
    lanes = picked.shape[1]
    times = wave.shape[0]
    half = linear.shape[1] - lanes
    for index in range(pieces):
        at = slice(index * rows, (index + 1) * rows)
        field_high[at, :nodes], field_low[at, :nodes] = split(vectors[index][...])
    field_high[:, nodes:] = dot(field_high[:, :nodes], picked[...]).astype(BF16)
    field_low[:, nodes:] = dot(field_low[:, :nodes], picked[...]).astype(BF16)
    wave[...] = dot_split(
        (forward[0, :times], forward[1, :times]), (field_high[...], field_low[...])
    )
    slope = dot_split(
        (forward[0, times : 2 * times], forward[1, times : 2 * times]),
        (field_high[:, nodes:], field_low[:, nodes:]),
    )
    high, low = split(conductances[:, :nodes] * wave[:, :nodes])
    current[:times] = high
    current[times:] = low
    at_cut = conductances[:, nodes:] * wave[:, nodes:]
    cut_current[...] = jnp.transpose(at_cut)
    image = (
        linear[:, half:] * wave[:, nodes:]
        + at_cut
        + capacity[:, half:] * slope
        + coupled(
            high, current[...], coupling_high, coupling_low, slice(0, nodes), slice(None)
        )
    )
    image = jnp.transpose(image)
    at_cut = jnp.transpose(conductances[:, nodes:])
    slots = steps * CAP
    shared, start = packet_layout(steps, times)
    for target, wanted in zip(sent, packet_steps(steps)):
        target[...] = jnp.zeros(target.shape, F32)
        if shared:
            target[:slots, :times] = cut_current[:slots]
        for row, values, size in ((0, cut_halo, slots), (1, image, times), (2, at_cut, times)):
            blocks = [values[(step - 1) * CAP : step * CAP, :size] for step in wanted]
            block = blocks[0] if len(blocks) == 1 else jnp.where(side == 0, *blocks)
            target[row * CAP : (row + 1) * CAP, start : start + size] = block


def local_kernel(
    field_high,
    field_low,
    forward,
    wave,
    current,
    conductances,
    coupling_high,
    coupling_low,
    linear,
    capacity,
    place,
    load,
    slope,
    own_wave,
    dual,
    dual_slope,
):
    times, half = load.shape
    sources = slice(0, current.shape[1])
    mine = half_of(place[0] % 2, half)
    others = dot_split(
        (forward[0, times:], forward[1, times:]), (field_high[:, mine], field_low[:, mine])
    )
    slope[...] = capacity[:, :half] * others[:times]
    dual[...] = others[times : 2 * times]
    dual_slope[...] = capacity[:, :half] * others[2 * times :]
    own_wave[...] = wave[:, mine]
    load[...] = own_wave[...] * (linear[:, :half] + conductances[:, mine])
    high = current[:times]
    step = 256
    for block in range(half // step):
        lanes = slice(block * step, (block + 1) * step)
        load[:, lanes] += coupled(
            high, current[...], coupling_high, coupling_low, sources, lanes
        )


def signed_sums(values):
    rows = values.shape[0]
    folded = functools.reduce(jnp.add, [values[row : row + 8] for row in range(0, rows, 8)])
    even = lax.broadcasted_iota(I32, folded.shape, 0) % 2 == 0
    return (
        jnp.sum(folded, axis=0, keepdims=True),
        jnp.sum(jnp.where(even, folded, -folded), axis=0, keepdims=True),
    )


def analysed(back, load):
    spectrum = dot_split((back[0], back[1]), split(load))
    middle = spectrum.shape[0] // 2
    return spectrum[:middle], spectrum[middle:]


def unpack(side, arrived, others, cut_current, lanes):
    steps = len(arrived)
    times = cut_current.shape[1]
    if steps == 3:
        both, own, near = (packet[...] for packet in arrived)
        arrived = [
            jnp.where(side == 0, own, near),
            both,
            jnp.where(side == 0, near, own),
        ]
    slots = steps * CAP
    blank = jnp.zeros((lanes - slots, times), F32)

    def stack(blocks):
        return jnp.transpose(jnp.concatenate([*blocks, blank], axis=0))

    def sender(step, block):
        at = slice((block - 1) * CAP, block * CAP)
        if step == 0:
            return cut_current[at]
        return others[0][step, at] if others else arrived[step - 1][at, :times]

    current = stack([sender(step, step) for step in range(1, steps + 1)])
    return arrived, stack, sender, current


def first_kernel(*refs, steps, apart):
    arrived, others = refs[1 : steps + 1], refs[steps + 1 : steps + 1 + apart]
    (
        cut_current,
        local_load,
        slope,
        own_wave,
        coupling_high,
        coupling_low,
        image,
        load,
        sums,
    ) = refs[1 + steps + apart :]
    half = load.shape[1]
    lanes = -(-steps * CAP // LANES) * LANES
    nodes = coupling_high.shape[0] - lanes
    current = unpack(refs[0][0] % 2, arrived, others, cut_current, lanes)[-1]
    high, low = split(current)
    share = coupled(
        high,
        jnp.concatenate([high, low], axis=0),
        coupling_high,
        coupling_low,
        slice(nodes, None),
        slice(0, half),
    )
    load[...] = local_load[...] + share
    answer = load[...] + slope[...]
    image[...] = answer
    lines = [*signed_sums(answer), *signed_sums(own_wave[...])]
    sums[...] = jnp.concatenate(lines + [jnp.zeros((4, half), F32)], axis=0)


def spread_kernel(*refs, steps, apart):
    arrived, others = refs[1 : steps + 1], refs[steps + 1 : steps + 1 + apart]
    cut_current, image, back, halo, kept, sent = refs[1 + steps + apart :]
    times = image.shape[0]
    slots = steps * CAP
    start = packet_layout(steps, times)[1]
    arrived, stack, sender, _ = unpack(
        refs[0][0] % 2, arrived, others, cut_current, halo.shape[1]
    )
    kept[...], sent[...] = analysed(back, image[...])
    currents = []
    for step in range(1, steps + 1):
        theirs = jnp.concatenate(
            [sender(step ^ block, block) for block in range(1, steps + 1)], axis=0
        )
        gains = arrived[step - 1][:CAP, start : start + slots]
        image_part = arrived[step - 1][CAP : 2 * CAP, start : start + times]
        there = arrived[step - 1][2 * CAP : 3 * CAP, start : start + times]
        currents.append(there * (image_part + dot_split(split(gains), split(theirs))))
    halo[...] = stack(currents)


def second_kernel(
    place,
    halo,
    near_image,
    image,
    back,
    conductances,
    coupling_high,
    coupling_low,
    linear,
    load,
    kept,
    sent,
    current,
):
    times, half = image.shape
    nodes = current.shape[1]
    side = place[0] % 2
    mine, other = half_of(side, half), half_of(1 - side, half)
    for at, field in ((mine, image), (other, near_image)):
        current[:times, at], current[times:, at] = split(conductances[:, at] * field[...])
    load[...] = image[...] * (linear[:, :half] + conductances[:, mine])
    high, low = split(halo[...])
    halo_stacked = jnp.concatenate([high, low], axis=0)
    step = 256
    for block in range(half // step):
        lanes = slice(block * step, (block + 1) * step)
        load[:, lanes] += coupled(
            current[:times], current[...], coupling_high, coupling_low, slice(0, nodes), lanes
        ) + coupled(high, halo_stacked, coupling_high, coupling_low, slice(nodes, None), lanes)
    kept[...], sent[...] = analysed(back, load[...])


def sum_kernel(after, *refs):
    total = refs[0][...]
    for value in refs[1:-1]:
        total = total + value[...]
    refs[-1][...] = total


def turned(field, first_pair, half_order):
    count = field.shape[0]
    row = lax.broadcasted_iota(I32, field.shape, 0)
    scaling = (first_pair + row // 2).astype(F32) * (1.0 / half_order)
    above = pltpu.roll(field, count - 1, 0)
    below = pltpu.roll(field, 1, 0)
    return scaling * jnp.where(row % 2 == 0, above, -below)


def combine_kernel(after, place, kept, arrived, *targets):
    half = kept.shape[1]
    rows = targets[0].shape[0]
    side = place[0] % 2
    for index, target in enumerate(targets):
        at = slice(index * rows, (index + 1) * rows)
        target[:, half_of(side, half)] = kept[at]
        target[:, half_of(1 - side, half)] = arrived[at]


def joined(parts):
    return functools.reduce(jnp.add, [part[...] for part in parts])


def guess(cross, squares):
    ratio = cross / jnp.where(squares > 0.0, squares, 1.0)
    return jnp.clip(jnp.where(squares > 0.0, ratio, 0.0), -40.0, 40.0)


def products_kernel(
    place,
    vector,
    load,
    second_load,
    image,
    wave,
    dual,
    dual_slope,
    own_sums,
    far_sums,
    scalars,
    *,
    length,
):
    start, first = wave[...], load[...]
    field, sums = vector[...], own_sums[...] + far_sums[...]
    coeff = guess(scalar_sum(start * image[...]), scalar_sum(start * start))
    rest = image[...] - coeff * start
    change = second_load[...] - coeff * first
    start_sums = [sums[line + 2 : line + 3] for line in (0, 1)]
    rest_sums = [sums[line : line + 1] - coeff * start_sums[line] for line in (0, 1)]
    start_ends, rest_ends, first_ends, change_ends = (
        signed_sums(values) for values in (start, rest, first, change)
    )

    def mixed(values, value_sums, others, other_ends):
        ends = value_sums[0] * other_ends[0] + value_sums[1] * other_ends[1]
        return lane_sums(values * others) * (2.0 / length) - lane_sums(ends) * (
            1.0 / length / length
        )

    found = [
        lane_sums(field * field),
        lane_sums(dual[...] * rest),
        lane_sums(dual[...] * start),
        mixed(rest, rest_sums, rest, rest_ends),
        mixed(rest, rest_sums, start, start_ends) + mixed(start, start_sums, rest, rest_ends),
        mixed(start, start_sums, start, start_ends),
        lane_sums(dual[...] * change - dual_slope[...] * rest),
        lane_sums(dual[...] * first - dual_slope[...] * start),
        mixed(rest, rest_sums, change, change_ends),
        mixed(rest, rest_sums, first, first_ends) + mixed(start, start_sums, change, change_ends),
        mixed(start, start_sums, first, first_ends),
    ]
    device = place[1] * place[3] + place[0]
    lane = lax.broadcasted_iota(I32, scalars.shape, 1)
    column = jnp.concatenate(found + [jnp.zeros((5, LANES), F32)], axis=0)
    column = jnp.sum(column, axis=1, keepdims=True)
    line = lax.broadcasted_iota(I32, column.shape, 0)
    column = jnp.where(line == len(found), coeff, column)
    scalars[...] = jnp.where(lane == device, column, 0.0)


def settle_kernel(place, vector, capacity, *refs, length):
    *parts, answer, slope, skew = refs
    rows = vector.shape[0]
    first_pair = place[0] * (rows // 2)
    answer[...] = joined(parts)
    field, start = answer[...], vector[...]
    slope[...] = capacity[...] * turned(field, first_pair, length // 2)
    start_slope = capacity[...] * turned(start, first_pair, length // 2)
    products = [
        scalar_sum(field * slope[...]),
        scalar_sum(field * start_slope + start * slope[...]),
        scalar_sum(start * start_slope),
        jnp.zeros((5, 1), F32),
    ]
    skew[...] = jnp.broadcast_to(jnp.concatenate(products, axis=0), skew.shape)


def last_kernel(
    gathered,
    vector,
    answer,
    slope,
    skew,
    *refs,
    entries,
    devices,
):
    *parts, basis_two, next_residue = refs
    own = [gathered[line : line + 1, :] for line in range(12)]
    local = own.pop()

    def everywhere(values):
        return jnp.sum(values, axis=1, keepdims=True) / entries

    scale_square = everywhere(own[0]) + EPSILON
    coeff = everywhere(own[1] + local * own[2]) / scale_square
    near = local - coeff
    rest_square = everywhere(own[3] + near * (own[4] + near * own[5]))
    along_one = everywhere(own[6] + near * own[7])
    along_two = everywhere(own[8] + near * (own[9] + near * own[10]))
    turn = skew[0:1, :1] - coeff * (skew[1:2, :1] - coeff * skew[2:3, :1])
    along_two = along_two + turn * (devices / entries)
    scale = jnp.sqrt(scale_square)
    second_norm = jnp.sqrt(jnp.maximum(rest_square, 0.0) / scale_square + EPSILON)
    inverse = 1.0 / (second_norm * scale)
    along_one = along_one * inverse / scale_square
    along_two = along_two * inverse * inverse
    second = (answer[...] - coeff * vector[...]) * inverse
    basis_two[...] = second
    next_residue[...] = (
        (joined(parts) + slope[...] - coeff * answer[...]) * inverse
        - along_one * vector[...]
        - along_two * second
    )


VMEM = pl.BlockSpec(memory_space=pltpu.VMEM)
SMEM = pl.BlockSpec(memory_space=pltpu.SMEM)


HBM = pl.BlockSpec(memory_space=pltpu.HBM)


def run(kernel, name, specs, operands, outs, scratch=(), micros=1, room=12, spaces=None):
    spaces = spaces or [pltpu.VMEM] * len(outs)
    return pl.pallas_call(
        kernel,
        out_shape=[space(shape, dtype) for space, (shape, dtype) in zip(spaces, outs)],
        in_specs=specs,
        out_specs=[pl.BlockSpec(memory_space=space) for space in spaces],
        scratch_shapes=list(scratch),
        compiler_params=pltpu.CompilerParams(vmem_limit_bytes=room * 2**20),
        cost_estimate=pl.CostEstimate(
            flops=0, bytes_accessed=int(micros * 3e6), transcendentals=0
        ),
        name=name,
    )(*operands)


def swap(value, mask):
    count = lax.axis_size("samples")
    return lax.ppermute(value, "samples", [(at, at ^ mask) for at in range(count)])


def trade(value, masks):
    count, parts = lax.axis_size("nodes"), lax.axis_size("samples")
    pairs = [
        (at * parts + which, (at ^ masks[which % len(masks)]) * parts + which)
        for at in range(count)
        for which in range(parts)
    ]
    return lax.ppermute(value, ("nodes", "samples"), pairs)


def add(after, terms):
    (value,) = run(
        sum_kernel,
        "sum",
        [VMEM] * (len(terms) + 1),
        (after, *terms),
        [(terms[0].shape, F32)],
    )
    return value


def exchange(value, axis, after):
    count, stride, terms = lax.axis_size(axis), 1, [value]
    while stride < count:
        if stride > 1:
            value = add(after, terms)
        radix = 4 if count // stride % 4 == 0 else 2
        terms = [value] + [
            lax.ppermute(value, axis, [(at, at ^ (step * stride)) for at in range(count)])
            for step in range(1, radix)
        ]
        stride *= radix
    return terms


def hand_out(after, place, kept, arrived):
    count = lax.axis_size("samples") // 2
    field = ((kept.shape[0] // count, 2 * kept.shape[1]), F32)
    parts = run(
        combine_kernel,
        "combine",
        [VMEM, SMEM] + [VMEM] * 2,
        (after, place, kept, arrived),
        [field] * count,
    )
    return [parts[0]] + [swap(part, 2 * mask) for mask, part in enumerate(parts) if mask]


def shards(
    vector, operating, table, linear, capacity, weights, degree, neighbours, boundary, send_list
):
    rows, nodes = vector.shape
    parts, node_groups = lax.axis_size("samples"), lax.axis_size("nodes")
    length, half, times = rows * parts, nodes // 2, 2 * rows
    entries = float(length * nodes * node_groups)
    steps = node_groups - 1
    slots = steps * CAP
    lanes = -(-slots // LANES) * LANES
    sources, width = nodes + lanes, half + lanes
    forward, back = (jnp.asarray(table) for table in transform_tables(length, parts))
    linear, capacity, degree, table = (
        value.reshape(1, -1) for value in (linear, capacity, degree, table)
    )

    slot_count = weights.shape[0]
    (
        own_vector,
        picked,
        linear_wide,
        capacity_wide,
        capacity,
        table,
        own_operating,
        forward,
        back,
        entry_rows,
        weight_rows,
        place,
    ) = run(
        fetch_kernel,
        "fetch",
        [HBM] * 12,
        tuple(
            pltpu.with_memory_space_constraint(value, pltpu.HBM)
            for value in (vector, neighbours, weights, degree, linear, capacity, send_list)
            + (boundary, table, operating, forward, back)
        ),
        [
            ((rows, nodes), F32),
            ((nodes, lanes), BF16),
            ((1, width), F32),
            ((1, width), F32),
            ((1, nodes), F32),
            (table.shape, F32),
            ((rows, nodes), F32),
            (forward.shape[1:], BF16),
            (back.shape[1:], BF16),
            ((slot_count, width), I32),
            ((slot_count, width), F32),
            ((4,), I32),
        ],
        scratch=[
            pltpu.VMEM((slot_count, nodes), I32),
            pltpu.VMEM((slot_count, nodes), F32),
            pltpu.VMEM((1, nodes), I32),
            pltpu.VMEM((1, nodes), F32),
            pltpu.SMEM(send_list.shape, I32),
            pltpu.SMEM(boundary.shape, I32),
            pltpu.SemaphoreType.DMA((12,)),
        ],
        micros=2,
        spaces=[pltpu.VMEM] * 11 + [pltpu.SMEM],
    )
    coupling_high, coupling_low = run(
        prepare_kernel,
        "prepare",
        [VMEM] * 2,
        (entry_rows, weight_rows),
        [((sources, half), BF16)] * 2,
        micros=6,
    )
    near_operating = swap(operating, 1)
    vectors, bit = [vector], parts // 2
    while bit > 1:
        vectors = vectors + [swap(piece, bit) for piece in vectors]
        bit //= 2
    far = len(vectors) - 1
    if far:
        vectors[1:] = run(
            relay_kernel,
            "relay",
            [VMEM] * (far + 1),
            (coupling_low, *vectors[1:]),
            [((rows, nodes), F32)] * far,
        )
    vectors = vectors + [swap(piece, 1) for piece in vectors]
    vectors[0] = own_vector
    cut_high, cut_low, cut_halo = run(
        prepare_cut_kernel,
        "prepare_cut",
        [VMEM] * 3,
        (vectors[far], entry_rows, weight_rows),
        [((sources, lanes), BF16), ((sources, lanes), BF16), ((lanes, lanes), F32)],
        micros=1,
    )
    (conductances,) = run(
        conductance_kernel,
        "conductance",
        [SMEM] + [VMEM] * 4,
        (place, near_operating, own_operating, table, picked),
        [((times, sources), F32)],
        micros=1,
    )

    wide = ((times, half), F32)
    shared, start = packet_layout(steps, times)
    packet = (
        max(slots if shared else 0, 3 * CAP),
        -(-(start + max(times, slots)) // LANES) * LANES,
    )
    field_high, field_low, wave, current, cut_current, *sent = run(
        functools.partial(wave_kernel, pieces=parts, steps=steps),
        "wave",
        [SMEM] + [VMEM] * (parts + 8),
        (place, *vectors, forward, conductances, picked, cut_high, cut_low)
        + (linear_wide, capacity_wide, cut_halo),
        [
            ((length, sources), BF16),
            ((length, sources), BF16),
            ((times, sources), F32),
            ((2 * times, nodes), BF16),
            ((lanes, times), F32),
        ]
        + [(packet, F32)] * len(packet_steps(steps)),
        micros=2,
    )
    arrived = [trade(packet, masks) for packet, masks in zip(sent, packet_steps(steps))]
    if steps == 3:
        arrived.append(swap(arrived[-1], 1))
    others = []
    if not shared:
        gathered = lax.all_gather(cut_current, "nodes")
        distance = jnp.arange(node_groups, dtype=I32)
        others = [gathered[lax.axis_index("nodes") ^ distance]]
    local_load, slope, own_wave, dual, dual_slope = run(
        local_kernel,
        "local",
        [VMEM] * 10 + [SMEM],
        (field_high, field_low, forward, wave, current, conductances)
        + (coupling_high, coupling_low, linear_wide, capacity_wide, place),
        [wide] * 5,
        micros=3,
    )
    block = ((length // 2, half), F32)
    packets = (place, *arrived, *others, cut_current)
    packet_specs = [SMEM] + [VMEM] * (len(packets) - 1)
    image, load, own_sums = run(
        functools.partial(first_kernel, steps=steps, apart=len(others)),
        "first",
        packet_specs + [VMEM] * 5,
        (*packets, local_load, slope, own_wave, coupling_high, coupling_low),
        [wide, wide, ((8, half), F32)],
        micros=1,
    )
    halo, kept, sent = run(
        functools.partial(spread_kernel, steps=steps, apart=len(others)),
        "spread",
        packet_specs + [VMEM] * 2,
        (*packets, image, back),
        [((times, lanes), F32), block, block],
        micros=1,
    )
    near_image = swap(image, 1)
    bit = 2
    while 2 * bit < parts:
        own_sums = own_sums + swap(own_sums, bit)
        bit *= 2
    far_sums = swap(own_sums, bit) if bit < parts else jnp.zeros_like(own_sums)
    arrived = swap(sent, 1)

    second_load, second_kept, second_sent = run(
        second_kernel,
        "second",
        [SMEM] + [VMEM] * 8,
        (place, halo, near_image, image, back, conductances)
        + (coupling_high, coupling_low, linear_wide),
        [wide, block, block],
        scratch=[pltpu.VMEM((2 * times, nodes), BF16)],
        micros=3,
    )
    answer_parts = hand_out(second_load, place, kept, arrived)
    (second_sent,) = run(
        relay_kernel,
        "relay",
        [VMEM] * 2,
        (far_sums, second_sent),
        [(second_sent.shape, F32)],
    )
    second_arrived = swap(second_sent, 1)
    gathered = -(-node_groups * parts // LANES) * LANES
    (scalars,) = run(
        functools.partial(products_kernel, length=length),
        "products",
        [SMEM] + [VMEM] * 9,
        (place, own_vector, load, second_load, image, own_wave, dual, dual_slope)
        + (own_sums, far_sums),
        [((16, gathered), F32)],
        micros=1,
    )
    second_parts = hand_out(scalars, place, second_kept, second_arrived)
    scalars = add(cut_halo, exchange(scalars, "nodes", cut_halo))
    answer, slope, skew = run(
        functools.partial(settle_kernel, length=length),
        "settle",
        [SMEM] + [VMEM] * (len(answer_parts) + 2),
        (place, own_vector, capacity, *answer_parts),
        [((rows, nodes), F32), ((rows, nodes), F32), ((8, LANES), F32)],
        micros=1,
    )
    scalars = add(skew, exchange(scalars, "samples", cut_halo))
    field = jax.ShapeDtypeStruct((rows, nodes), F32)
    return tuple(
        pl.pallas_call(
            functools.partial(
                last_kernel, entries=entries, devices=float(node_groups * parts)
            ),
            out_shape=[field, field],
            in_specs=[VMEM] * (5 + len(second_parts)),
            out_specs=[VMEM] * 2,
            compiler_params=pltpu.CompilerParams(vmem_limit_bytes=12 * 2**20),
            name="last",
        )(scalars, own_vector, answer, slope, skew, *second_parts)
    )


def solution(mesh):
    return jax.shard_map(
        shards,
        mesh=mesh,
        in_specs=(
            P("samples", ("copies", "nodes")),
            P("samples", ("copies", "nodes")),
            P(),
            P("nodes"),
            P("nodes"),
            P(None, "nodes"),
            P("nodes"),
            P(None, "nodes"),
            P("nodes"),
            P("nodes"),
        ),
        out_specs=(P("samples", ("copies", "nodes")), P("samples", ("copies", "nodes"))),
        check_vma=False,
    )
```

```python
import functools
import math

import jax
import jax.numpy as jnp
import numpy as np
from jax import lax
from jax.experimental import pallas as pl
from jax.experimental.pallas import tpu as pltpu
from jax.sharding import PartitionSpec as P

CAP = 16
EPSILON = 1e-06
LANES = 128
BF16 = jnp.bfloat16
F32 = jnp.float32
I32 = jnp.int32


def spectral_tables(length):
    indices = np.arange(length)
    frequency = np.where(indices == 1, length // 2, indices // 2)
    angles = (indices[:, None] * frequency[None, :] % length) * (2.0 * math.pi / length)
    cosine_column = (indices % 2 == 0) | (indices == 1)
    synthesis = np.where(cosine_column[None, :], np.cos(angles), np.sin(angles))
    factor = np.where(indices < 2, 1.0 / length, 2.0 / length)
    analysis = synthesis.T * factor[:, None]
    turn = np.zeros((length, length))
    for pair in range(length // 2):
        turn[2 * pair, 2 * pair + 1] = pair / (length // 2)
        turn[2 * pair + 1, 2 * pair] = -pair / (length // 2)
    return synthesis, analysis, turn


def halves(table):
    high = table.astype(np.float32).astype(BF16)
    low = (table - high.astype(np.float64)).astype(np.float32).astype(BF16)
    return np.stack([high, low])


def piece_order(count):
    masks, bit = [0], count // 2
    while bit:
        masks = masks + [mask ^ bit for mask in masks]
        bit //= 2
    return masks


def transform_tables(length, parts):
    synthesis, analysis, turn = spectral_tables(length)
    slope, dual_slope = synthesis @ turn, analysis.T @ turn
    rows = length // parts
    forward, back = [], []
    for place in range(parts):
        times = np.arange(place // 2 * 2 * rows, (place // 2 + 1) * 2 * rows)
        block = lambda owner: np.arange(owner * rows, (owner + 1) * rows)
        coefs = np.concatenate([block(place ^ mask) for mask in piece_order(parts)])
        forward.append(
            np.concatenate(
                [
                    synthesis[np.ix_(times, coefs)],
                    slope[np.ix_(times, coefs)],
                    analysis[np.ix_(coefs, times)].T,
                    dual_slope[np.ix_(times, coefs)],
                ]
            )
        )
        sent = np.concatenate(
            [block(place ^ mask ^ side) for side in (0, 1) for mask in range(0, parts, 2)]
        )
        back.append(analysis[np.ix_(sent, times)])
    return (
        np.moveaxis(halves(np.stack(forward)), 0, 1),
        np.moveaxis(halves(np.stack(back)), 0, 1),
    )


def split(values):
    high = values.astype(BF16)
    return high, (values - high.astype(F32)).astype(BF16)


def dot(first, second):
    return jnp.dot(first, second, preferred_element_type=F32)


def dot_split(first, second):
    (first_high, first_low), (second_high, second_low) = first, second
    rows = first_high.shape[0]
    both = dot(jnp.concatenate([first_high, first_low], axis=0), second_high)
    return both[:rows] + both[rows:] + dot(first_high, second_low)


def lane_sums(values):
    rows, lanes = values.shape
    step = 8 if rows % 8 == 0 else rows
    total = functools.reduce(
        jnp.add,
        [
            values[row : row + step, lane : lane + LANES]
            for row in range(0, rows, step)
            for lane in range(0, lanes, LANES)
        ],
    )
    return jnp.sum(total, axis=0, keepdims=True)


def half_of(side, half):
    return pl.ds(pl.multiple_of(side * half, LANES), half)


def scalar_sum(values):
    return jnp.sum(lane_sums(values), axis=1, keepdims=True)


def pick(values, picked):
    high, _ = split(values)
    middle, low = split(values - high.astype(F32))
    rows = values.shape[0]
    found = dot(jnp.concatenate([high, middle, low], axis=0), picked)
    return found[:rows] + (found[rows : 2 * rows] + found[2 * rows :])


def conductance(operating, table):
    points = table.shape[1]
    spread = jnp.concatenate([table, jnp.zeros((1, LANES - points), F32)], axis=1)
    spread = jnp.broadcast_to(spread, (operating.shape[0], LANES))
    pieces = []
    for block in range(operating.shape[1] // LANES):
        scaled = (operating[:, block * LANES : (block + 1) * LANES] + 4.0) * ((points - 1) / 8.0)
        knot = jnp.clip(jnp.floor(scaled), 0.0, points - 2.0)
        weight = scaled - knot
        place = knot.astype(I32)
        left = jnp.take_along_axis(spread, place, axis=1, mode="promise_in_bounds")
        right = jnp.take_along_axis(spread, place + 1, axis=1, mode="promise_in_bounds")
        pieces.append(left + weight * (right - left))
    return jnp.concatenate(pieces, axis=1)


def fetch_kernel(
    vector_in,
    neighbours_in,
    weights_in,
    degree_in,
    linear_in,
    capacity_in,
    send_list_in,
    boundary_in,
    table_in,
    operating_in,
    forward_in,
    back_in,
    vector,
    picked,
    linear,
    capacity,
    capacity_all,
    table,
    operating,
    forward,
    back,
    entry_rows,
    weight_rows,
    place,
    neighbours,
    weights,
    degree,
    linear_all,
    send_list,
    boundary,
    copied,
):
    place[0], place[1] = lax.axis_index("samples"), lax.axis_index("nodes")
    place[2], place[3] = lax.axis_size("nodes"), lax.axis_size("samples")
    slots, nodes = neighbours.shape
    lanes = picked.shape[1]
    half = linear.shape[1] - lanes
    node_groups = send_list.shape[0] // CAP
    side, part = place[0] % 2, place[1]
    copies = [
        pltpu.make_async_copy(source, target, copied.at[index])
        for index, (source, target) in enumerate(
            [
                (vector_in, vector),
                (send_list_in, send_list),
                (boundary_in, boundary),
                (neighbours_in, neighbours),
                (weights_in, weights),
                (degree_in, degree),
                (linear_in, linear_all),
                (capacity_in, capacity_all),
                (table_in, table),
                (operating_in, operating),
                (forward_in.at[place[0]], forward),
                (back_in.at[place[0]], back),
            ]
        )
    ]
    for copy in copies:
        copy.start()
    for copy in copies[1:3]:
        copy.wait()

    lane = lax.broadcasted_iota(I32, (8, lanes), 1)

    def name(slot, found):
        target = part ^ (slot // CAP + 1)
        node = boundary[send_list[target * CAP + slot % CAP]]
        return jnp.where(lane == slot, node, found)

    cut_nodes = lax.fori_loop(
        0, (node_groups - 1) * CAP, name, jnp.full((8, lanes), -1, I32), unroll=8
    )
    hit = lax.broadcasted_iota(I32, (nodes, lanes), 0) == cut_nodes[:1]
    picked[...] = jnp.where(hit, 1.0, 0.0).astype(BF16)

    for copy in copies[3:8]:
        copy.wait()
    mine = half_of(side, half)
    entry = neighbours[...]
    remote = entry - nodes
    distance = part ^ (remote >> 4)
    entry = jnp.where(remote < 0, entry, nodes + (distance - 1) * CAP + (remote & 15))
    live = lax.broadcasted_iota(I32, (slots, nodes), 0) < degree[...]
    neighbours[...] = entry
    weights[...] = jnp.where(live, weights[...], 0.0)
    columns = jnp.concatenate(
        [
            entry.astype(F32),
            weights[...],
            linear_all[...],
            capacity_all[...],
            jnp.zeros((6, nodes), F32),
        ],
        axis=0,
    )
    at_cut = pick(columns, picked[...])
    linear[:, :half] = linear_all[:, mine]
    linear[:, half:] = at_cut[2 * slots : 2 * slots + 1]
    capacity[:, :half] = capacity_all[:, mine]
    capacity[:, half:] = at_cut[2 * slots + 1 : 2 * slots + 2]
    entry_rows[:, :half] = neighbours[:, mine]
    entry_rows[:, half:] = at_cut[:slots].astype(I32)
    weight_rows[:, :half] = weights[:, mine]
    weight_rows[:, half:] = at_cut[slots : 2 * slots]
    entries = [entry_rows[slot : slot + 1, :] for slot in range(slots)]
    gains = [weight_rows[slot : slot + 1, :] for slot in range(slots)]
    for slot in range(slots):
        for later in range(slot + 1, slots):
            same = entries[slot] == entries[later]
            gains[slot] = gains[slot] + jnp.where(same, gains[later], 0.0)
            entries[later] = jnp.where(same, -1, entries[later])
    for slot in range(slots):
        entry_rows[slot : slot + 1, :] = entries[slot]
        weight_rows[slot : slot + 1, :] = gains[slot]
    copies[0].wait()
    for copy in copies[8:]:
        copy.wait()


def build(entry_rows, weight_rows, coupling_high, coupling_low):
    slots, width = entry_rows.shape
    sources = coupling_high.shape[0]
    blocks = sources // CAP
    unroll = max(count for count in range(1, 35) if blocks % count == 0)
    wide = (CAP, LANES)

    def column_block(block, carry):
        at_lanes = pl.ds(pl.multiple_of(block * LANES, LANES), LANES)
        names = [
            jnp.broadcast_to(entry_rows[slot : slot + 1, at_lanes], wide).astype(jnp.int16)
            for slot in range(slots)
        ]
        parts = [
            split(jnp.broadcast_to(weight_rows[slot : slot + 1, at_lanes], wide))
            for slot in range(slots)
        ]

        def source_rows(step, row):
            for inner in range(unroll):
                high = jnp.zeros(wide, BF16)
                low = jnp.zeros(wide, BF16)
                for slot in range(slots):
                    hit = names[slot] == row + jnp.int16(CAP * inner)
                    high = jnp.where(hit, parts[slot][0], high)
                    low = jnp.where(hit, parts[slot][1], low)
                at = pl.ds(pl.multiple_of((step * unroll + inner) * CAP, CAP), CAP)
                coupling_high[at, at_lanes] = high
                coupling_low[at, at_lanes] = low
            return row + jnp.int16(CAP * unroll)

        lax.fori_loop(
            0,
            blocks // unroll,
            source_rows,
            lax.broadcasted_iota(I32, wide, 0).astype(jnp.int16),
        )
        return carry

    lax.fori_loop(0, width // LANES, column_block, 0)


def prepare_kernel(entry_rows, weight_rows, coupling_high, coupling_low):
    half = coupling_high.shape[1]
    build(entry_rows.at[:, :half], weight_rows.at[:, :half], coupling_high, coupling_low)


def prepare_cut_kernel(after, entry_rows, weight_rows, cut_high, cut_low, cut_halo):
    lanes = cut_high.shape[1]
    half = entry_rows.shape[1] - lanes
    build(entry_rows.at[:, half:], weight_rows.at[:, half:], cut_high, cut_low)
    nodes = cut_high.shape[0] - lanes
    cut_halo[...] = jnp.transpose(cut_high[nodes:].astype(F32) + cut_low[nodes:].astype(F32))


def relay_kernel(*refs):
    count = (len(refs) - 1) // 2
    for source, target in zip(refs[1 : 1 + count], refs[1 + count :]):
        target[...] = source[...]


def conductance_kernel(place, near_operating, operating, table, picked, conductances):
    rows, nodes = operating.shape
    side = place[0] % 2
    for at, values in ((side, operating), (1 - side, near_operating)):
        conductances[pl.ds(pl.multiple_of(at * rows, 8), rows), :nodes] = conductance(
            values[...], table[...]
        )
    conductances[:, nodes:] = pick(conductances[:, :nodes], picked[...])


def coupled(high, stacked, coupling_high, coupling_low, sources, lanes):
    rows = high.shape[0]
    both = dot(stacked, coupling_high[sources, lanes])
    return both[:rows] + both[rows:] + dot(high, coupling_low[sources, lanes])


def packet_layout(steps, times):
    shared = steps * CAP <= LANES
    return shared, times if shared else 0


def packet_steps(steps):
    return [(2,), (1, 3)] if steps == 3 else [(step,) for step in range(1, steps + 1)]


def wave_kernel(*refs, pieces, steps):
    vectors = refs[1 : 1 + pieces]
    (
        forward,
        conductances,
        picked,
        coupling_high,
        coupling_low,
        linear,
        capacity,
        cut_halo,
        field_high,
        field_low,
        wave,
        current,
        cut_current,
    ) = refs[1 + pieces : 1 + pieces + 13]
    sent = refs[1 + pieces + 13 :]
    side = refs[0][0] % 2
    rows, nodes = vectors[0].shape
    lanes = picked.shape[1]
    times = wave.shape[0]
    half = linear.shape[1] - lanes
    for index in range(pieces):
        at = slice(index * rows, (index + 1) * rows)
        field_high[at, :nodes], field_low[at, :nodes] = split(vectors[index][...])
    field_high[:, nodes:] = dot(field_high[:, :nodes], picked[...]).astype(BF16)
    field_low[:, nodes:] = dot(field_low[:, :nodes], picked[...]).astype(BF16)
    wave[...] = dot_split(
        (forward[0, :times], forward[1, :times]), (field_high[...], field_low[...])
    )
    slope = dot_split(
        (forward[0, times : 2 * times], forward[1, times : 2 * times]),
        (field_high[:, nodes:], field_low[:, nodes:]),
    )
    high, low = split(conductances[:, :nodes] * wave[:, :nodes])
    current[:times] = high
    current[times:] = low
    at_cut = conductances[:, nodes:] * wave[:, nodes:]
    cut_current[...] = jnp.transpose(at_cut)
    image = (
        linear[:, half:] * wave[:, nodes:]
        + at_cut
        + capacity[:, half:] * slope
        + coupled(
            high, current[...], coupling_high, coupling_low, slice(0, nodes), slice(None)
        )
    )
    image = jnp.transpose(image)
    at_cut = jnp.transpose(conductances[:, nodes:])
    slots = steps * CAP
    shared, start = packet_layout(steps, times)
    for target, wanted in zip(sent, packet_steps(steps)):
        target[...] = jnp.zeros(target.shape, F32)
        if shared:
            target[:slots, :times] = cut_current[:slots]
        for row, values, size in ((0, cut_halo, slots), (1, image, times), (2, at_cut, times)):
            blocks = [values[(step - 1) * CAP : step * CAP, :size] for step in wanted]
            block = blocks[0] if len(blocks) == 1 else jnp.where(side == 0, *blocks)
            target[row * CAP : (row + 1) * CAP, start : start + size] = block


def local_kernel(
    field_high,
    field_low,
    forward,
    wave,
    current,
    conductances,
    coupling_high,
    coupling_low,
    linear,
    capacity,
    place,
    load,
    slope,
    own_wave,
    dual,
    dual_slope,
):
    times, half = load.shape
    sources = slice(0, current.shape[1])
    mine = half_of(place[0] % 2, half)
    others = dot_split(
        (forward[0, times:], forward[1, times:]), (field_high[:, mine], field_low[:, mine])
    )
    slope[...] = capacity[:, :half] * others[:times]
    dual[...] = others[times : 2 * times]
    dual_slope[...] = capacity[:, :half] * others[2 * times :]
    own_wave[...] = wave[:, mine]
    load[...] = own_wave[...] * (linear[:, :half] + conductances[:, mine])
    for lanes in blocks_of(0, half // 2):
        load[:, lanes] += coupled(
            current[:times], current[...], coupling_high, coupling_low, sources, lanes
        )


def local_rest_kernel(load, current, coupling_high, coupling_low, rest):
    times, half = load.shape
    sources = slice(0, current.shape[1])
    for lanes, at in zip(blocks_of(half // 2, half), blocks_of(0, half // 2)):
        rest[:, at] = load[:, lanes] + coupled(
            current[:times], current[...], coupling_high, coupling_low, sources, lanes
        )


def blocks_of(start, stop, step=256):
    return [slice(at, at + step) for at in range(start, stop, step)]


def signed_sums(values):
    rows = values.shape[0]
    folded = functools.reduce(jnp.add, [values[row : row + 8] for row in range(0, rows, 8)])
    even = lax.broadcasted_iota(I32, folded.shape, 0) % 2 == 0
    return (
        jnp.sum(folded, axis=0, keepdims=True),
        jnp.sum(jnp.where(even, folded, -folded), axis=0, keepdims=True),
    )


def analysed(back, load):
    spectrum = dot_split((back[0], back[1]), split(load))
    middle = spectrum.shape[0] // 2
    return spectrum[:middle], spectrum[middle:]


def unpack(side, arrived, others, cut_current, lanes):
    steps = len(arrived)
    times = cut_current.shape[1]
    if steps == 3:
        both, own, near = (packet[...] for packet in arrived)
        arrived = [
            jnp.where(side == 0, own, near),
            both,
            jnp.where(side == 0, near, own),
        ]
    slots = steps * CAP
    blank = jnp.zeros((lanes - slots, times), F32)

    def stack(blocks):
        return jnp.transpose(jnp.concatenate([*blocks, blank], axis=0))

    def sender(step, block):
        at = slice((block - 1) * CAP, block * CAP)
        if step == 0:
            return cut_current[at]
        return others[0][step, at] if others else arrived[step - 1][at, :times]

    current = stack([sender(step, step) for step in range(1, steps + 1)])
    return arrived, stack, sender, current


def first_kernel(*refs, steps, apart):
    arrived, others = refs[1 : steps + 1], refs[steps + 1 : steps + 1 + apart]
    (
        cut_current,
        local_load,
        local_rest,
        slope,
        own_wave,
        coupling_high,
        coupling_low,
        image,
        load,
        sums,
    ) = refs[1 + steps + apart :]
    half = load.shape[1]
    lanes = -(-steps * CAP // LANES) * LANES
    nodes = coupling_high.shape[0] - lanes
    current = unpack(refs[0][0] % 2, arrived, others, cut_current, lanes)[-1]
    high, low = split(current)
    share = coupled(
        high,
        jnp.concatenate([high, low], axis=0),
        coupling_high,
        coupling_low,
        slice(nodes, None),
        slice(0, half),
    )
    load[:, : half // 2] = local_load[:, : half // 2] + share[:, : half // 2]
    load[:, half // 2 :] = local_rest[...] + share[:, half // 2 :]
    answer = load[...] + slope[...]
    image[...] = answer
    lines = [*signed_sums(answer), *signed_sums(own_wave[...])]
    sums[...] = jnp.concatenate(lines + [jnp.zeros((4, half), F32)], axis=0)


def spread_kernel(*refs, steps, apart):
    arrived, others = refs[1 : steps + 1], refs[steps + 1 : steps + 1 + apart]
    cut_current, image, back, halo, kept, sent = refs[1 + steps + apart :]
    times = image.shape[0]
    slots = steps * CAP
    start = packet_layout(steps, times)[1]
    arrived, stack, sender, _ = unpack(
        refs[0][0] % 2, arrived, others, cut_current, halo.shape[1]
    )
    kept[...], sent[...] = analysed(back, image[...])
    currents = []
    for step in range(1, steps + 1):
        theirs = jnp.concatenate(
            [sender(step ^ block, block) for block in range(1, steps + 1)], axis=0
        )
        gains = arrived[step - 1][:CAP, start : start + slots]
        image_part = arrived[step - 1][CAP : 2 * CAP, start : start + times]
        there = arrived[step - 1][2 * CAP : 3 * CAP, start : start + times]
        currents.append(there * (image_part + dot_split(split(gains), split(theirs))))
    halo[...] = stack(currents)


def second_kernel(
    place,
    halo,
    near_image,
    image,
    back,
    conductances,
    coupling_high,
    coupling_low,
    linear,
    load,
    kept,
    sent,
    current,
):
    times, half = image.shape
    nodes = current.shape[1]
    side = place[0] % 2
    mine, other = half_of(side, half), half_of(1 - side, half)
    for at, field in ((mine, image), (other, near_image)):
        current[:times, at], current[times:, at] = split(conductances[:, at] * field[...])
    load[...] = image[...] * (linear[:, :half] + conductances[:, mine])
    high, low = split(halo[...])
    halo_stacked = jnp.concatenate([high, low], axis=0)
    for lanes in blocks_of(0, half):
        load[:, lanes] += coupled(
            current[:times], current[...], coupling_high, coupling_low, slice(0, nodes), lanes
        ) + coupled(high, halo_stacked, coupling_high, coupling_low, slice(nodes, None), lanes)
    kept[...], sent[...] = analysed(back, load[...])


def sum_kernel(after, *refs):
    total = refs[0][...]
    for value in refs[1:-1]:
        total = total + value[...]
    refs[-1][...] = total


def turned(field, first_pair, half_order):
    count = field.shape[0]
    row = lax.broadcasted_iota(I32, field.shape, 0)
    scaling = (first_pair + row // 2).astype(F32) * (1.0 / half_order)
    above = pltpu.roll(field, count - 1, 0)
    below = pltpu.roll(field, 1, 0)
    return scaling * jnp.where(row % 2 == 0, above, -below)


def combine_kernel(after, place, kept, arrived, *targets):
    half = kept.shape[1]
    rows = targets[0].shape[0]
    side = place[0] % 2
    for index, target in enumerate(targets):
        at = slice(index * rows, (index + 1) * rows)
        target[:, half_of(side, half)] = kept[at]
        target[:, half_of(1 - side, half)] = arrived[at]


def joined(parts):
    return functools.reduce(jnp.add, [part[...] for part in parts])


def guess(cross, squares):
    ratio = cross / jnp.where(squares > 0.0, squares, 1.0)
    return jnp.clip(jnp.where(squares > 0.0, ratio, 0.0), -40.0, 40.0)


def products_kernel(
    place,
    vector,
    load,
    second_load,
    image,
    wave,
    dual,
    dual_slope,
    own_sums,
    far_sums,
    scalars,
    *,
    length,
):
    start, first = wave[...], load[...]
    field, sums = vector[...], own_sums[...] + far_sums[...]
    coeff = guess(scalar_sum(start * image[...]), scalar_sum(start * start))
    rest = image[...] - coeff * start
    change = second_load[...] - coeff * first
    start_sums = [sums[line + 2 : line + 3] for line in (0, 1)]
    rest_sums = [sums[line : line + 1] - coeff * start_sums[line] for line in (0, 1)]
    start_ends, rest_ends, first_ends, change_ends = (
        signed_sums(values) for values in (start, rest, first, change)
    )

    def mixed(values, value_sums, others, other_ends):
        ends = value_sums[0] * other_ends[0] + value_sums[1] * other_ends[1]
        return lane_sums(values * others) * (2.0 / length) - lane_sums(ends) * (
            1.0 / length / length
        )

    found = [
        lane_sums(field * field),
        lane_sums(dual[...] * rest),
        lane_sums(dual[...] * start),
        mixed(rest, rest_sums, rest, rest_ends),
        mixed(rest, rest_sums, start, start_ends) + mixed(start, start_sums, rest, rest_ends),
        mixed(start, start_sums, start, start_ends),
        lane_sums(dual[...] * change - dual_slope[...] * rest),
        lane_sums(dual[...] * first - dual_slope[...] * start),
        mixed(rest, rest_sums, change, change_ends),
        mixed(rest, rest_sums, first, first_ends) + mixed(start, start_sums, change, change_ends),
        mixed(start, start_sums, first, first_ends),
    ]
    device = place[1] * place[3] + place[0]
    lane = lax.broadcasted_iota(I32, scalars.shape, 1)
    column = jnp.concatenate(found + [jnp.zeros((5, LANES), F32)], axis=0)
    column = jnp.sum(column, axis=1, keepdims=True)
    line = lax.broadcasted_iota(I32, column.shape, 0)
    column = jnp.where(line == len(found), coeff, column)
    scalars[...] = jnp.where(lane == device, column, 0.0)


def settle_kernel(place, vector, capacity, *refs, length):
    *parts, answer, slope, skew = refs
    rows = vector.shape[0]
    first_pair = place[0] * (rows // 2)
    answer[...] = joined(parts)
    field, start = answer[...], vector[...]
    slope[...] = capacity[...] * turned(field, first_pair, length // 2)
    start_slope = capacity[...] * turned(start, first_pair, length // 2)
    products = [
        scalar_sum(field * slope[...]),
        scalar_sum(field * start_slope + start * slope[...]),
        scalar_sum(start * start_slope),
        jnp.zeros((5, 1), F32),
    ]
    skew[...] = jnp.broadcast_to(jnp.concatenate(products, axis=0), skew.shape)


def last_kernel(
    gathered,
    vector,
    answer,
    slope,
    skew,
    *refs,
    entries,
    devices,
):
    *parts, basis_two, next_residue = refs
    own = [gathered[line : line + 1, :] for line in range(12)]
    local = own.pop()

    def everywhere(values):
        return jnp.sum(values, axis=1, keepdims=True) / entries

    scale_square = everywhere(own[0]) + EPSILON
    coeff = everywhere(own[1] + local * own[2]) / scale_square
    near = local - coeff
    rest_square = everywhere(own[3] + near * (own[4] + near * own[5]))
    along_one = everywhere(own[6] + near * own[7])
    along_two = everywhere(own[8] + near * (own[9] + near * own[10]))
    turn = skew[0:1, :1] - coeff * (skew[1:2, :1] - coeff * skew[2:3, :1])
    along_two = along_two + turn * (devices / entries)
    scale = jnp.sqrt(scale_square)
    second_norm = jnp.sqrt(jnp.maximum(rest_square, 0.0) / scale_square + EPSILON)
    inverse = 1.0 / (second_norm * scale)
    along_one = along_one * inverse / scale_square
    along_two = along_two * inverse * inverse
    second = (answer[...] - coeff * vector[...]) * inverse
    basis_two[...] = second
    next_residue[...] = (
        (joined(parts) + slope[...] - coeff * answer[...]) * inverse
        - along_one * vector[...]
        - along_two * second
    )


VMEM = pl.BlockSpec(memory_space=pltpu.VMEM)
SMEM = pl.BlockSpec(memory_space=pltpu.SMEM)


HBM = pl.BlockSpec(memory_space=pltpu.HBM)


def run(kernel, name, specs, operands, outs, scratch=(), micros=1, room=12, spaces=None):
    spaces = spaces or [pltpu.VMEM] * len(outs)
    return pl.pallas_call(
        kernel,
        out_shape=[space(shape, dtype) for space, (shape, dtype) in zip(spaces, outs)],
        in_specs=specs,
        out_specs=[pl.BlockSpec(memory_space=space) for space in spaces],
        scratch_shapes=list(scratch),
        compiler_params=pltpu.CompilerParams(vmem_limit_bytes=room * 2**20),
        cost_estimate=pl.CostEstimate(
            flops=0, bytes_accessed=int(micros * 3e6), transcendentals=0
        ),
        name=name,
    )(*operands)


def swap(value, mask):
    count = lax.axis_size("samples")
    return lax.ppermute(value, "samples", [(at, at ^ mask) for at in range(count)])


def trade(value, masks):
    count, parts = lax.axis_size("nodes"), lax.axis_size("samples")
    pairs = [
        (at * parts + which, (at ^ masks[which % len(masks)]) * parts + which)
        for at in range(count)
        for which in range(parts)
    ]
    return lax.ppermute(value, ("nodes", "samples"), pairs)


def add(after, terms):
    (value,) = run(
        sum_kernel,
        "sum",
        [VMEM] * (len(terms) + 1),
        (after, *terms),
        [(terms[0].shape, F32)],
    )
    return value


def exchange(value, axis, after):
    count, stride, terms = lax.axis_size(axis), 1, [value]
    while stride < count:
        if stride > 1:
            value = add(after, terms)
        radix = 4 if count // stride % 4 == 0 else 2
        terms = [value] + [
            lax.ppermute(value, axis, [(at, at ^ (step * stride)) for at in range(count)])
            for step in range(1, radix)
        ]
        stride *= radix
    return terms


def hand_out(after, place, kept, arrived):
    count = lax.axis_size("samples") // 2
    field = ((kept.shape[0] // count, 2 * kept.shape[1]), F32)
    parts = run(
        combine_kernel,
        "combine",
        [VMEM, SMEM] + [VMEM] * 2,
        (after, place, kept, arrived),
        [field] * count,
    )
    return [parts[0]] + [swap(part, 2 * mask) for mask, part in enumerate(parts) if mask]


def shards(
    vector, operating, table, linear, capacity, weights, degree, neighbours, boundary, send_list
):
    rows, nodes = vector.shape
    parts, node_groups = lax.axis_size("samples"), lax.axis_size("nodes")
    length, half, times = rows * parts, nodes // 2, 2 * rows
    entries = float(length * nodes * node_groups)
    steps = node_groups - 1
    slots = steps * CAP
    lanes = -(-slots // LANES) * LANES
    sources, width = nodes + lanes, half + lanes
    forward, back = (jnp.asarray(table) for table in transform_tables(length, parts))
    linear, capacity, degree, table = (
        value.reshape(1, -1) for value in (linear, capacity, degree, table)
    )

    slot_count = weights.shape[0]
    (
        own_vector,
        picked,
        linear_wide,
        capacity_wide,
        capacity,
        table,
        own_operating,
        forward,
        back,
        entry_rows,
        weight_rows,
        place,
    ) = run(
        fetch_kernel,
        "fetch",
        [HBM] * 12,
        tuple(
            pltpu.with_memory_space_constraint(value, pltpu.HBM)
            for value in (vector, neighbours, weights, degree, linear, capacity, send_list)
            + (boundary, table, operating, forward, back)
        ),
        [
            ((rows, nodes), F32),
            ((nodes, lanes), BF16),
            ((1, width), F32),
            ((1, width), F32),
            ((1, nodes), F32),
            (table.shape, F32),
            ((rows, nodes), F32),
            (forward.shape[1:], BF16),
            (back.shape[1:], BF16),
            ((slot_count, width), I32),
            ((slot_count, width), F32),
            ((4,), I32),
        ],
        scratch=[
            pltpu.VMEM((slot_count, nodes), I32),
            pltpu.VMEM((slot_count, nodes), F32),
            pltpu.VMEM((1, nodes), I32),
            pltpu.VMEM((1, nodes), F32),
            pltpu.SMEM(send_list.shape, I32),
            pltpu.SMEM(boundary.shape, I32),
            pltpu.SemaphoreType.DMA((12,)),
        ],
        micros=2,
        spaces=[pltpu.VMEM] * 11 + [pltpu.SMEM],
    )
    coupling_high, coupling_low = run(
        prepare_kernel,
        "prepare",
        [VMEM] * 2,
        (entry_rows, weight_rows),
        [((sources, half), BF16)] * 2,
        micros=6,
    )
    near_operating = swap(operating, 1)
    vectors, bit = [vector], parts // 2
    while bit > 1:
        vectors = vectors + [swap(piece, bit) for piece in vectors]
        bit //= 2
    far = len(vectors) - 1
    if far:
        vectors[1:] = run(
            relay_kernel,
            "relay",
            [VMEM] * (far + 1),
            (coupling_low, *vectors[1:]),
            [((rows, nodes), F32)] * far,
        )
    vectors = vectors + [swap(piece, 1) for piece in vectors]
    vectors[0] = own_vector
    cut_high, cut_low, cut_halo = run(
        prepare_cut_kernel,
        "prepare_cut",
        [VMEM] * 3,
        (vectors[far], entry_rows, weight_rows),
        [((sources, lanes), BF16), ((sources, lanes), BF16), ((lanes, lanes), F32)],
        micros=1,
    )
    (conductances,) = run(
        conductance_kernel,
        "conductance",
        [SMEM] + [VMEM] * 4,
        (place, near_operating, own_operating, table, picked),
        [((times, sources), F32)],
        micros=1,
    )

    wide = ((times, half), F32)
    shared, start = packet_layout(steps, times)
    packet = (
        max(slots if shared else 0, 3 * CAP),
        -(-(start + max(times, slots)) // LANES) * LANES,
    )
    field_high, field_low, wave, current, cut_current, *sent = run(
        functools.partial(wave_kernel, pieces=parts, steps=steps),
        "wave",
        [SMEM] + [VMEM] * (parts + 8),
        (place, *vectors, forward, conductances, picked, cut_high, cut_low)
        + (linear_wide, capacity_wide, cut_halo),
        [
            ((length, sources), BF16),
            ((length, sources), BF16),
            ((times, sources), F32),
            ((2 * times, nodes), BF16),
            ((lanes, times), F32),
        ]
        + [(packet, F32)] * len(packet_steps(steps)),
        micros=2,
    )
    arrived = [trade(packet, masks) for packet, masks in zip(sent, packet_steps(steps))]
    others = []
    if not shared:
        gathered = lax.all_gather(cut_current, "nodes")
        distance = jnp.arange(node_groups, dtype=I32)
        others = [gathered[lax.axis_index("nodes") ^ distance]]
    local_load, slope, own_wave, dual, dual_slope = run(
        local_kernel,
        "local",
        [VMEM] * 10 + [SMEM],
        (field_high, field_low, forward, wave, current, conductances)
        + (coupling_high, coupling_low, linear_wide, capacity_wide, place),
        [wide] * 5,
        micros=3,
    )
    if steps == 3:
        (traded,) = run(
            relay_kernel, "relay", [VMEM] * 2, (dual, arrived[-1]), [(packet, F32)]
        )
        arrived[-1:] = [traded, swap(traded, 1)]
    (local_rest,) = run(
        local_rest_kernel,
        "local_rest",
        [VMEM] * 4,
        (local_load, current, coupling_high, coupling_low),
        [((times, half // 2), F32)],
    )
    block = ((length // 2, half), F32)
    packets = (place, *arrived, *others, cut_current)
    packet_specs = [SMEM] + [VMEM] * (len(packets) - 1)
    image, load, own_sums = run(
        functools.partial(first_kernel, steps=steps, apart=len(others)),
        "first",
        packet_specs + [VMEM] * 6,
        (*packets, local_load, local_rest, slope, own_wave, coupling_high, coupling_low),
        [wide, wide, ((8, half), F32)],
        micros=1,
    )
    halo, kept, sent = run(
        functools.partial(spread_kernel, steps=steps, apart=len(others)),
        "spread",
        packet_specs + [VMEM] * 2,
        (*packets, image, back),
        [((times, lanes), F32), block, block],
        micros=1,
    )
    near_image = swap(image, 1)
    bit = 2
    while 2 * bit < parts:
        own_sums = own_sums + swap(own_sums, bit)
        bit *= 2
    far_sums = swap(own_sums, bit) if bit < parts else jnp.zeros_like(own_sums)
    arrived = swap(sent, 1)

    second_load, second_kept, second_sent = run(
        second_kernel,
        "second",
        [SMEM] + [VMEM] * 8,
        (place, halo, near_image, image, back, conductances)
        + (coupling_high, coupling_low, linear_wide),
        [wide, block, block],
        scratch=[pltpu.VMEM((2 * times, nodes), BF16)],
        micros=3,
    )
    answer_parts = hand_out(load, place, kept, arrived)
    (second_sent,) = run(
        relay_kernel,
        "relay",
        [VMEM] * 2,
        (far_sums, second_sent),
        [(second_sent.shape, F32)],
    )
    second_arrived = swap(second_sent, 1)
    gathered = -(-node_groups * parts // LANES) * LANES
    (scalars,) = run(
        functools.partial(products_kernel, length=length),
        "products",
        [SMEM] + [VMEM] * 9,
        (place, own_vector, load, second_load, image, own_wave, dual, dual_slope)
        + (own_sums, far_sums),
        [((16, gathered), F32)],
        micros=1,
    )
    second_parts = hand_out(scalars, place, second_kept, second_arrived)
    scalars = add(cut_halo, exchange(scalars, "nodes", cut_halo))
    answer, slope, skew = run(
        functools.partial(settle_kernel, length=length),
        "settle",
        [SMEM] + [VMEM] * (len(answer_parts) + 2),
        (place, own_vector, capacity, *answer_parts),
        [((rows, nodes), F32), ((rows, nodes), F32), ((8, LANES), F32)],
        micros=1,
    )
    scalars = add(skew, exchange(scalars, "samples", cut_halo))
    field = jax.ShapeDtypeStruct((rows, nodes), F32)
    return tuple(
        pl.pallas_call(
            functools.partial(
                last_kernel, entries=entries, devices=float(node_groups * parts)
            ),
            out_shape=[field, field],
            in_specs=[VMEM] * (5 + len(second_parts)),
            out_specs=[VMEM] * 2,
            compiler_params=pltpu.CompilerParams(vmem_limit_bytes=12 * 2**20),
            name="last",
        )(scalars, own_vector, answer, slope, skew, *second_parts)
    )


def solution(mesh):
    return jax.shard_map(
        shards,
        mesh=mesh,
        in_specs=(
            P("samples", ("copies", "nodes")),
            P("samples", ("copies", "nodes")),
            P(),
            P("nodes"),
            P("nodes"),
            P(None, "nodes"),
            P("nodes"),
            P(None, "nodes"),
            P("nodes"),
            P("nodes"),
        ),
        out_specs=(P("samples", ("copies", "nodes")), P("samples", ("copies", "nodes"))),
        check_vma=False,
    )
```

```python
import functools
import math

import jax
import jax.numpy as jnp
import numpy as np
from jax import lax
from jax.experimental import pallas as pl
from jax.experimental.pallas import tpu as pltpu
from jax.sharding import PartitionSpec as P

CAP = 16
EPSILON = 1e-06
LANES = 128
BF16 = jnp.bfloat16
F32 = jnp.float32
I32 = jnp.int32


def spectral_tables(length):
    indices = np.arange(length)
    frequency = np.where(indices == 1, length // 2, indices // 2)
    angles = (indices[:, None] * frequency[None, :] % length) * (2.0 * math.pi / length)
    cosine_column = (indices % 2 == 0) | (indices == 1)
    synthesis = np.where(cosine_column[None, :], np.cos(angles), np.sin(angles))
    factor = np.where(indices < 2, 1.0 / length, 2.0 / length)
    analysis = synthesis.T * factor[:, None]
    turn = np.zeros((length, length))
    for pair in range(length // 2):
        turn[2 * pair, 2 * pair + 1] = pair / (length // 2)
        turn[2 * pair + 1, 2 * pair] = -pair / (length // 2)
    return synthesis, analysis, turn


def halves(table):
    high = table.astype(np.float32).astype(BF16)
    low = (table - high.astype(np.float64)).astype(np.float32).astype(BF16)
    return np.stack([high, low])


def piece_order(count):
    masks, bit = [0], count // 2
    while bit:
        masks = masks + [mask ^ bit for mask in masks]
        bit //= 2
    return masks


def transform_tables(length, parts):
    synthesis, analysis, turn = spectral_tables(length)
    slope, dual_slope = synthesis @ turn, analysis.T @ turn
    rows = length // parts
    forward, back = [], []
    for place in range(parts):
        times = np.arange(place // 2 * 2 * rows, (place // 2 + 1) * 2 * rows)
        block = lambda owner: np.arange(owner * rows, (owner + 1) * rows)
        coefs = np.concatenate([block(place ^ mask) for mask in piece_order(parts)])
        forward.append(
            np.concatenate(
                [
                    synthesis[np.ix_(times, coefs)],
                    slope[np.ix_(times, coefs)],
                    analysis[np.ix_(coefs, times)].T,
                    dual_slope[np.ix_(times, coefs)],
                ]
            )
        )
        sent = np.concatenate(
            [block(place ^ mask ^ side) for side in (0, 1) for mask in range(0, parts, 2)]
        )
        back.append(analysis[np.ix_(sent, times)])
    return (
        np.moveaxis(halves(np.stack(forward)), 0, 1),
        np.moveaxis(halves(np.stack(back)), 0, 1),
    )


def split(values):
    high = values.astype(BF16)
    return high, (values - high.astype(F32)).astype(BF16)


def dot(first, second):
    return jnp.dot(first, second, preferred_element_type=F32)


def dot_split(first, second):
    (first_high, first_low), (second_high, second_low) = first, second
    rows = first_high.shape[0]
    both = dot(jnp.concatenate([first_high, first_low], axis=0), second_high)
    return both[:rows] + both[rows:] + dot(first_high, second_low)


def lane_sums(values):
    rows, lanes = values.shape
    step = 8 if rows % 8 == 0 else rows
    total = functools.reduce(
        jnp.add,
        [
            values[row : row + step, lane : lane + LANES]
            for row in range(0, rows, step)
            for lane in range(0, lanes, LANES)
        ],
    )
    return jnp.sum(total, axis=0, keepdims=True)


def half_of(side, half):
    return pl.ds(pl.multiple_of(side * half, LANES), half)


def scalar_sum(values):
    return jnp.sum(lane_sums(values), axis=1, keepdims=True)


def pick(values, picked):
    high, _ = split(values)
    middle, low = split(values - high.astype(F32))
    rows = values.shape[0]
    found = dot(jnp.concatenate([high, middle, low], axis=0), picked)
    return found[:rows] + (found[rows : 2 * rows] + found[2 * rows :])


def conductance(operating, table):
    points = table.shape[1]
    spread = jnp.concatenate([table, jnp.zeros((1, LANES - points), F32)], axis=1)
    spread = jnp.broadcast_to(spread, (operating.shape[0], LANES))
    pieces = []
    for block in range(operating.shape[1] // LANES):
        scaled = (operating[:, block * LANES : (block + 1) * LANES] + 4.0) * ((points - 1) / 8.0)
        knot = jnp.clip(jnp.floor(scaled), 0.0, points - 2.0)
        weight = scaled - knot
        place = knot.astype(I32)
        left = jnp.take_along_axis(spread, place, axis=1, mode="promise_in_bounds")
        right = jnp.take_along_axis(spread, place + 1, axis=1, mode="promise_in_bounds")
        pieces.append(left + weight * (right - left))
    return jnp.concatenate(pieces, axis=1)


def fetch_kernel(
    neighbours_in,
    weights_in,
    degree_in,
    linear_in,
    capacity_in,
    send_list_in,
    boundary_in,
    table_in,
    operating_in,
    picked,
    linear,
    capacity,
    capacity_all,
    entry_rows,
    weight_rows,
    own_conductances,
    place,
    table,
    operating,
    neighbours,
    weights,
    degree,
    linear_all,
    send_list,
    boundary,
    copied,
):
    place[0], place[1] = lax.axis_index("samples"), lax.axis_index("nodes")
    place[2], place[3] = lax.axis_size("nodes"), lax.axis_size("samples")
    slots, nodes = neighbours.shape
    lanes = picked.shape[1]
    half = linear.shape[1] - lanes
    node_groups = send_list.shape[0] // CAP
    side, part = place[0] % 2, place[1]
    copies = [
        pltpu.make_async_copy(source, target, copied.at[index])
        for index, (source, target) in enumerate(
            [
                (send_list_in, send_list),
                (boundary_in, boundary),
                (neighbours_in, neighbours),
                (weights_in, weights),
                (degree_in, degree),
                (linear_in, linear_all),
                (capacity_in, capacity_all),
                (table_in, table),
                (operating_in, operating),
            ]
        )
    ]
    for copy in copies:
        copy.start()
    for copy in copies[:2]:
        copy.wait()

    lane = lax.broadcasted_iota(I32, (8, lanes), 1)

    def name(slot, found):
        target = part ^ (slot // CAP + 1)
        node = boundary[send_list[target * CAP + slot % CAP]]
        return jnp.where(lane == slot, node, found)

    cut_nodes = lax.fori_loop(
        0, (node_groups - 1) * CAP, name, jnp.full((8, lanes), -1, I32), unroll=8
    )
    hit = lax.broadcasted_iota(I32, (nodes, lanes), 0) == cut_nodes[:1]
    picked[...] = jnp.where(hit, 1.0, 0.0).astype(BF16)

    for copy in copies[2:7]:
        copy.wait()
    mine = half_of(side, half)
    entry = neighbours[...]
    remote = entry - nodes
    distance = part ^ (remote >> 4)
    entry = jnp.where(remote < 0, entry, nodes + (distance - 1) * CAP + (remote & 15))
    live = lax.broadcasted_iota(I32, (slots, nodes), 0) < degree[...]
    neighbours[...] = entry
    weights[...] = jnp.where(live, weights[...], 0.0)
    columns = jnp.concatenate(
        [
            entry.astype(F32),
            weights[...],
            linear_all[...],
            capacity_all[...],
            jnp.zeros((6, nodes), F32),
        ],
        axis=0,
    )
    at_cut = pick(columns, picked[...])
    linear[:, :half] = linear_all[:, mine]
    linear[:, half:] = at_cut[2 * slots : 2 * slots + 1]
    capacity[:, :half] = capacity_all[:, mine]
    capacity[:, half:] = at_cut[2 * slots + 1 : 2 * slots + 2]
    entry_rows[:, :half] = neighbours[:, mine]
    entry_rows[:, half:] = at_cut[:slots].astype(I32)
    weight_rows[:, :half] = weights[:, mine]
    weight_rows[:, half:] = at_cut[slots : 2 * slots]
    entries = [entry_rows[slot : slot + 1, :] for slot in range(slots)]
    gains = [weight_rows[slot : slot + 1, :] for slot in range(slots)]
    for slot in range(slots):
        for later in range(slot + 1, slots):
            same = entries[slot] == entries[later]
            gains[slot] = gains[slot] + jnp.where(same, gains[later], 0.0)
            entries[later] = jnp.where(same, -1, entries[later])
    for slot in range(slots):
        entry_rows[slot : slot + 1, :] = entries[slot]
        weight_rows[slot : slot + 1, :] = gains[slot]
    for copy in copies[7:]:
        copy.wait()
    own_conductances[...] = conductance(operating[...], table[...])


def build(entry_rows, weight_rows, coupling_high, coupling_low):
    slots, width = entry_rows.shape
    sources = coupling_high.shape[0]
    blocks = sources // CAP
    unroll = max(count for count in range(1, 35) if blocks % count == 0)
    wide = (CAP, LANES)

    def column_block(block, carry):
        at_lanes = pl.ds(pl.multiple_of(block * LANES, LANES), LANES)
        names = [
            jnp.broadcast_to(entry_rows[slot : slot + 1, at_lanes], wide).astype(jnp.int16)
            for slot in range(slots)
        ]
        parts = [
            split(jnp.broadcast_to(weight_rows[slot : slot + 1, at_lanes], wide))
            for slot in range(slots)
        ]

        def source_rows(step, row):
            for inner in range(unroll):
                high = jnp.zeros(wide, BF16)
                low = jnp.zeros(wide, BF16)
                for slot in range(slots):
                    hit = names[slot] == row + jnp.int16(CAP * inner)
                    high = jnp.where(hit, parts[slot][0], high)
                    low = jnp.where(hit, parts[slot][1], low)
                at = pl.ds(pl.multiple_of((step * unroll + inner) * CAP, CAP), CAP)
                coupling_high[at, at_lanes] = high
                coupling_low[at, at_lanes] = low
            return row + jnp.int16(CAP * unroll)

        lax.fori_loop(
            0,
            blocks // unroll,
            source_rows,
            lax.broadcasted_iota(I32, wide, 0).astype(jnp.int16),
        )
        return carry

    lax.fori_loop(0, width // LANES, column_block, 0)


def prepare_kernel(
    place,
    entry_rows,
    weight_rows,
    vector_in,
    forward_in,
    back_in,
    coupling_high,
    coupling_low,
    vector,
    forward,
    back,
    copied,
):
    copies = [
        pltpu.make_async_copy(source, target, copied.at[index])
        for index, (source, target) in enumerate(
            [
                (vector_in, vector),
                (forward_in.at[place[0]], forward),
                (back_in.at[place[0]], back),
            ]
        )
    ]
    for copy in copies:
        copy.start()
    width = coupling_high.shape[1]
    build(entry_rows.at[:, :width], weight_rows.at[:, :width], coupling_high, coupling_low)
    for copy in copies:
        copy.wait()


def prepare_cut_kernel(after, entry_rows, weight_rows, tail_high, tail_low, cut_halo):
    width = tail_high.shape[1]
    start = entry_rows.shape[1] - width
    build(entry_rows.at[:, start:], weight_rows.at[:, start:], tail_high, tail_low)
    nodes = tail_high.shape[0] - (width - LANES)
    cut_halo[...] = jnp.transpose(
        tail_high[nodes:, LANES:].astype(F32) + tail_low[nodes:, LANES:].astype(F32)
    )


def relay_kernel(*refs):
    count = (len(refs) - 1) // 2
    for source, target in zip(refs[1 : 1 + count], refs[1 + count :]):
        target[...] = source[...]


def conductance_kernel(place, near, own, picked, conductances):
    rows, nodes = own.shape
    side = place[0] % 2
    for at, values in ((side, own), (1 - side, near)):
        conductances[pl.ds(pl.multiple_of(at * rows, 8), rows), :nodes] = values[...]
    conductances[:, nodes:] = pick(conductances[:, :nodes], picked[...])


def columns_of(coupling, sources, lanes):
    main, tail = coupling
    width = main.shape[1]
    if lanes.stop <= width:
        return main[sources, lanes]
    last = tail[sources, max(lanes.start - width, 0) : lanes.stop - width]
    if lanes.start >= width:
        return last
    return jnp.concatenate([main[sources, lanes.start : width], last], axis=1)


def coupled(high, stacked, coupling_high, coupling_low, sources, lanes):
    rows = high.shape[0]
    both = dot(stacked, columns_of(coupling_high, sources, lanes))
    return both[:rows] + both[rows:] + dot(high, columns_of(coupling_low, sources, lanes))


def packet_layout(steps, times):
    shared = steps * CAP <= LANES
    return shared, times if shared else 0


def packet_steps(steps):
    return [(2,), (1, 3)] if steps == 3 else [(step,) for step in range(1, steps + 1)]


def wave_kernel(*refs, pieces, steps):
    vectors = refs[1 : 1 + pieces]
    (
        forward,
        conductances,
        picked,
        coupling_high,
        coupling_low,
        linear,
        capacity,
        cut_halo,
        field_high,
        field_low,
        wave,
        current,
        cut_current,
    ) = refs[1 + pieces : 1 + pieces + 13]
    sent = refs[1 + pieces + 13 :]
    side = refs[0][0] % 2
    rows, nodes = vectors[0].shape
    lanes = picked.shape[1]
    times = wave.shape[0]
    half = linear.shape[1] - lanes
    for index in range(pieces):
        at = slice(index * rows, (index + 1) * rows)
        field_high[at, :nodes], field_low[at, :nodes] = split(vectors[index][...])
    field_high[:, nodes:] = dot(field_high[:, :nodes], picked[...]).astype(BF16)
    field_low[:, nodes:] = dot(field_low[:, :nodes], picked[...]).astype(BF16)
    wave[...] = dot_split(
        (forward[0, :times], forward[1, :times]), (field_high[...], field_low[...])
    )
    slope = dot_split(
        (forward[0, times : 2 * times], forward[1, times : 2 * times]),
        (field_high[:, nodes:], field_low[:, nodes:]),
    )
    high, low = split(conductances[:, :nodes] * wave[:, :nodes])
    current[:times] = high
    current[times:] = low
    at_cut = conductances[:, nodes:] * wave[:, nodes:]
    cut_current[...] = jnp.transpose(at_cut)
    image = (
        linear[:, half:] * wave[:, nodes:]
        + at_cut
        + capacity[:, half:] * slope
        + coupled(
            high,
            current[...],
            (coupling_high, coupling_high),
            (coupling_low, coupling_low),
            slice(0, nodes),
            slice(LANES, LANES + lanes),
        )
    )
    image = jnp.transpose(image)
    at_cut = jnp.transpose(conductances[:, nodes:])
    slots = steps * CAP
    shared, start = packet_layout(steps, times)
    for target, wanted in zip(sent, packet_steps(steps)):
        target[...] = jnp.zeros(target.shape, F32)
        if shared:
            target[:slots, :times] = cut_current[:slots]
        for row, values, size in ((0, cut_halo, slots), (1, image, times), (2, at_cut, times)):
            blocks = [values[(step - 1) * CAP : step * CAP, :size] for step in wanted]
            block = blocks[0] if len(blocks) == 1 else jnp.where(side == 0, *blocks)
            target[row * CAP : (row + 1) * CAP, start : start + size] = block


def local_kernel(
    field_high,
    field_low,
    forward,
    wave,
    current,
    conductances,
    coupling_high,
    coupling_low,
    tail_high,
    tail_low,
    linear,
    capacity,
    place,
    load,
    slope,
    own_wave,
    dual,
    dual_slope,
):
    times, half = load.shape
    sources = slice(0, current.shape[1])
    coupling = (coupling_high, tail_high), (coupling_low, tail_low)
    mine = half_of(place[0] % 2, half)
    others = dot_split(
        (forward[0, times:], forward[1, times:]), (field_high[:, mine], field_low[:, mine])
    )
    slope[...] = capacity[:, :half] * others[:times]
    dual[...] = others[times : 2 * times]
    dual_slope[...] = capacity[:, :half] * others[2 * times :]
    own_wave[...] = wave[:, mine]
    load[...] = own_wave[...] * (linear[:, :half] + conductances[:, mine])
    for lanes in blocks_of(0, half // 2):
        load[:, lanes] += coupled(
            current[:times], current[...], *coupling, sources, lanes
        )


def local_rest_kernel(load, current, coupling_high, coupling_low, tail_high, tail_low, rest):
    times, half = load.shape
    coupling = (coupling_high, tail_high), (coupling_low, tail_low)
    sources = slice(0, current.shape[1])
    for lanes, at in zip(blocks_of(half // 2, half), blocks_of(0, half // 2)):
        rest[:, at] = load[:, lanes] + coupled(
            current[:times], current[...], *coupling, sources, lanes
        )


def blocks_of(start, stop, step=256):
    return [slice(at, at + step) for at in range(start, stop, step)]


def signed_sums(values):
    rows = values.shape[0]
    folded = functools.reduce(jnp.add, [values[row : row + 8] for row in range(0, rows, 8)])
    even = lax.broadcasted_iota(I32, folded.shape, 0) % 2 == 0
    return (
        jnp.sum(folded, axis=0, keepdims=True),
        jnp.sum(jnp.where(even, folded, -folded), axis=0, keepdims=True),
    )


def analysed(back, load):
    spectrum = dot_split((back[0], back[1]), split(load))
    middle = spectrum.shape[0] // 2
    return spectrum[:middle], spectrum[middle:]


def unpack(side, arrived, others, cut_current, lanes):
    steps = len(arrived)
    times = cut_current.shape[1]
    if steps == 3:
        both, own, near = (packet[...] for packet in arrived)
        arrived = [
            jnp.where(side == 0, own, near),
            both,
            jnp.where(side == 0, near, own),
        ]
    slots = steps * CAP
    blank = jnp.zeros((lanes - slots, times), F32)

    def stack(blocks):
        return jnp.transpose(jnp.concatenate([*blocks, blank], axis=0))

    def sender(step, block):
        at = slice((block - 1) * CAP, block * CAP)
        if step == 0:
            return cut_current[at]
        return others[0][step, at] if others else arrived[step - 1][at, :times]

    current = stack([sender(step, step) for step in range(1, steps + 1)])
    return arrived, stack, sender, current


def first_kernel(*refs, steps, apart):
    arrived, others = refs[1 : steps + 1], refs[steps + 1 : steps + 1 + apart]
    (
        cut_current,
        local_load,
        local_rest,
        slope,
        own_wave,
        coupling_high,
        coupling_low,
        tail_high,
        tail_low,
        image,
        load,
        sums,
    ) = refs[1 + steps + apart :]
    half = load.shape[1]
    lanes = -(-steps * CAP // LANES) * LANES
    nodes = coupling_high.shape[0] - lanes
    current = unpack(refs[0][0] % 2, arrived, others, cut_current, lanes)[-1]
    high, low = split(current)
    share = coupled(
        high,
        jnp.concatenate([high, low], axis=0),
        (coupling_high, tail_high),
        (coupling_low, tail_low),
        slice(nodes, None),
        slice(0, half),
    )
    load[:, : half // 2] = local_load[:, : half // 2] + share[:, : half // 2]
    load[:, half // 2 :] = local_rest[...] + share[:, half // 2 :]
    answer = load[...] + slope[...]
    image[...] = answer
    lines = [*signed_sums(answer), *signed_sums(own_wave[...])]
    sums[...] = jnp.concatenate(lines + [jnp.zeros((4, half), F32)], axis=0)


def spread_kernel(*refs, steps, apart):
    arrived, others = refs[1 : steps + 1], refs[steps + 1 : steps + 1 + apart]
    cut_current, image, back, halo, kept, sent = refs[1 + steps + apart :]
    times = image.shape[0]
    slots = steps * CAP
    start = packet_layout(steps, times)[1]
    arrived, stack, sender, _ = unpack(
        refs[0][0] % 2, arrived, others, cut_current, halo.shape[1]
    )
    kept[...], sent[...] = analysed(back, image[...])
    currents = []
    for step in range(1, steps + 1):
        theirs = jnp.concatenate(
            [sender(step ^ block, block) for block in range(1, steps + 1)], axis=0
        )
        gains = arrived[step - 1][:CAP, start : start + slots]
        image_part = arrived[step - 1][CAP : 2 * CAP, start : start + times]
        there = arrived[step - 1][2 * CAP : 3 * CAP, start : start + times]
        currents.append(there * (image_part + dot_split(split(gains), split(theirs))))
    halo[...] = stack(currents)


def second_kernel(
    place,
    halo,
    near_image,
    image,
    back,
    conductances,
    coupling_high,
    coupling_low,
    tail_high,
    tail_low,
    linear,
    load,
    kept,
    sent,
    current,
):
    times, half = image.shape
    nodes = current.shape[1]
    side = place[0] % 2
    mine, other = half_of(side, half), half_of(1 - side, half)
    coupling = (coupling_high, tail_high), (coupling_low, tail_low)
    for at, field in ((mine, image), (other, near_image)):
        current[:times, at], current[times:, at] = split(conductances[:, at] * field[...])
    load[...] = image[...] * (linear[:, :half] + conductances[:, mine])
    high, low = split(halo[...])
    halo_stacked = jnp.concatenate([high, low], axis=0)
    for lanes in blocks_of(0, half):
        load[:, lanes] += coupled(
            current[:times], current[...], *coupling, slice(0, nodes), lanes
        ) + coupled(high, halo_stacked, *coupling, slice(nodes, None), lanes)
    kept[...], sent[...] = analysed(back, load[...])


def sum_kernel(after, *refs):
    total = refs[0][...]
    for value in refs[1:-1]:
        total = total + value[...]
    refs[-1][...] = total


def turned(field, first_pair, half_order):
    count = field.shape[0]
    row = lax.broadcasted_iota(I32, field.shape, 0)
    scaling = (first_pair + row // 2).astype(F32) * (1.0 / half_order)
    above = pltpu.roll(field, count - 1, 0)
    below = pltpu.roll(field, 1, 0)
    return scaling * jnp.where(row % 2 == 0, above, -below)


def combine_kernel(after, place, kept, arrived, *targets):
    half = kept.shape[1]
    rows = targets[0].shape[0]
    side = place[0] % 2
    for index, target in enumerate(targets):
        at = slice(index * rows, (index + 1) * rows)
        target[:, half_of(side, half)] = kept[at]
        target[:, half_of(1 - side, half)] = arrived[at]


def joined(parts):
    return functools.reduce(jnp.add, [part[...] for part in parts])


def guess(cross, squares):
    ratio = cross / jnp.where(squares > 0.0, squares, 1.0)
    return jnp.clip(jnp.where(squares > 0.0, ratio, 0.0), -40.0, 40.0)


def products_kernel(
    place,
    vector,
    load,
    second_load,
    image,
    wave,
    dual,
    dual_slope,
    own_sums,
    far_sums,
    scalars,
    *,
    length,
):
    start, first = wave[...], load[...]
    field, sums = vector[...], own_sums[...] + far_sums[...]
    coeff = guess(scalar_sum(start * image[...]), scalar_sum(start * start))
    rest = image[...] - coeff * start
    change = second_load[...] - coeff * first
    start_sums = [sums[line + 2 : line + 3] for line in (0, 1)]
    rest_sums = [sums[line : line + 1] - coeff * start_sums[line] for line in (0, 1)]
    start_ends, rest_ends, first_ends, change_ends = (
        signed_sums(values) for values in (start, rest, first, change)
    )

    def mixed(values, value_sums, others, other_ends):
        ends = value_sums[0] * other_ends[0] + value_sums[1] * other_ends[1]
        return lane_sums(values * others) * (2.0 / length) - lane_sums(ends) * (
            1.0 / length / length
        )

    found = [
        lane_sums(field * field),
        lane_sums(dual[...] * rest),
        lane_sums(dual[...] * start),
        mixed(rest, rest_sums, rest, rest_ends),
        mixed(rest, rest_sums, start, start_ends) + mixed(start, start_sums, rest, rest_ends),
        mixed(start, start_sums, start, start_ends),
        lane_sums(dual[...] * change - dual_slope[...] * rest),
        lane_sums(dual[...] * first - dual_slope[...] * start),
        mixed(rest, rest_sums, change, change_ends),
        mixed(rest, rest_sums, first, first_ends) + mixed(start, start_sums, change, change_ends),
        mixed(start, start_sums, first, first_ends),
    ]
    device = place[1] * place[3] + place[0]
    lane = lax.broadcasted_iota(I32, scalars.shape, 1)
    column = jnp.concatenate(found + [jnp.zeros((5, LANES), F32)], axis=0)
    column = jnp.sum(column, axis=1, keepdims=True)
    line = lax.broadcasted_iota(I32, column.shape, 0)
    column = jnp.where(line == len(found), coeff, column)
    scalars[...] = jnp.where(lane == device, column, 0.0)


def settle_kernel(place, vector, capacity, *refs, length):
    *parts, answer, slope, skew = refs
    rows = vector.shape[0]
    first_pair = place[0] * (rows // 2)
    answer[...] = joined(parts)
    field, start = answer[...], vector[...]
    slope[...] = capacity[...] * turned(field, first_pair, length // 2)
    start_slope = capacity[...] * turned(start, first_pair, length // 2)
    products = [
        scalar_sum(field * slope[...]),
        scalar_sum(field * start_slope + start * slope[...]),
        scalar_sum(start * start_slope),
        jnp.zeros((5, 1), F32),
    ]
    skew[...] = jnp.broadcast_to(jnp.concatenate(products, axis=0), skew.shape)


def last_kernel(
    gathered,
    vector,
    answer,
    slope,
    skew,
    *refs,
    entries,
    devices,
):
    *parts, basis_two, next_residue = refs
    own = [gathered[line : line + 1, :] for line in range(12)]
    local = own.pop()

    def everywhere(values):
        return jnp.sum(values, axis=1, keepdims=True) / entries

    scale_square = everywhere(own[0]) + EPSILON
    coeff = everywhere(own[1] + local * own[2]) / scale_square
    near = local - coeff
    rest_square = everywhere(own[3] + near * (own[4] + near * own[5]))
    along_one = everywhere(own[6] + near * own[7])
    along_two = everywhere(own[8] + near * (own[9] + near * own[10]))
    turn = skew[0:1, :1] - coeff * (skew[1:2, :1] - coeff * skew[2:3, :1])
    along_two = along_two + turn * (devices / entries)
    scale = jnp.sqrt(scale_square)
    second_norm = jnp.sqrt(jnp.maximum(rest_square, 0.0) / scale_square + EPSILON)
    inverse = 1.0 / (second_norm * scale)
    along_one = along_one * inverse / scale_square
    along_two = along_two * inverse * inverse
    second = (answer[...] - coeff * vector[...]) * inverse
    basis_two[...] = second
    next_residue[...] = (
        (joined(parts) + slope[...] - coeff * answer[...]) * inverse
        - along_one * vector[...]
        - along_two * second
    )


VMEM = pl.BlockSpec(memory_space=pltpu.VMEM)
SMEM = pl.BlockSpec(memory_space=pltpu.SMEM)


HBM = pl.BlockSpec(memory_space=pltpu.HBM)


def run(kernel, name, specs, operands, outs, scratch=(), micros=1, room=12, spaces=None):
    spaces = spaces or [pltpu.VMEM] * len(outs)
    return pl.pallas_call(
        kernel,
        out_shape=[space(shape, dtype) for space, (shape, dtype) in zip(spaces, outs)],
        in_specs=specs,
        out_specs=[pl.BlockSpec(memory_space=space) for space in spaces],
        scratch_shapes=list(scratch),
        compiler_params=pltpu.CompilerParams(vmem_limit_bytes=room * 2**20),
        cost_estimate=pl.CostEstimate(
            flops=0, bytes_accessed=int(micros * 3e6), transcendentals=0
        ),
        name=name,
    )(*operands)


def swap(value, mask):
    count = lax.axis_size("samples")
    return lax.ppermute(value, "samples", [(at, at ^ mask) for at in range(count)])


def trade(value, masks):
    count, parts = lax.axis_size("nodes"), lax.axis_size("samples")
    pairs = [
        (at * parts + which, (at ^ masks[which % len(masks)]) * parts + which)
        for at in range(count)
        for which in range(parts)
    ]
    return lax.ppermute(value, ("nodes", "samples"), pairs)


def add(after, terms):
    (value,) = run(
        sum_kernel,
        "sum",
        [VMEM] * (len(terms) + 1),
        (after, *terms),
        [(terms[0].shape, F32)],
    )
    return value


def exchange(value, axis, after):
    count, stride, terms = lax.axis_size(axis), 1, [value]
    while stride < count:
        if stride > 1:
            value = add(after, terms)
        radix = 4 if count // stride % 4 == 0 else 2
        terms = [value] + [
            lax.ppermute(value, axis, [(at, at ^ (step * stride)) for at in range(count)])
            for step in range(1, radix)
        ]
        stride *= radix
    return terms


def hand_out(after, place, kept, arrived):
    count = lax.axis_size("samples") // 2
    field = ((kept.shape[0] // count, 2 * kept.shape[1]), F32)
    parts = run(
        combine_kernel,
        "combine",
        [VMEM, SMEM] + [VMEM] * 2,
        (after, place, kept, arrived),
        [field] * count,
    )
    return [parts[0]] + [swap(part, 2 * mask) for mask, part in enumerate(parts) if mask]


def shards(
    vector, operating, table, linear, capacity, weights, degree, neighbours, boundary, send_list
):
    rows, nodes = vector.shape
    parts, node_groups = lax.axis_size("samples"), lax.axis_size("nodes")
    length, half, times = rows * parts, nodes // 2, 2 * rows
    entries = float(length * nodes * node_groups)
    steps = node_groups - 1
    slots = steps * CAP
    lanes = -(-slots // LANES) * LANES
    sources, width = nodes + lanes, half + lanes
    forward, back = (jnp.asarray(table) for table in transform_tables(length, parts))
    linear, capacity, degree, table = (
        value.reshape(1, -1) for value in (linear, capacity, degree, table)
    )

    slot_count = weights.shape[0]
    def kept_outside(*values):
        return tuple(pltpu.with_memory_space_constraint(value, pltpu.HBM) for value in values)

    (
        picked,
        linear_wide,
        capacity_wide,
        capacity_all,
        entry_rows,
        weight_rows,
        own_conductances,
        place,
    ) = run(
        fetch_kernel,
        "fetch",
        [HBM] * 9,
        kept_outside(neighbours, weights, degree, linear, capacity, send_list, boundary)
        + kept_outside(table, operating),
        [
            ((nodes, lanes), BF16),
            ((1, width), F32),
            ((1, width), F32),
            ((1, nodes), F32),
            ((slot_count, width), I32),
            ((slot_count, width), F32),
            ((rows, nodes), F32),
            ((4,), I32),
        ],
        scratch=[
            pltpu.VMEM(table.shape, F32),
            pltpu.VMEM((rows, nodes), F32),
            pltpu.VMEM((slot_count, nodes), I32),
            pltpu.VMEM((slot_count, nodes), F32),
            pltpu.VMEM((1, nodes), I32),
            pltpu.VMEM((1, nodes), F32),
            pltpu.SMEM(send_list.shape, I32),
            pltpu.SMEM(boundary.shape, I32),
            pltpu.SemaphoreType.DMA((9,)),
        ],
        micros=2,
        spaces=[pltpu.VMEM] * 7 + [pltpu.SMEM],
    )
    coupling_high, coupling_low, own_vector, forward, back = run(
        prepare_kernel,
        "prepare",
        [SMEM] + [VMEM] * 2 + [HBM] * 3,
        (place, entry_rows, weight_rows) + kept_outside(vector, forward, back),
        [
            ((sources, half - LANES), BF16),
            ((sources, half - LANES), BF16),
            ((rows, nodes), F32),
            (forward.shape[1:], BF16),
            (back.shape[1:], BF16),
        ],
        scratch=[pltpu.SemaphoreType.DMA((3,))],
        micros=6,
    )
    near_conductances = swap(own_conductances, 1)
    vectors, bit = [vector], parts // 2
    while bit > 1:
        vectors = vectors + [swap(piece, bit) for piece in vectors]
        bit //= 2
    far = len(vectors) - 1
    if far:
        vectors[1:] = run(
            relay_kernel,
            "relay",
            [VMEM] * (far + 1),
            (coupling_low, *vectors[1:]),
            [((rows, nodes), F32)] * far,
        )
    vectors = vectors + [swap(piece, 1) for piece in vectors]
    vectors[0] = own_vector
    tail_high, tail_low, cut_halo = run(
        prepare_cut_kernel,
        "prepare_cut",
        [VMEM] * 3,
        (vectors[far], entry_rows, weight_rows),
        [((sources, LANES + lanes), BF16)] * 2 + [((lanes, lanes), F32)],
        micros=1,
    )
    (conductances,) = run(
        conductance_kernel,
        "conductance",
        [SMEM] + [VMEM] * 3,
        (place, near_conductances, own_conductances, picked),
        [((times, sources), F32)],
        micros=1,
    )

    wide = ((times, half), F32)
    shared, start = packet_layout(steps, times)
    packet = (
        max(slots if shared else 0, 3 * CAP),
        -(-(start + max(times, slots)) // LANES) * LANES,
    )
    field_high, field_low, wave, current, cut_current, *sent = run(
        functools.partial(wave_kernel, pieces=parts, steps=steps),
        "wave",
        [SMEM] + [VMEM] * (parts + 8),
        (place, *vectors, forward, conductances, picked, tail_high, tail_low)
        + (linear_wide, capacity_wide, cut_halo),
        [
            ((length, sources), BF16),
            ((length, sources), BF16),
            ((times, sources), F32),
            ((2 * times, nodes), BF16),
            ((lanes, times), F32),
        ]
        + [(packet, F32)] * len(packet_steps(steps)),
        micros=2,
    )
    arrived = [trade(packet, masks) for packet, masks in zip(sent, packet_steps(steps))]
    others = []
    if not shared:
        gathered = lax.all_gather(cut_current, "nodes")
        distance = jnp.arange(node_groups, dtype=I32)
        others = [gathered[lax.axis_index("nodes") ^ distance]]
    local_load, slope, own_wave, dual, dual_slope = run(
        local_kernel,
        "local",
        [VMEM] * 12 + [SMEM],
        (field_high, field_low, forward, wave, current, conductances)
        + (coupling_high, coupling_low, tail_high, tail_low, linear_wide, capacity_wide, place),
        [wide] * 5,
        micros=3,
    )
    if steps == 3:
        (traded,) = run(
            relay_kernel, "relay", [VMEM] * 2, (dual, arrived[-1]), [(packet, F32)]
        )
        arrived[-1:] = [traded, swap(traded, 1)]
    (local_rest,) = run(
        local_rest_kernel,
        "local_rest",
        [VMEM] * 6,
        (local_load, current, coupling_high, coupling_low, tail_high, tail_low),
        [((times, half // 2), F32)],
    )
    block = ((length // 2, half), F32)
    packets = (place, *arrived, *others, cut_current)
    packet_specs = [SMEM] + [VMEM] * (len(packets) - 1)
    image, load, own_sums = run(
        functools.partial(first_kernel, steps=steps, apart=len(others)),
        "first",
        packet_specs + [VMEM] * 8,
        (*packets, local_load, local_rest, slope, own_wave)
        + (coupling_high, coupling_low, tail_high, tail_low),
        [wide, wide, ((8, half), F32)],
        micros=1,
    )
    halo, kept, sent = run(
        functools.partial(spread_kernel, steps=steps, apart=len(others)),
        "spread",
        packet_specs + [VMEM] * 2,
        (*packets, image, back),
        [((times, lanes), F32), block, block],
        micros=1,
    )
    near_image = swap(image, 1)
    bit = 2
    while 2 * bit < parts:
        own_sums = own_sums + swap(own_sums, bit)
        bit *= 2
    far_sums = swap(own_sums, bit) if bit < parts else jnp.zeros_like(own_sums)
    arrived = swap(sent, 1)

    second_load, second_kept, second_sent = run(
        second_kernel,
        "second",
        [SMEM] + [VMEM] * 10,
        (place, halo, near_image, image, back, conductances)
        + (coupling_high, coupling_low, tail_high, tail_low, linear_wide),
        [wide, block, block],
        scratch=[pltpu.VMEM((2 * times, nodes), BF16)],
        micros=3,
    )
    answer_parts = hand_out(load, place, kept, arrived)
    (second_sent,) = run(
        relay_kernel,
        "relay",
        [VMEM] * 2,
        (far_sums, second_sent),
        [(second_sent.shape, F32)],
    )
    second_arrived = swap(second_sent, 1)
    gathered = -(-node_groups * parts // LANES) * LANES
    (scalars,) = run(
        functools.partial(products_kernel, length=length),
        "products",
        [SMEM] + [VMEM] * 9,
        (place, own_vector, load, second_load, image, own_wave, dual, dual_slope)
        + (own_sums, far_sums),
        [((16, gathered), F32)],
        micros=1,
    )
    second_parts = hand_out(scalars, place, second_kept, second_arrived)
    scalars = add(cut_halo, exchange(scalars, "nodes", cut_halo))
    answer, slope, skew = run(
        functools.partial(settle_kernel, length=length),
        "settle",
        [SMEM] + [VMEM] * (len(answer_parts) + 2),
        (place, own_vector, capacity_all, *answer_parts),
        [((rows, nodes), F32), ((rows, nodes), F32), ((8, LANES), F32)],
        micros=1,
    )
    scalars = add(skew, exchange(scalars, "samples", cut_halo))
    field = jax.ShapeDtypeStruct((rows, nodes), F32)
    return tuple(
        pl.pallas_call(
            functools.partial(
                last_kernel, entries=entries, devices=float(node_groups * parts)
            ),
            out_shape=[field, field],
            in_specs=[VMEM] * (5 + len(second_parts)),
            out_specs=[VMEM] * 2,
            compiler_params=pltpu.CompilerParams(vmem_limit_bytes=12 * 2**20),
            name="last",
        )(scalars, own_vector, answer, slope, skew, *second_parts)
    )


def solution(mesh):
    return jax.shard_map(
        shards,
        mesh=mesh,
        in_specs=(
            P("samples", ("copies", "nodes")),
            P("samples", ("copies", "nodes")),
            P(),
            P("nodes"),
            P("nodes"),
            P(None, "nodes"),
            P("nodes"),
            P(None, "nodes"),
            P("nodes"),
            P("nodes"),
        ),
        out_specs=(P("samples", ("copies", "nodes")), P("samples", ("copies", "nodes"))),
        check_vma=False,
    )
```

```python
import functools
import math

import jax
import jax.numpy as jnp
import numpy as np
from jax import lax
from jax.experimental import pallas as pl
from jax.experimental.pallas import tpu as pltpu
from jax.sharding import PartitionSpec as P

CAP = 16
EPSILON = 1e-06
LANES = 128
BF16 = jnp.bfloat16
F32 = jnp.float32
I32 = jnp.int32


def spectral_tables(length):
    indices = np.arange(length)
    frequency = np.where(indices == 1, length // 2, indices // 2)
    angles = (indices[:, None] * frequency[None, :] % length) * (2.0 * math.pi / length)
    cosine_column = (indices % 2 == 0) | (indices == 1)
    synthesis = np.where(cosine_column[None, :], np.cos(angles), np.sin(angles))
    factor = np.where(indices < 2, 1.0 / length, 2.0 / length)
    analysis = synthesis.T * factor[:, None]
    turn = np.zeros((length, length))
    for pair in range(length // 2):
        turn[2 * pair, 2 * pair + 1] = pair / (length // 2)
        turn[2 * pair + 1, 2 * pair] = -pair / (length // 2)
    return synthesis, analysis, turn


def thirds(table):
    parts = []
    for _ in range(3):
        parts.append(table.astype(np.float32).astype(BF16))
        table = table - parts[-1].astype(np.float64)
    return np.stack(parts)


def piece_order(count):
    masks, bit = [0], count // 2
    while bit:
        masks = masks + [mask ^ bit for mask in masks]
        bit //= 2
    return masks


def transform_tables(length, parts):
    synthesis, analysis, turn = spectral_tables(length)
    slope, dual_slope = synthesis @ turn, analysis.T @ turn
    rows = length // parts
    forward, back = [], []
    for place in range(parts):
        times = np.arange(place // 2 * 2 * rows, (place // 2 + 1) * 2 * rows)
        block = lambda owner: np.arange(owner * rows, (owner + 1) * rows)
        coefs = np.concatenate([block(place ^ mask) for mask in piece_order(parts)])
        forward.append(
            np.concatenate(
                [
                    synthesis[np.ix_(times, coefs)],
                    slope[np.ix_(times, coefs)],
                    analysis[np.ix_(coefs, times)].T,
                    dual_slope[np.ix_(times, coefs)],
                ]
            )
        )
        sent = np.concatenate(
            [block(place ^ mask ^ side) for side in (0, 1) for mask in range(0, parts, 2)]
        )
        back.append(analysis[np.ix_(sent, times)])
    return (
        np.moveaxis(thirds(np.stack(forward)), 0, 1),
        np.moveaxis(thirds(np.stack(back)), 0, 1),
    )


def split(values):
    high = values.astype(BF16)
    return high, (values - high.astype(F32)).astype(BF16)


def split_three(values):
    high = values.astype(BF16)
    rest = values - high.astype(F32)
    middle = rest.astype(BF16)
    return high, middle, (rest - middle.astype(F32)).astype(BF16)


def dot(first, second):
    return jnp.dot(first, second, preferred_element_type=F32)


def dot_split(first, second):
    (first_high, first_low), (second_high, second_low) = first, second
    rows = first_high.shape[0]
    both = dot(jnp.concatenate([first_high, first_low], axis=0), second_high)
    return both[:rows] + both[rows:] + dot(first_high, second_low)


def dot_three(first, second):
    rows = first[0].shape[0]
    one = dot(jnp.concatenate(first, axis=0), second[0])
    two = dot(jnp.concatenate(first[:2], axis=0), second[1])
    small = one[2 * rows :] + two[rows:] + dot(first[0], second[2])
    return one[:rows] + ((one[rows : 2 * rows] + two[:rows]) + small)


def lane_sums(values):
    rows, lanes = values.shape
    step = 8 if rows % 8 == 0 else rows
    total = functools.reduce(
        jnp.add,
        [
            values[row : row + step, lane : lane + LANES]
            for row in range(0, rows, step)
            for lane in range(0, lanes, LANES)
        ],
    )
    return jnp.sum(total, axis=0, keepdims=True)


def half_of(side, half):
    return pl.ds(pl.multiple_of(side * half, LANES), half)


def scalar_sum(values):
    return jnp.sum(lane_sums(values), axis=1, keepdims=True)


def pick(values, picked):
    high, _ = split(values)
    middle, low = split(values - high.astype(F32))
    rows = values.shape[0]
    found = dot(jnp.concatenate([high, middle, low], axis=0), picked)
    return found[:rows] + (found[rows : 2 * rows] + found[2 * rows :])


def conductance(operating, table):
    points = table.shape[1]
    spread = jnp.concatenate([table, jnp.zeros((1, LANES - points), F32)], axis=1)
    spread = jnp.broadcast_to(spread, (operating.shape[0], LANES))
    pieces = []
    for block in range(operating.shape[1] // LANES):
        scaled = (operating[:, block * LANES : (block + 1) * LANES] + 4.0) * ((points - 1) / 8.0)
        knot = jnp.clip(jnp.floor(scaled), 0.0, points - 2.0)
        weight = scaled - knot
        place = knot.astype(I32)
        left = jnp.take_along_axis(spread, place, axis=1, mode="promise_in_bounds")
        right = jnp.take_along_axis(spread, place + 1, axis=1, mode="promise_in_bounds")
        pieces.append(left + weight * (right - left))
    return jnp.concatenate(pieces, axis=1)


def fetch_kernel(
    vector_in,
    neighbours_in,
    weights_in,
    degree_in,
    linear_in,
    capacity_in,
    send_list_in,
    boundary_in,
    table_in,
    operating_in,
    forward_in,
    back_in,
    vector,
    picked,
    linear,
    capacity,
    capacity_all,
    table,
    operating,
    forward,
    back,
    entry_rows,
    weight_rows,
    place,
    neighbours,
    weights,
    degree,
    linear_all,
    send_list,
    boundary,
    copied,
):
    place[0], place[1] = lax.axis_index("samples"), lax.axis_index("nodes")
    place[2], place[3] = lax.axis_size("nodes"), lax.axis_size("samples")
    slots, nodes = neighbours.shape
    lanes = picked.shape[1]
    half = linear.shape[1] - lanes
    node_groups = send_list.shape[0] // CAP
    side, part = place[0] % 2, place[1]
    copies = [
        pltpu.make_async_copy(source, target, copied.at[index])
        for index, (source, target) in enumerate(
            [
                (vector_in, vector),
                (send_list_in, send_list),
                (boundary_in, boundary),
                (neighbours_in, neighbours),
                (weights_in, weights),
                (degree_in, degree),
                (linear_in, linear_all),
                (capacity_in, capacity_all),
                (table_in, table),
                (operating_in, operating),
                (forward_in.at[place[0]], forward),
                (back_in.at[place[0]], back),
            ]
        )
    ]
    for copy in copies:
        copy.start()
    for copy in copies[1:3]:
        copy.wait()

    lane = lax.broadcasted_iota(I32, (8, lanes), 1)

    def name(slot, found):
        target = part ^ (slot // CAP + 1)
        node = boundary[send_list[target * CAP + slot % CAP]]
        return jnp.where(lane == slot, node, found)

    cut_nodes = lax.fori_loop(
        0, (node_groups - 1) * CAP, name, jnp.full((8, lanes), -1, I32), unroll=8
    )
    hit = lax.broadcasted_iota(I32, (nodes, lanes), 0) == cut_nodes[:1]
    picked[...] = jnp.where(hit, 1.0, 0.0).astype(BF16)

    for copy in copies[3:8]:
        copy.wait()
    mine = half_of(side, half)
    entry = neighbours[...]
    remote = entry - nodes
    distance = part ^ (remote >> 4)
    entry = jnp.where(remote < 0, entry, nodes + (distance - 1) * CAP + (remote & 15))
    live = lax.broadcasted_iota(I32, (slots, nodes), 0) < degree[...]
    neighbours[...] = entry
    weights[...] = jnp.where(live, weights[...], 0.0)
    columns = jnp.concatenate(
        [
            entry.astype(F32),
            weights[...],
            linear_all[...],
            capacity_all[...],
            jnp.zeros((6, nodes), F32),
        ],
        axis=0,
    )
    at_cut = pick(columns, picked[...])
    linear[:, :half] = linear_all[:, mine]
    linear[:, half:] = at_cut[2 * slots : 2 * slots + 1]
    capacity[:, :half] = capacity_all[:, mine]
    capacity[:, half:] = at_cut[2 * slots + 1 : 2 * slots + 2]
    entry_rows[:, :half] = neighbours[:, mine]
    entry_rows[:, half:] = at_cut[:slots].astype(I32)
    weight_rows[:, :half] = weights[:, mine]
    weight_rows[:, half:] = at_cut[slots : 2 * slots]
    entries = [entry_rows[slot : slot + 1, :] for slot in range(slots)]
    gains = [weight_rows[slot : slot + 1, :] for slot in range(slots)]
    for slot in range(slots):
        for later in range(slot + 1, slots):
            same = entries[slot] == entries[later]
            gains[slot] = gains[slot] + jnp.where(same, gains[later], 0.0)
            entries[later] = jnp.where(same, -1, entries[later])
    for slot in range(slots):
        entry_rows[slot : slot + 1, :] = entries[slot]
        weight_rows[slot : slot + 1, :] = gains[slot]
    copies[0].wait()
    for copy in copies[8:]:
        copy.wait()


def build(entry_rows, weight_rows, coupling_high, coupling_low):
    slots, width = entry_rows.shape
    sources = coupling_high.shape[0]
    blocks = sources // CAP
    unroll = max(count for count in range(1, 35) if blocks % count == 0)
    wide = (CAP, LANES)

    def column_block(block, carry):
        at_lanes = pl.ds(pl.multiple_of(block * LANES, LANES), LANES)
        names = [
            jnp.broadcast_to(entry_rows[slot : slot + 1, at_lanes], wide).astype(jnp.int16)
            for slot in range(slots)
        ]
        parts = [
            split(jnp.broadcast_to(weight_rows[slot : slot + 1, at_lanes], wide))
            for slot in range(slots)
        ]

        def source_rows(step, row):
            for inner in range(unroll):
                high = jnp.zeros(wide, BF16)
                low = jnp.zeros(wide, BF16)
                for slot in range(slots):
                    hit = names[slot] == row + jnp.int16(CAP * inner)
                    high = jnp.where(hit, parts[slot][0], high)
                    low = jnp.where(hit, parts[slot][1], low)
                at = pl.ds(pl.multiple_of((step * unroll + inner) * CAP, CAP), CAP)
                coupling_high[at, at_lanes] = high
                coupling_low[at, at_lanes] = low
            return row + jnp.int16(CAP * unroll)

        lax.fori_loop(
            0,
            blocks // unroll,
            source_rows,
            lax.broadcasted_iota(I32, wide, 0).astype(jnp.int16),
        )
        return carry

    lax.fori_loop(0, width // LANES, column_block, 0)


def prepare_kernel(entry_rows, weight_rows, coupling_high, coupling_low):
    half = coupling_high.shape[1]
    build(entry_rows.at[:, :half], weight_rows.at[:, :half], coupling_high, coupling_low)


def prepare_cut_kernel(after, entry_rows, weight_rows, cut_high, cut_low, cut_halo):
    lanes = cut_high.shape[1]
    half = entry_rows.shape[1] - lanes
    build(entry_rows.at[:, half:], weight_rows.at[:, half:], cut_high, cut_low)
    nodes = cut_high.shape[0] - lanes
    cut_halo[...] = jnp.transpose(cut_high[nodes:].astype(F32) + cut_low[nodes:].astype(F32))


def relay_kernel(*refs):
    count = (len(refs) - 1) // 2
    for source, target in zip(refs[1 : 1 + count], refs[1 + count :]):
        target[...] = source[...]


def conductance_kernel(place, near_operating, operating, table, picked, conductances):
    rows, nodes = operating.shape
    side = place[0] % 2
    for at, values in ((side, operating), (1 - side, near_operating)):
        conductances[pl.ds(pl.multiple_of(at * rows, 8), rows), :nodes] = conductance(
            values[...], table[...]
        )
    conductances[:, nodes:] = pick(conductances[:, :nodes], picked[...])


def coupled(high, stacked, coupling_high, coupling_low, sources, lanes):
    rows = high.shape[0]
    both = dot(stacked, coupling_high[sources, lanes])
    return both[:rows] + both[rows:] + dot(high, coupling_low[sources, lanes])


def packet_layout(steps, times):
    shared = steps * CAP <= LANES
    return shared, times if shared else 0


def packet_steps(steps):
    return [(2,), (1, 3)] if steps == 3 else [(step,) for step in range(1, steps + 1)]


def wave_kernel(*refs, pieces, steps):
    vectors = refs[1 : 1 + pieces]
    (
        forward,
        conductances,
        picked,
        coupling_high,
        coupling_low,
        linear,
        capacity,
        cut_halo,
        field_high,
        field_low,
        wave,
        current,
        cut_current,
    ) = refs[1 + pieces : 1 + pieces + 13]
    *sent, field_last = refs[1 + pieces + 13 :]
    side = refs[0][0] % 2
    rows, nodes = vectors[0].shape
    lanes = picked.shape[1]
    times = wave.shape[0]
    half = linear.shape[1] - lanes
    for index in range(pieces):
        at = slice(index * rows, (index + 1) * rows)
        parts = split_three(vectors[index][...])
        field_high[at, :nodes], field_low[at, :nodes], field_last[at, :nodes] = parts
    field_high[:, nodes:] = dot(field_high[:, :nodes], picked[...]).astype(BF16)
    field_low[:, nodes:] = dot(field_low[:, :nodes], picked[...]).astype(BF16)
    field_last[:, nodes:] = dot(field_last[:, :nodes], picked[...]).astype(BF16)
    wave[...] = dot_three(
        [forward[part, :times] for part in range(3)],
        (field_high[...], field_low[...], field_last[...]),
    )
    slope = dot_split(
        (forward[0, times : 2 * times], forward[1, times : 2 * times]),
        (field_high[:, nodes:], field_low[:, nodes:]),
    )
    high, low = split(conductances[:, :nodes] * wave[:, :nodes])
    current[:times] = high
    current[times:] = low
    at_cut = conductances[:, nodes:] * wave[:, nodes:]
    cut_current[...] = jnp.transpose(at_cut)
    image = (
        linear[:, half:] * wave[:, nodes:]
        + at_cut
        + capacity[:, half:] * slope
        + coupled(
            high, current[...], coupling_high, coupling_low, slice(0, nodes), slice(None)
        )
    )
    image = jnp.transpose(image)
    at_cut = jnp.transpose(conductances[:, nodes:])
    slots = steps * CAP
    shared, start = packet_layout(steps, times)
    for target, wanted in zip(sent, packet_steps(steps)):
        target[...] = jnp.zeros(target.shape, F32)
        if shared:
            target[:slots, :times] = cut_current[:slots]
        for row, values, size in ((0, cut_halo, slots), (1, image, times), (2, at_cut, times)):
            blocks = [values[(step - 1) * CAP : step * CAP, :size] for step in wanted]
            block = blocks[0] if len(blocks) == 1 else jnp.where(side == 0, *blocks)
            target[row * CAP : (row + 1) * CAP, start : start + size] = block


def local_kernel(
    field_high,
    field_low,
    forward,
    wave,
    current,
    conductances,
    coupling_high,
    coupling_low,
    linear,
    capacity,
    place,
    load,
    slope,
    own_wave,
    dual,
    dual_slope,
):
    times, half = load.shape
    sources = slice(0, current.shape[1])
    mine = half_of(place[0] % 2, half)
    others = dot_split(
        (forward[0, times:], forward[1, times:]), (field_high[:, mine], field_low[:, mine])
    )
    slope[...] = capacity[:, :half] * others[:times]
    dual[...] = others[times : 2 * times]
    dual_slope[...] = capacity[:, :half] * others[2 * times :]
    own_wave[...] = wave[:, mine]
    load[...] = own_wave[...] * (linear[:, :half] + conductances[:, mine])
    for lanes in blocks_of(0, half // 2):
        load[:, lanes] += coupled(
            current[:times], current[...], coupling_high, coupling_low, sources, lanes
        )


def local_rest_kernel(load, current, coupling_high, coupling_low, rest):
    times, half = load.shape
    sources = slice(0, current.shape[1])
    for lanes, at in zip(blocks_of(half // 2, half), blocks_of(0, half // 2)):
        rest[:, at] = load[:, lanes] + coupled(
            current[:times], current[...], coupling_high, coupling_low, sources, lanes
        )


def blocks_of(start, stop, step=256):
    return [slice(at, at + step) for at in range(start, stop, step)]


def signed_sums(values):
    rows = values.shape[0]
    folded = functools.reduce(jnp.add, [values[row : row + 8] for row in range(0, rows, 8)])
    even = lax.broadcasted_iota(I32, folded.shape, 0) % 2 == 0
    return (
        jnp.sum(folded, axis=0, keepdims=True),
        jnp.sum(jnp.where(even, folded, -folded), axis=0, keepdims=True),
    )


def analysed(back, load):
    spectrum = dot_three([back[part] for part in range(3)], split_three(load))
    middle = spectrum.shape[0] // 2
    return spectrum[:middle], spectrum[middle:]


def unpack(side, arrived, others, cut_current, lanes):
    steps = len(arrived)
    times = cut_current.shape[1]
    if steps == 3:
        both, own, near = (packet[...] for packet in arrived)
        arrived = [
            jnp.where(side == 0, own, near),
            both,
            jnp.where(side == 0, near, own),
        ]
    slots = steps * CAP
    blank = jnp.zeros((lanes - slots, times), F32)

    def stack(blocks):
        return jnp.transpose(jnp.concatenate([*blocks, blank], axis=0))

    def sender(step, block):
        at = slice((block - 1) * CAP, block * CAP)
        if step == 0:
            return cut_current[at]
        return others[0][step, at] if others else arrived[step - 1][at, :times]

    current = stack([sender(step, step) for step in range(1, steps + 1)])
    return arrived, stack, sender, current


def first_kernel(*refs, steps, apart):
    arrived, others = refs[1 : steps + 1], refs[steps + 1 : steps + 1 + apart]
    (
        cut_current,
        local_load,
        local_rest,
        slope,
        own_wave,
        coupling_high,
        coupling_low,
        image,
        load,
        sums,
    ) = refs[1 + steps + apart :]
    half = load.shape[1]
    lanes = -(-steps * CAP // LANES) * LANES
    nodes = coupling_high.shape[0] - lanes
    current = unpack(refs[0][0] % 2, arrived, others, cut_current, lanes)[-1]
    high, low = split(current)
    share = coupled(
        high,
        jnp.concatenate([high, low], axis=0),
        coupling_high,
        coupling_low,
        slice(nodes, None),
        slice(0, half),
    )
    load[:, : half // 2] = local_load[:, : half // 2] + share[:, : half // 2]
    load[:, half // 2 :] = local_rest[...] + share[:, half // 2 :]
    answer = load[...] + slope[...]
    image[...] = answer
    lines = [*signed_sums(answer), *signed_sums(own_wave[...])]
    sums[...] = jnp.concatenate(lines + [jnp.zeros((4, half), F32)], axis=0)


def spread_kernel(*refs, steps, apart):
    arrived, others = refs[1 : steps + 1], refs[steps + 1 : steps + 1 + apart]
    cut_current, image, back, halo, kept, sent = refs[1 + steps + apart :]
    times = image.shape[0]
    slots = steps * CAP
    start = packet_layout(steps, times)[1]
    arrived, stack, sender, _ = unpack(
        refs[0][0] % 2, arrived, others, cut_current, halo.shape[1]
    )
    kept[...], sent[...] = analysed(back, image[...])
    currents = []
    for step in range(1, steps + 1):
        theirs = jnp.concatenate(
            [sender(step ^ block, block) for block in range(1, steps + 1)], axis=0
        )
        gains = arrived[step - 1][:CAP, start : start + slots]
        image_part = arrived[step - 1][CAP : 2 * CAP, start : start + times]
        there = arrived[step - 1][2 * CAP : 3 * CAP, start : start + times]
        currents.append(there * (image_part + dot_split(split(gains), split(theirs))))
    halo[...] = stack(currents)


def second_kernel(
    place,
    halo,
    near_image,
    image,
    back,
    conductances,
    coupling_high,
    coupling_low,
    linear,
    load,
    kept,
    sent,
    current,
):
    times, half = image.shape
    nodes = current.shape[1]
    side = place[0] % 2
    mine, other = half_of(side, half), half_of(1 - side, half)
    for at, field in ((mine, image), (other, near_image)):
        current[:times, at], current[times:, at] = split(conductances[:, at] * field[...])
    load[...] = image[...] * (linear[:, :half] + conductances[:, mine])
    high, low = split(halo[...])
    halo_stacked = jnp.concatenate([high, low], axis=0)
    for lanes in blocks_of(0, half):
        load[:, lanes] += coupled(
            current[:times], current[...], coupling_high, coupling_low, slice(0, nodes), lanes
        ) + coupled(high, halo_stacked, coupling_high, coupling_low, slice(nodes, None), lanes)
    kept[...], sent[...] = analysed(back, load[...])


def sum_kernel(after, *refs):
    total = refs[0][...]
    for value in refs[1:-1]:
        total = total + value[...]
    refs[-1][...] = total


def turned(field, first_pair, half_order):
    count = field.shape[0]
    row = lax.broadcasted_iota(I32, field.shape, 0)
    scaling = (first_pair + row // 2).astype(F32) * (1.0 / half_order)
    above = pltpu.roll(field, count - 1, 0)
    below = pltpu.roll(field, 1, 0)
    return scaling * jnp.where(row % 2 == 0, above, -below)


def combine_kernel(after, place, kept, arrived, *targets):
    half = kept.shape[1]
    rows = targets[0].shape[0]
    side = place[0] % 2
    for index, target in enumerate(targets):
        at = slice(index * rows, (index + 1) * rows)
        target[:, half_of(side, half)] = kept[at]
        target[:, half_of(1 - side, half)] = arrived[at]


def joined(parts):
    return functools.reduce(jnp.add, [part[...] for part in parts])


def guess(cross, squares):
    ratio = cross / jnp.where(squares > 0.0, squares, 1.0)
    return jnp.clip(jnp.where(squares > 0.0, ratio, 0.0), -40.0, 40.0)


def products_kernel(
    place,
    vector,
    load,
    second_load,
    image,
    wave,
    dual,
    dual_slope,
    own_sums,
    far_sums,
    scalars,
    *,
    length,
):
    start, first = wave[...], load[...]
    field, sums = vector[...], own_sums[...] + far_sums[...]
    coeff = guess(scalar_sum(start * image[...]), scalar_sum(start * start))
    rest = image[...] - coeff * start
    change = second_load[...] - coeff * first
    start_sums = [sums[line + 2 : line + 3] for line in (0, 1)]
    rest_sums = [sums[line : line + 1] - coeff * start_sums[line] for line in (0, 1)]
    start_ends, rest_ends, first_ends, change_ends = (
        signed_sums(values) for values in (start, rest, first, change)
    )

    def mixed(values, value_sums, others, other_ends):
        ends = value_sums[0] * other_ends[0] + value_sums[1] * other_ends[1]
        return lane_sums(values * others) * (2.0 / length) - lane_sums(ends) * (
            1.0 / length / length
        )

    found = [
        lane_sums(field * field),
        lane_sums(dual[...] * rest),
        lane_sums(dual[...] * start),
        mixed(rest, rest_sums, rest, rest_ends),
        mixed(rest, rest_sums, start, start_ends) + mixed(start, start_sums, rest, rest_ends),
        mixed(start, start_sums, start, start_ends),
        lane_sums(dual[...] * change - dual_slope[...] * rest),
        lane_sums(dual[...] * first - dual_slope[...] * start),
        mixed(rest, rest_sums, change, change_ends),
        mixed(rest, rest_sums, first, first_ends) + mixed(start, start_sums, change, change_ends),
        mixed(start, start_sums, first, first_ends),
    ]
    device = place[1] * place[3] + place[0]
    lane = lax.broadcasted_iota(I32, scalars.shape, 1)
    column = jnp.concatenate(found + [jnp.zeros((5, LANES), F32)], axis=0)
    column = jnp.sum(column, axis=1, keepdims=True)
    line = lax.broadcasted_iota(I32, column.shape, 0)
    column = jnp.where(line == len(found), coeff, column)
    scalars[...] = jnp.where(lane == device, column, 0.0)


def settle_kernel(place, vector, capacity, *refs, length):
    *parts, answer, slope, skew = refs
    rows = vector.shape[0]
    first_pair = place[0] * (rows // 2)
    answer[...] = joined(parts)
    field, start = answer[...], vector[...]
    slope[...] = capacity[...] * turned(field, first_pair, length // 2)
    start_slope = capacity[...] * turned(start, first_pair, length // 2)
    products = [
        scalar_sum(field * slope[...]),
        scalar_sum(field * start_slope + start * slope[...]),
        scalar_sum(start * start_slope),
        jnp.zeros((5, 1), F32),
    ]
    skew[...] = jnp.broadcast_to(jnp.concatenate(products, axis=0), skew.shape)


def last_kernel(
    gathered,
    vector,
    answer,
    slope,
    skew,
    *refs,
    entries,
    devices,
):
    *parts, basis_two, next_residue = refs
    own = [gathered[line : line + 1, :] for line in range(12)]
    local = own.pop()

    def everywhere(values):
        return jnp.sum(values, axis=1, keepdims=True) / entries

    scale_square = everywhere(own[0]) + EPSILON
    coeff = everywhere(own[1] + local * own[2]) / scale_square
    near = local - coeff
    rest_square = everywhere(own[3] + near * (own[4] + near * own[5]))
    along_one = everywhere(own[6] + near * own[7])
    along_two = everywhere(own[8] + near * (own[9] + near * own[10]))
    turn = skew[0:1, :1] - coeff * (skew[1:2, :1] - coeff * skew[2:3, :1])
    along_two = along_two + turn * (devices / entries)
    scale = jnp.sqrt(scale_square)
    second_norm = jnp.sqrt(jnp.maximum(rest_square, 0.0) / scale_square + EPSILON)
    inverse = 1.0 / (second_norm * scale)
    along_one = along_one * inverse / scale_square
    along_two = along_two * inverse * inverse
    second = (answer[...] - coeff * vector[...]) * inverse
    basis_two[...] = second
    next_residue[...] = (
        (joined(parts) + slope[...] - coeff * answer[...]) * inverse
        - along_one * vector[...]
        - along_two * second
    )


VMEM = pl.BlockSpec(memory_space=pltpu.VMEM)
SMEM = pl.BlockSpec(memory_space=pltpu.SMEM)


HBM = pl.BlockSpec(memory_space=pltpu.HBM)


def run(kernel, name, specs, operands, outs, scratch=(), micros=1, room=12, spaces=None):
    spaces = spaces or [pltpu.VMEM] * len(outs)
    return pl.pallas_call(
        kernel,
        out_shape=[space(shape, dtype) for space, (shape, dtype) in zip(spaces, outs)],
        in_specs=specs,
        out_specs=[pl.BlockSpec(memory_space=space) for space in spaces],
        scratch_shapes=list(scratch),
        compiler_params=pltpu.CompilerParams(vmem_limit_bytes=room * 2**20),
        cost_estimate=pl.CostEstimate(
            flops=0, bytes_accessed=int(micros * 3e6), transcendentals=0
        ),
        name=name,
    )(*operands)


def swap(value, mask):
    count = lax.axis_size("samples")
    return lax.ppermute(value, "samples", [(at, at ^ mask) for at in range(count)])


def trade(value, masks):
    count, parts = lax.axis_size("nodes"), lax.axis_size("samples")
    pairs = [
        (at * parts + which, (at ^ masks[which % len(masks)]) * parts + which)
        for at in range(count)
        for which in range(parts)
    ]
    return lax.ppermute(value, ("nodes", "samples"), pairs)


def add(after, terms):
    (value,) = run(
        sum_kernel,
        "sum",
        [VMEM] * (len(terms) + 1),
        (after, *terms),
        [(terms[0].shape, F32)],
    )
    return value


def exchange(value, axis, after):
    count, stride, terms = lax.axis_size(axis), 1, [value]
    while stride < count:
        if stride > 1:
            value = add(after, terms)
        radix = 4 if count // stride % 4 == 0 else 2
        terms = [value] + [
            lax.ppermute(value, axis, [(at, at ^ (step * stride)) for at in range(count)])
            for step in range(1, radix)
        ]
        stride *= radix
    return terms


def hand_out(after, place, kept, arrived):
    count = lax.axis_size("samples") // 2
    field = ((kept.shape[0] // count, 2 * kept.shape[1]), F32)
    parts = run(
        combine_kernel,
        "combine",
        [VMEM, SMEM] + [VMEM] * 2,
        (after, place, kept, arrived),
        [field] * count,
    )
    return [parts[0]] + [swap(part, 2 * mask) for mask, part in enumerate(parts) if mask]


def shards(
    vector, operating, table, linear, capacity, weights, degree, neighbours, boundary, send_list
):
    rows, nodes = vector.shape
    parts, node_groups = lax.axis_size("samples"), lax.axis_size("nodes")
    length, half, times = rows * parts, nodes // 2, 2 * rows
    entries = float(length * nodes * node_groups)
    steps = node_groups - 1
    slots = steps * CAP
    lanes = -(-slots // LANES) * LANES
    sources, width = nodes + lanes, half + lanes
    forward, back = (jnp.asarray(table) for table in transform_tables(length, parts))
    linear, capacity, degree, table = (
        value.reshape(1, -1) for value in (linear, capacity, degree, table)
    )

    slot_count = weights.shape[0]
    (
        own_vector,
        picked,
        linear_wide,
        capacity_wide,
        capacity,
        table,
        own_operating,
        forward,
        back,
        entry_rows,
        weight_rows,
        place,
    ) = run(
        fetch_kernel,
        "fetch",
        [HBM] * 12,
        tuple(
            pltpu.with_memory_space_constraint(value, pltpu.HBM)
            for value in (vector, neighbours, weights, degree, linear, capacity, send_list)
            + (boundary, table, operating, forward, back)
        ),
        [
            ((rows, nodes), F32),
            ((nodes, lanes), BF16),
            ((1, width), F32),
            ((1, width), F32),
            ((1, nodes), F32),
            (table.shape, F32),
            ((rows, nodes), F32),
            (forward.shape[1:], BF16),
            (back.shape[1:], BF16),
            ((slot_count, width), I32),
            ((slot_count, width), F32),
            ((4,), I32),
        ],
        scratch=[
            pltpu.VMEM((slot_count, nodes), I32),
            pltpu.VMEM((slot_count, nodes), F32),
            pltpu.VMEM((1, nodes), I32),
            pltpu.VMEM((1, nodes), F32),
            pltpu.SMEM(send_list.shape, I32),
            pltpu.SMEM(boundary.shape, I32),
            pltpu.SemaphoreType.DMA((12,)),
        ],
        micros=2,
        spaces=[pltpu.VMEM] * 11 + [pltpu.SMEM],
    )
    coupling_high, coupling_low = run(
        prepare_kernel,
        "prepare",
        [VMEM] * 2,
        (entry_rows, weight_rows),
        [((sources, half), BF16)] * 2,
        micros=6,
    )
    near_operating = swap(operating, 1)
    vectors, bit = [vector], parts // 2
    while bit > 1:
        vectors = vectors + [swap(piece, bit) for piece in vectors]
        bit //= 2
    far = len(vectors) - 1
    if far:
        vectors[1:] = run(
            relay_kernel,
            "relay",
            [VMEM] * (far + 1),
            (coupling_low, *vectors[1:]),
            [((rows, nodes), F32)] * far,
        )
    vectors = vectors + [swap(piece, 1) for piece in vectors]
    vectors[0] = own_vector
    cut_high, cut_low, cut_halo = run(
        prepare_cut_kernel,
        "prepare_cut",
        [VMEM] * 3,
        (vectors[far], entry_rows, weight_rows),
        [((sources, lanes), BF16), ((sources, lanes), BF16), ((lanes, lanes), F32)],
        micros=1,
    )
    (conductances,) = run(
        conductance_kernel,
        "conductance",
        [SMEM] + [VMEM] * 4,
        (place, near_operating, own_operating, table, picked),
        [((times, sources), F32)],
        micros=1,
    )

    wide = ((times, half), F32)
    shared, start = packet_layout(steps, times)
    packet = (
        max(slots if shared else 0, 3 * CAP),
        -(-(start + max(times, slots)) // LANES) * LANES,
    )
    field_high, field_low, wave, current, cut_current, *sent = run(
        functools.partial(wave_kernel, pieces=parts, steps=steps),
        "wave",
        [SMEM] + [VMEM] * (parts + 8),
        (place, *vectors, forward, conductances, picked, cut_high, cut_low)
        + (linear_wide, capacity_wide, cut_halo),
        [
            ((length, sources), BF16),
            ((length, sources), BF16),
            ((times, sources), F32),
            ((2 * times, nodes), BF16),
            ((lanes, times), F32),
        ]
        + [(packet, F32)] * len(packet_steps(steps)),
        scratch=[pltpu.VMEM((length, sources), BF16)],
        micros=2,
    )
    arrived = [trade(packet, masks) for packet, masks in zip(sent, packet_steps(steps))]
    others = []
    if not shared:
        gathered = lax.all_gather(cut_current, "nodes")
        distance = jnp.arange(node_groups, dtype=I32)
        others = [gathered[lax.axis_index("nodes") ^ distance]]
    local_load, slope, own_wave, dual, dual_slope = run(
        local_kernel,
        "local",
        [VMEM] * 10 + [SMEM],
        (field_high, field_low, forward, wave, current, conductances)
        + (coupling_high, coupling_low, linear_wide, capacity_wide, place),
        [wide] * 5,
        micros=3,
    )
    if steps == 3:
        (traded,) = run(
            relay_kernel, "relay", [VMEM] * 2, (dual, arrived[-1]), [(packet, F32)]
        )
        arrived[-1:] = [traded, swap(traded, 1)]
    (local_rest,) = run(
        local_rest_kernel,
        "local_rest",
        [VMEM] * 4,
        (local_load, current, coupling_high, coupling_low),
        [((times, half // 2), F32)],
    )
    block = ((length // 2, half), F32)
    packets = (place, *arrived, *others, cut_current)
    packet_specs = [SMEM] + [VMEM] * (len(packets) - 1)
    image, load, own_sums = run(
        functools.partial(first_kernel, steps=steps, apart=len(others)),
        "first",
        packet_specs + [VMEM] * 6,
        (*packets, local_load, local_rest, slope, own_wave, coupling_high, coupling_low),
        [wide, wide, ((8, half), F32)],
        micros=1,
    )
    halo, kept, sent = run(
        functools.partial(spread_kernel, steps=steps, apart=len(others)),
        "spread",
        packet_specs + [VMEM] * 2,
        (*packets, image, back),
        [((times, lanes), F32), block, block],
        micros=1,
    )
    near_image = swap(image, 1)
    bit = 2
    while 2 * bit < parts:
        own_sums = own_sums + swap(own_sums, bit)
        bit *= 2
    far_sums = swap(own_sums, bit) if bit < parts else jnp.zeros_like(own_sums)
    arrived = swap(sent, 1)

    second_load, second_kept, second_sent = run(
        second_kernel,
        "second",
        [SMEM] + [VMEM] * 8,
        (place, halo, near_image, image, back, conductances)
        + (coupling_high, coupling_low, linear_wide),
        [wide, block, block],
        scratch=[pltpu.VMEM((2 * times, nodes), BF16)],
        micros=3,
    )
    answer_parts = hand_out(load, place, kept, arrived)
    (second_sent,) = run(
        relay_kernel,
        "relay",
        [VMEM] * 2,
        (far_sums, second_sent),
        [(second_sent.shape, F32)],
    )
    second_arrived = swap(second_sent, 1)
    gathered = -(-node_groups * parts // LANES) * LANES
    (scalars,) = run(
        functools.partial(products_kernel, length=length),
        "products",
        [SMEM] + [VMEM] * 9,
        (place, own_vector, load, second_load, image, own_wave, dual, dual_slope)
        + (own_sums, far_sums),
        [((16, gathered), F32)],
        micros=1,
    )
    second_parts = hand_out(scalars, place, second_kept, second_arrived)
    scalars = add(cut_halo, exchange(scalars, "nodes", cut_halo))
    answer, slope, skew = run(
        functools.partial(settle_kernel, length=length),
        "settle",
        [SMEM] + [VMEM] * (len(answer_parts) + 2),
        (place, own_vector, capacity, *answer_parts),
        [((rows, nodes), F32), ((rows, nodes), F32), ((8, LANES), F32)],
        micros=1,
    )
    scalars = add(skew, exchange(scalars, "samples", cut_halo))
    field = jax.ShapeDtypeStruct((rows, nodes), F32)
    return tuple(
        pl.pallas_call(
            functools.partial(
                last_kernel, entries=entries, devices=float(node_groups * parts)
            ),
            out_shape=[field, field],
            in_specs=[VMEM] * (5 + len(second_parts)),
            out_specs=[VMEM] * 2,
            compiler_params=pltpu.CompilerParams(vmem_limit_bytes=12 * 2**20),
            name="last",
        )(scalars, own_vector, answer, slope, skew, *second_parts)
    )


def solution(mesh):
    return jax.shard_map(
        shards,
        mesh=mesh,
        in_specs=(
            P("samples", ("copies", "nodes")),
            P("samples", ("copies", "nodes")),
            P(),
            P("nodes"),
            P("nodes"),
            P(None, "nodes"),
            P("nodes"),
            P(None, "nodes"),
            P("nodes"),
            P("nodes"),
        ),
        out_specs=(P("samples", ("copies", "nodes")), P("samples", ("copies", "nodes"))),
        check_vma=False,
    )
```

```python
import functools
import math

import jax
import jax.numpy as jnp
import numpy as np
from jax import lax
from jax.experimental import pallas as pl
from jax.experimental.pallas import tpu as pltpu
from jax.sharding import PartitionSpec as P

CAP = 16
EPSILON = 1e-06
LANES = 128
BF16 = jnp.bfloat16
F32 = jnp.float32
I32 = jnp.int32


def spectral_tables(length):
    indices = np.arange(length)
    frequency = np.where(indices == 1, length // 2, indices // 2)
    angles = (indices[:, None] * frequency[None, :] % length) * (2.0 * math.pi / length)
    cosine_column = (indices % 2 == 0) | (indices == 1)
    synthesis = np.where(cosine_column[None, :], np.cos(angles), np.sin(angles))
    factor = np.where(indices < 2, 1.0 / length, 2.0 / length)
    analysis = synthesis.T * factor[:, None]
    turn = np.zeros((length, length))
    for pair in range(length // 2):
        turn[2 * pair, 2 * pair + 1] = pair / (length // 2)
        turn[2 * pair + 1, 2 * pair] = -pair / (length // 2)
    return synthesis, analysis, turn


def thirds(table):
    parts = []
    for _ in range(3):
        parts.append(table.astype(np.float32).astype(BF16))
        table = table - parts[-1].astype(np.float64)
    return np.stack(parts)


def piece_order(count):
    masks, bit = [0], count // 2
    while bit:
        masks = masks + [mask ^ bit for mask in masks]
        bit //= 2
    return masks


def transform_tables(length, parts):
    synthesis, analysis, turn = spectral_tables(length)
    slope, dual_slope = synthesis @ turn, analysis.T @ turn
    rows = length // parts
    forward, back = [], []
    for place in range(parts):
        times = np.arange(place // 2 * 2 * rows, (place // 2 + 1) * 2 * rows)
        block = lambda owner: np.arange(owner * rows, (owner + 1) * rows)
        coefs = np.concatenate([block(place ^ mask) for mask in piece_order(parts)])
        forward.append(
            np.concatenate(
                [
                    synthesis[np.ix_(times, coefs)],
                    slope[np.ix_(times, coefs)],
                    analysis[np.ix_(coefs, times)].T,
                    dual_slope[np.ix_(times, coefs)],
                ]
            )
        )
        sent = np.concatenate(
            [block(place ^ mask ^ side) for side in (0, 1) for mask in range(0, parts, 2)]
        )
        back.append(analysis[np.ix_(sent, times)])
    return (
        np.moveaxis(thirds(np.stack(forward)), 0, 1),
        np.moveaxis(thirds(np.stack(back)), 0, 1),
    )


def split(values):
    high = values.astype(BF16)
    return high, (values - high.astype(F32)).astype(BF16)


def split_three(values):
    high = values.astype(BF16)
    rest = values - high.astype(F32)
    middle = rest.astype(BF16)
    return high, middle, (rest - middle.astype(F32)).astype(BF16)


def dot(first, second):
    return jnp.dot(first, second, preferred_element_type=F32)


def dot_split(first, second):
    (first_high, first_low), (second_high, second_low) = first, second
    rows = first_high.shape[0]
    both = dot(jnp.concatenate([first_high, first_low], axis=0), second_high)
    return both[:rows] + both[rows:] + dot(first_high, second_low)


def dot_three(first, second):
    rows = first[0].shape[0]
    one = dot(jnp.concatenate(first, axis=0), second[0])
    two = dot(jnp.concatenate(first[:2], axis=0), second[1])
    small = one[2 * rows :] + two[rows:] + dot(first[0], second[2])
    return one[:rows] + ((one[rows : 2 * rows] + two[:rows]) + small)


def lane_sums(values):
    rows, lanes = values.shape
    step = 8 if rows % 8 == 0 else rows
    total = functools.reduce(
        jnp.add,
        [
            values[row : row + step, lane : lane + LANES]
            for row in range(0, rows, step)
            for lane in range(0, lanes, LANES)
        ],
    )
    return jnp.sum(total, axis=0, keepdims=True)


def half_of(side, half):
    return pl.ds(pl.multiple_of(side * half, LANES), half)


def scalar_sum(values):
    return jnp.sum(lane_sums(values), axis=1, keepdims=True)


def pick(values, picked):
    high, _ = split(values)
    middle, low = split(values - high.astype(F32))
    rows = values.shape[0]
    found = dot(jnp.concatenate([high, middle, low], axis=0), picked)
    return found[:rows] + (found[rows : 2 * rows] + found[2 * rows :])


def conductance(operating, table):
    points = table.shape[1]
    spread = jnp.concatenate([table, jnp.zeros((1, LANES - points), F32)], axis=1)
    spread = jnp.broadcast_to(spread, (operating.shape[0], LANES))
    pieces = []
    for block in range(operating.shape[1] // LANES):
        scaled = (operating[:, block * LANES : (block + 1) * LANES] + 4.0) * ((points - 1) / 8.0)
        knot = jnp.clip(jnp.floor(scaled), 0.0, points - 2.0)
        weight = scaled - knot
        place = knot.astype(I32)
        left = jnp.take_along_axis(spread, place, axis=1, mode="promise_in_bounds")
        right = jnp.take_along_axis(spread, place + 1, axis=1, mode="promise_in_bounds")
        pieces.append(left + weight * (right - left))
    return jnp.concatenate(pieces, axis=1)


def fetch_kernel(
    vector_in,
    neighbours_in,
    weights_in,
    degree_in,
    linear_in,
    capacity_in,
    send_list_in,
    boundary_in,
    table_in,
    operating_in,
    forward_in,
    back_in,
    vector,
    picked,
    linear,
    capacity,
    capacity_all,
    table,
    operating,
    forward,
    back,
    entry_rows,
    weight_rows,
    place,
    neighbours,
    weights,
    degree,
    linear_all,
    send_list,
    boundary,
    copied,
):
    place[0], place[1] = lax.axis_index("samples"), lax.axis_index("nodes")
    place[2], place[3] = lax.axis_size("nodes"), lax.axis_size("samples")
    slots, nodes = neighbours.shape
    lanes = picked.shape[1]
    half = linear.shape[1] - lanes
    node_groups = send_list.shape[0] // CAP
    side, part = place[0] % 2, place[1]
    copies = [
        pltpu.make_async_copy(source, target, copied.at[index])
        for index, (source, target) in enumerate(
            [
                (vector_in, vector),
                (send_list_in, send_list),
                (boundary_in, boundary),
                (neighbours_in, neighbours),
                (weights_in, weights),
                (degree_in, degree),
                (linear_in, linear_all),
                (capacity_in, capacity_all),
                (table_in, table),
                (operating_in, operating),
                (forward_in.at[place[0]], forward),
                (back_in.at[place[0]], back),
            ]
        )
    ]
    for copy in copies:
        copy.start()
    for copy in copies[1:3]:
        copy.wait()

    lane = lax.broadcasted_iota(I32, (8, lanes), 1)

    def name(slot, found):
        target = part ^ (slot // CAP + 1)
        node = boundary[send_list[target * CAP + slot % CAP]]
        return jnp.where(lane == slot, node, found)

    cut_nodes = lax.fori_loop(
        0, (node_groups - 1) * CAP, name, jnp.full((8, lanes), -1, I32), unroll=8
    )
    hit = lax.broadcasted_iota(I32, (nodes, lanes), 0) == cut_nodes[:1]
    picked[...] = jnp.where(hit, 1.0, 0.0).astype(BF16)

    for copy in copies[3:8]:
        copy.wait()
    mine = half_of(side, half)
    entry = neighbours[...]
    remote = entry - nodes
    distance = part ^ (remote >> 4)
    entry = jnp.where(remote < 0, entry, nodes + (distance - 1) * CAP + (remote & 15))
    live = lax.broadcasted_iota(I32, (slots, nodes), 0) < degree[...]
    neighbours[...] = entry
    weights[...] = jnp.where(live, weights[...], 0.0)
    columns = jnp.concatenate(
        [
            entry.astype(F32),
            weights[...],
            linear_all[...],
            capacity_all[...],
            jnp.zeros((6, nodes), F32),
        ],
        axis=0,
    )
    at_cut = pick(columns, picked[...])
    linear[:, :half] = linear_all[:, mine]
    linear[:, half:] = at_cut[2 * slots : 2 * slots + 1]
    capacity[:, :half] = capacity_all[:, mine]
    capacity[:, half:] = at_cut[2 * slots + 1 : 2 * slots + 2]
    entry_rows[:, :half] = neighbours[:, mine]
    entry_rows[:, half:] = at_cut[:slots].astype(I32)
    weight_rows[:, :half] = weights[:, mine]
    weight_rows[:, half:] = at_cut[slots : 2 * slots]
    entries = [entry_rows[slot : slot + 1, :] for slot in range(slots)]
    gains = [weight_rows[slot : slot + 1, :] for slot in range(slots)]
    for slot in range(slots):
        for later in range(slot + 1, slots):
            same = entries[slot] == entries[later]
            gains[slot] = gains[slot] + jnp.where(same, gains[later], 0.0)
            entries[later] = jnp.where(same, -1, entries[later])
    for slot in range(slots):
        entry_rows[slot : slot + 1, :] = entries[slot]
        weight_rows[slot : slot + 1, :] = gains[slot]
    copies[0].wait()
    for copy in copies[8:]:
        copy.wait()


def build(entry_rows, weight_rows, coupling_high, coupling_low):
    slots, width = entry_rows.shape
    sources = coupling_high.shape[0]
    blocks = sources // CAP
    unroll = max(count for count in range(1, 35) if blocks % count == 0)
    wide = (CAP, LANES)

    def column_block(block, carry):
        at_lanes = pl.ds(pl.multiple_of(block * LANES, LANES), LANES)
        names = [
            jnp.broadcast_to(entry_rows[slot : slot + 1, at_lanes], wide).astype(jnp.int16)
            for slot in range(slots)
        ]
        parts = [
            split(jnp.broadcast_to(weight_rows[slot : slot + 1, at_lanes], wide))
            for slot in range(slots)
        ]

        def source_rows(step, row):
            for inner in range(unroll):
                high = jnp.zeros(wide, BF16)
                low = jnp.zeros(wide, BF16)
                for slot in range(slots):
                    hit = names[slot] == row + jnp.int16(CAP * inner)
                    high = jnp.where(hit, parts[slot][0], high)
                    low = jnp.where(hit, parts[slot][1], low)
                at = pl.ds(pl.multiple_of((step * unroll + inner) * CAP, CAP), CAP)
                coupling_high[at, at_lanes] = high
                coupling_low[at, at_lanes] = low
            return row + jnp.int16(CAP * unroll)

        lax.fori_loop(
            0,
            blocks // unroll,
            source_rows,
            lax.broadcasted_iota(I32, wide, 0).astype(jnp.int16),
        )
        return carry

    lax.fori_loop(0, width // LANES, column_block, 0)


def prepare_kernel(entry_rows, weight_rows, coupling_high, coupling_low):
    half = coupling_high.shape[1]
    build(entry_rows.at[:, :half], weight_rows.at[:, :half], coupling_high, coupling_low)


def prepare_cut_kernel(after, entry_rows, weight_rows, cut_high, cut_low, cut_halo):
    lanes = cut_high.shape[1]
    half = entry_rows.shape[1] - lanes
    build(entry_rows.at[:, half:], weight_rows.at[:, half:], cut_high, cut_low)
    nodes = cut_high.shape[0] - lanes
    cut_halo[...] = jnp.transpose(cut_high[nodes:].astype(F32) + cut_low[nodes:].astype(F32))


def relay_kernel(*refs):
    count = (len(refs) - 1) // 2
    for source, target in zip(refs[1 : 1 + count], refs[1 + count :]):
        target[...] = source[...]


def conductance_kernel(place, near_operating, operating, table, picked, conductances):
    rows, nodes = operating.shape
    side = place[0] % 2
    for at, values in ((side, operating), (1 - side, near_operating)):
        conductances[pl.ds(pl.multiple_of(at * rows, 8), rows), :nodes] = conductance(
            values[...], table[...]
        )
    conductances[:, nodes:] = pick(conductances[:, :nodes], picked[...])


def coupled(high, stacked, coupling_high, coupling_low, sources, lanes):
    rows = high.shape[0]
    both = dot(stacked, coupling_high[sources, lanes])
    return both[:rows] + both[rows:] + dot(high, coupling_low[sources, lanes])


def packet_layout(steps, times):
    shared = steps * CAP <= LANES
    return shared, times if shared else 0


def packet_steps(steps):
    return [(2,), (1, 3)] if steps == 3 else [(step,) for step in range(1, steps + 1)]


def wave_kernel(*refs, pieces, steps):
    vectors = refs[1 : 1 + pieces]
    (
        forward,
        conductances,
        picked,
        coupling_high,
        coupling_low,
        linear,
        capacity,
        cut_halo,
        field_high,
        field_low,
        wave,
        current,
        cut_current,
    ) = refs[1 + pieces : 1 + pieces + 13]
    *sent, field_last = refs[1 + pieces + 13 :]
    side = refs[0][0] % 2
    rows, nodes = vectors[0].shape
    lanes = picked.shape[1]
    times = wave.shape[0]
    half = linear.shape[1] - lanes
    for index in range(pieces):
        at = slice(index * rows, (index + 1) * rows)
        parts = split_three(vectors[index][...])
        field_high[at, :nodes], field_low[at, :nodes], field_last[at] = parts
    field_high[:, nodes:] = dot(field_high[:, :nodes], picked[...]).astype(BF16)
    field_low[:, nodes:] = dot(field_low[:, :nodes], picked[...]).astype(BF16)
    wave[:, :nodes] = dot_three(
        [forward[part, :times] for part in range(3)],
        (field_high[:, :nodes], field_low[:, :nodes], field_last[...]),
    )
    both = dot_split(
        (forward[0, : 2 * times], forward[1, : 2 * times]),
        (field_high[:, nodes:], field_low[:, nodes:]),
    )
    wave[:, nodes:], slope = both[:times], both[times:]
    high, low = split(conductances[:, :nodes] * wave[:, :nodes])
    current[:times] = high
    current[times:] = low
    at_cut = conductances[:, nodes:] * wave[:, nodes:]
    cut_current[...] = jnp.transpose(at_cut)
    image = (
        linear[:, half:] * wave[:, nodes:]
        + at_cut
        + capacity[:, half:] * slope
        + coupled(
            high, current[...], coupling_high, coupling_low, slice(0, nodes), slice(None)
        )
    )
    image = jnp.transpose(image)
    at_cut = jnp.transpose(conductances[:, nodes:])
    slots = steps * CAP
    shared, start = packet_layout(steps, times)
    for target, wanted in zip(sent, packet_steps(steps)):
        target[...] = jnp.zeros(target.shape, F32)
        if shared:
            target[:slots, :times] = cut_current[:slots]
        for row, values, size in ((0, cut_halo, slots), (1, image, times), (2, at_cut, times)):
            blocks = [values[(step - 1) * CAP : step * CAP, :size] for step in wanted]
            block = blocks[0] if len(blocks) == 1 else jnp.where(side == 0, *blocks)
            target[row * CAP : (row + 1) * CAP, start : start + size] = block


def local_kernel(
    field_high,
    field_low,
    forward,
    wave,
    current,
    conductances,
    coupling_high,
    coupling_low,
    linear,
    capacity,
    place,
    load,
    slope,
    own_wave,
    dual,
    dual_slope,
):
    times, half = load.shape
    sources = slice(0, current.shape[1])
    mine = half_of(place[0] % 2, half)
    others = dot_split(
        (forward[0, times:], forward[1, times:]), (field_high[:, mine], field_low[:, mine])
    )
    slope[...] = capacity[:, :half] * others[:times]
    dual[...] = others[times : 2 * times]
    dual_slope[...] = capacity[:, :half] * others[2 * times :]
    own_wave[...] = wave[:, mine]
    load[...] = own_wave[...] * (linear[:, :half] + conductances[:, mine])
    for lanes in blocks_of(0, half // 2):
        load[:, lanes] += coupled(
            current[:times], current[...], coupling_high, coupling_low, sources, lanes
        )


def local_rest_kernel(load, current, coupling_high, coupling_low, rest):
    times, half = load.shape
    sources = slice(0, current.shape[1])
    for lanes, at in zip(blocks_of(half // 2, half), blocks_of(0, half // 2)):
        rest[:, at] = load[:, lanes] + coupled(
            current[:times], current[...], coupling_high, coupling_low, sources, lanes
        )


def blocks_of(start, stop, step=256):
    return [slice(at, at + step) for at in range(start, stop, step)]


def signed_sums(values):
    rows = values.shape[0]
    folded = functools.reduce(jnp.add, [values[row : row + 8] for row in range(0, rows, 8)])
    even = lax.broadcasted_iota(I32, folded.shape, 0) % 2 == 0
    return (
        jnp.sum(folded, axis=0, keepdims=True),
        jnp.sum(jnp.where(even, folded, -folded), axis=0, keepdims=True),
    )


def analysed(back, load):
    spectrum = dot_three([back[part] for part in range(3)], split_three(load))
    middle = spectrum.shape[0] // 2
    return spectrum[:middle], spectrum[middle:]


def unpack(side, arrived, others, cut_current, lanes):
    steps = len(arrived)
    times = cut_current.shape[1]
    if steps == 3:
        both, own, near = (packet[...] for packet in arrived)
        arrived = [
            jnp.where(side == 0, own, near),
            both,
            jnp.where(side == 0, near, own),
        ]
    slots = steps * CAP
    blank = jnp.zeros((lanes - slots, times), F32)

    def stack(blocks):
        return jnp.transpose(jnp.concatenate([*blocks, blank], axis=0))

    def sender(step, block):
        at = slice((block - 1) * CAP, block * CAP)
        if step == 0:
            return cut_current[at]
        return others[0][step, at] if others else arrived[step - 1][at, :times]

    current = stack([sender(step, step) for step in range(1, steps + 1)])
    return arrived, stack, sender, current


def first_kernel(*refs, steps, apart):
    arrived, others = refs[1 : steps + 1], refs[steps + 1 : steps + 1 + apart]
    (
        cut_current,
        local_load,
        local_rest,
        slope,
        own_wave,
        coupling_high,
        coupling_low,
        image,
        load,
        sums,
    ) = refs[1 + steps + apart :]
    half = load.shape[1]
    lanes = -(-steps * CAP // LANES) * LANES
    nodes = coupling_high.shape[0] - lanes
    current = unpack(refs[0][0] % 2, arrived, others, cut_current, lanes)[-1]
    high, low = split(current)
    share = coupled(
        high,
        jnp.concatenate([high, low], axis=0),
        coupling_high,
        coupling_low,
        slice(nodes, None),
        slice(0, half),
    )
    load[:, : half // 2] = local_load[:, : half // 2] + share[:, : half // 2]
    load[:, half // 2 :] = local_rest[...] + share[:, half // 2 :]
    answer = load[...] + slope[...]
    image[...] = answer
    lines = [*signed_sums(answer), *signed_sums(own_wave[...])]
    sums[...] = jnp.concatenate(lines + [jnp.zeros((4, half), F32)], axis=0)


def spread_kernel(*refs, steps, apart):
    arrived, others = refs[1 : steps + 1], refs[steps + 1 : steps + 1 + apart]
    cut_current, image, back, halo, kept, sent = refs[1 + steps + apart :]
    times = image.shape[0]
    slots = steps * CAP
    start = packet_layout(steps, times)[1]
    arrived, stack, sender, _ = unpack(
        refs[0][0] % 2, arrived, others, cut_current, halo.shape[1]
    )
    kept[...], sent[...] = analysed(back, image[...])
    currents = []
    for step in range(1, steps + 1):
        theirs = jnp.concatenate(
            [sender(step ^ block, block) for block in range(1, steps + 1)], axis=0
        )
        gains = arrived[step - 1][:CAP, start : start + slots]
        image_part = arrived[step - 1][CAP : 2 * CAP, start : start + times]
        there = arrived[step - 1][2 * CAP : 3 * CAP, start : start + times]
        currents.append(there * (image_part + dot_split(split(gains), split(theirs))))
    halo[...] = stack(currents)


def second_kernel(
    place,
    halo,
    near_image,
    image,
    back,
    conductances,
    coupling_high,
    coupling_low,
    linear,
    load,
    kept,
    sent,
    current,
):
    times, half = image.shape
    nodes = current.shape[1]
    side = place[0] % 2
    mine, other = half_of(side, half), half_of(1 - side, half)
    for at, field in ((mine, image), (other, near_image)):
        current[:times, at], current[times:, at] = split(conductances[:, at] * field[...])
    load[...] = image[...] * (linear[:, :half] + conductances[:, mine])
    high, low = split(halo[...])
    halo_stacked = jnp.concatenate([high, low], axis=0)
    for lanes in blocks_of(0, half):
        load[:, lanes] += coupled(
            current[:times], current[...], coupling_high, coupling_low, slice(0, nodes), lanes
        ) + coupled(high, halo_stacked, coupling_high, coupling_low, slice(nodes, None), lanes)
    kept[...], sent[...] = analysed(back, load[...])


def sum_kernel(after, *refs):
    total = refs[0][...]
    for value in refs[1:-1]:
        total = total + value[...]
    refs[-1][...] = total


def turned(field, first_pair, half_order):
    count = field.shape[0]
    row = lax.broadcasted_iota(I32, field.shape, 0)
    scaling = (first_pair + row // 2).astype(F32) * (1.0 / half_order)
    above = pltpu.roll(field, count - 1, 0)
    below = pltpu.roll(field, 1, 0)
    return scaling * jnp.where(row % 2 == 0, above, -below)


def combine_kernel(after, place, kept, arrived, *targets):
    half = kept.shape[1]
    rows = targets[0].shape[0]
    side = place[0] % 2
    for index, target in enumerate(targets):
        at = slice(index * rows, (index + 1) * rows)
        target[:, half_of(side, half)] = kept[at]
        target[:, half_of(1 - side, half)] = arrived[at]


def joined(parts):
    return functools.reduce(jnp.add, [part[...] for part in parts])


def guess(cross, squares):
    ratio = cross / jnp.where(squares > 0.0, squares, 1.0)
    return jnp.clip(jnp.where(squares > 0.0, ratio, 0.0), -40.0, 40.0)


def products_kernel(
    place,
    vector,
    load,
    second_load,
    image,
    wave,
    dual,
    dual_slope,
    own_sums,
    far_sums,
    scalars,
    *,
    length,
):
    start, first = wave[...], load[...]
    field, sums = vector[...], own_sums[...] + far_sums[...]
    coeff = guess(scalar_sum(start * image[...]), scalar_sum(start * start))
    rest = image[...] - coeff * start
    change = second_load[...] - coeff * first
    start_sums = [sums[line + 2 : line + 3] for line in (0, 1)]
    rest_sums = [sums[line : line + 1] - coeff * start_sums[line] for line in (0, 1)]
    start_ends, rest_ends, first_ends, change_ends = (
        signed_sums(values) for values in (start, rest, first, change)
    )

    def mixed(values, value_sums, others, other_ends):
        ends = value_sums[0] * other_ends[0] + value_sums[1] * other_ends[1]
        return lane_sums(values * others) * (2.0 / length) - lane_sums(ends) * (
            1.0 / length / length
        )

    found = [
        lane_sums(field * field),
        lane_sums(dual[...] * rest),
        lane_sums(dual[...] * start),
        mixed(rest, rest_sums, rest, rest_ends),
        mixed(rest, rest_sums, start, start_ends) + mixed(start, start_sums, rest, rest_ends),
        mixed(start, start_sums, start, start_ends),
        lane_sums(dual[...] * change - dual_slope[...] * rest),
        lane_sums(dual[...] * first - dual_slope[...] * start),
        mixed(rest, rest_sums, change, change_ends),
        mixed(rest, rest_sums, first, first_ends) + mixed(start, start_sums, change, change_ends),
        mixed(start, start_sums, first, first_ends),
    ]
    device = place[1] * place[3] + place[0]
    lane = lax.broadcasted_iota(I32, scalars.shape, 1)
    column = jnp.concatenate(found + [jnp.zeros((5, LANES), F32)], axis=0)
    column = jnp.sum(column, axis=1, keepdims=True)
    line = lax.broadcasted_iota(I32, column.shape, 0)
    column = jnp.where(line == len(found), coeff, column)
    scalars[...] = jnp.where(lane == device, column, 0.0)


def settle_kernel(place, vector, capacity, *refs, length):
    *parts, answer, slope, skew = refs
    rows = vector.shape[0]
    first_pair = place[0] * (rows // 2)
    answer[...] = joined(parts)
    field, start = answer[...], vector[...]
    slope[...] = capacity[...] * turned(field, first_pair, length // 2)
    start_slope = capacity[...] * turned(start, first_pair, length // 2)
    products = [
        scalar_sum(field * slope[...]),
        scalar_sum(field * start_slope + start * slope[...]),
        scalar_sum(start * start_slope),
        jnp.zeros((5, 1), F32),
    ]
    skew[...] = jnp.broadcast_to(jnp.concatenate(products, axis=0), skew.shape)


def last_kernel(
    gathered,
    vector,
    answer,
    slope,
    skew,
    *refs,
    entries,
    devices,
):
    *parts, basis_two, next_residue = refs
    own = [gathered[line : line + 1, :] for line in range(12)]
    local = own.pop()

    def everywhere(values):
        return jnp.sum(values, axis=1, keepdims=True) / entries

    scale_square = everywhere(own[0]) + EPSILON
    coeff = everywhere(own[1] + local * own[2]) / scale_square
    near = local - coeff
    rest_square = everywhere(own[3] + near * (own[4] + near * own[5]))
    along_one = everywhere(own[6] + near * own[7])
    along_two = everywhere(own[8] + near * (own[9] + near * own[10]))
    turn = skew[0:1, :1] - coeff * (skew[1:2, :1] - coeff * skew[2:3, :1])
    along_two = along_two + turn * (devices / entries)
    scale = jnp.sqrt(scale_square)
    second_norm = jnp.sqrt(jnp.maximum(rest_square, 0.0) / scale_square + EPSILON)
    inverse = 1.0 / (second_norm * scale)
    along_one = along_one * inverse / scale_square
    along_two = along_two * inverse * inverse
    second = (answer[...] - coeff * vector[...]) * inverse
    basis_two[...] = second
    next_residue[...] = (
        (joined(parts) + slope[...] - coeff * answer[...]) * inverse
        - along_one * vector[...]
        - along_two * second
    )


VMEM = pl.BlockSpec(memory_space=pltpu.VMEM)
SMEM = pl.BlockSpec(memory_space=pltpu.SMEM)


HBM = pl.BlockSpec(memory_space=pltpu.HBM)


def run(kernel, name, specs, operands, outs, scratch=(), micros=1, room=12, spaces=None):
    spaces = spaces or [pltpu.VMEM] * len(outs)
    return pl.pallas_call(
        kernel,
        out_shape=[space(shape, dtype) for space, (shape, dtype) in zip(spaces, outs)],
        in_specs=specs,
        out_specs=[pl.BlockSpec(memory_space=space) for space in spaces],
        scratch_shapes=list(scratch),
        compiler_params=pltpu.CompilerParams(vmem_limit_bytes=room * 2**20),
        cost_estimate=pl.CostEstimate(
            flops=0, bytes_accessed=int(micros * 3e6), transcendentals=0
        ),
        name=name,
    )(*operands)


def swap(value, mask):
    count = lax.axis_size("samples")
    return lax.ppermute(value, "samples", [(at, at ^ mask) for at in range(count)])


def trade(value, masks):
    count, parts = lax.axis_size("nodes"), lax.axis_size("samples")
    pairs = [
        (at * parts + which, (at ^ masks[which % len(masks)]) * parts + which)
        for at in range(count)
        for which in range(parts)
    ]
    return lax.ppermute(value, ("nodes", "samples"), pairs)


def add(after, terms):
    (value,) = run(
        sum_kernel,
        "sum",
        [VMEM] * (len(terms) + 1),
        (after, *terms),
        [(terms[0].shape, F32)],
    )
    return value


def exchange(value, axis, after):
    count, stride, terms = lax.axis_size(axis), 1, [value]
    while stride < count:
        if stride > 1:
            value = add(after, terms)
        radix = 4 if count // stride % 4 == 0 else 2
        terms = [value] + [
            lax.ppermute(value, axis, [(at, at ^ (step * stride)) for at in range(count)])
            for step in range(1, radix)
        ]
        stride *= radix
    return terms


def hand_out(after, place, kept, arrived):
    count = lax.axis_size("samples") // 2
    field = ((kept.shape[0] // count, 2 * kept.shape[1]), F32)
    parts = run(
        combine_kernel,
        "combine",
        [VMEM, SMEM] + [VMEM] * 2,
        (after, place, kept, arrived),
        [field] * count,
    )
    return [parts[0]] + [swap(part, 2 * mask) for mask, part in enumerate(parts) if mask]


def shards(
    vector, operating, table, linear, capacity, weights, degree, neighbours, boundary, send_list
):
    rows, nodes = vector.shape
    parts, node_groups = lax.axis_size("samples"), lax.axis_size("nodes")
    length, half, times = rows * parts, nodes // 2, 2 * rows
    entries = float(length * nodes * node_groups)
    steps = node_groups - 1
    slots = steps * CAP
    lanes = -(-slots // LANES) * LANES
    sources, width = nodes + lanes, half + lanes
    forward, back = (jnp.asarray(table) for table in transform_tables(length, parts))
    linear, capacity, degree, table = (
        value.reshape(1, -1) for value in (linear, capacity, degree, table)
    )

    slot_count = weights.shape[0]
    (
        own_vector,
        picked,
        linear_wide,
        capacity_wide,
        capacity,
        table,
        own_operating,
        forward,
        back,
        entry_rows,
        weight_rows,
        place,
    ) = run(
        fetch_kernel,
        "fetch",
        [HBM] * 12,
        tuple(
            pltpu.with_memory_space_constraint(value, pltpu.HBM)
            for value in (vector, neighbours, weights, degree, linear, capacity, send_list)
            + (boundary, table, operating, forward, back)
        ),
        [
            ((rows, nodes), F32),
            ((nodes, lanes), BF16),
            ((1, width), F32),
            ((1, width), F32),
            ((1, nodes), F32),
            (table.shape, F32),
            ((rows, nodes), F32),
            (forward.shape[1:], BF16),
            (back.shape[1:], BF16),
            ((slot_count, width), I32),
            ((slot_count, width), F32),
            ((4,), I32),
        ],
        scratch=[
            pltpu.VMEM((slot_count, nodes), I32),
            pltpu.VMEM((slot_count, nodes), F32),
            pltpu.VMEM((1, nodes), I32),
            pltpu.VMEM((1, nodes), F32),
            pltpu.SMEM(send_list.shape, I32),
            pltpu.SMEM(boundary.shape, I32),
            pltpu.SemaphoreType.DMA((12,)),
        ],
        micros=2,
        spaces=[pltpu.VMEM] * 11 + [pltpu.SMEM],
    )
    coupling_high, coupling_low = run(
        prepare_kernel,
        "prepare",
        [VMEM] * 2,
        (entry_rows, weight_rows),
        [((sources, half), BF16)] * 2,
        micros=6,
    )
    near_operating = swap(operating, 1)
    vectors, bit = [vector], parts // 2
    while bit > 1:
        vectors = vectors + [swap(piece, bit) for piece in vectors]
        bit //= 2
    far = len(vectors) - 1
    if far:
        vectors[1:] = run(
            relay_kernel,
            "relay",
            [VMEM] * (far + 1),
            (coupling_low, *vectors[1:]),
            [((rows, nodes), F32)] * far,
        )
    vectors = vectors + [swap(piece, 1) for piece in vectors]
    vectors[0] = own_vector
    cut_high, cut_low, cut_halo = run(
        prepare_cut_kernel,
        "prepare_cut",
        [VMEM] * 3,
        (vectors[far], entry_rows, weight_rows),
        [((sources, lanes), BF16), ((sources, lanes), BF16), ((lanes, lanes), F32)],
        micros=1,
    )
    (conductances,) = run(
        conductance_kernel,
        "conductance",
        [SMEM] + [VMEM] * 4,
        (place, near_operating, own_operating, table, picked),
        [((times, sources), F32)],
        micros=1,
    )

    wide = ((times, half), F32)
    shared, start = packet_layout(steps, times)
    packet = (
        max(slots if shared else 0, 3 * CAP),
        -(-(start + max(times, slots)) // LANES) * LANES,
    )
    field_high, field_low, wave, current, cut_current, *sent = run(
        functools.partial(wave_kernel, pieces=parts, steps=steps),
        "wave",
        [SMEM] + [VMEM] * (parts + 8),
        (place, *vectors, forward, conductances, picked, cut_high, cut_low)
        + (linear_wide, capacity_wide, cut_halo),
        [
            ((length, sources), BF16),
            ((length, sources), BF16),
            ((times, sources), F32),
            ((2 * times, nodes), BF16),
            ((lanes, times), F32),
        ]
        + [(packet, F32)] * len(packet_steps(steps)),
        scratch=[pltpu.VMEM((length, nodes), BF16)],
        micros=2,
    )
    arrived = [trade(packet, masks) for packet, masks in zip(sent, packet_steps(steps))]
    others = []
    if not shared:
        gathered = lax.all_gather(cut_current, "nodes")
        distance = jnp.arange(node_groups, dtype=I32)
        others = [gathered[lax.axis_index("nodes") ^ distance]]
    local_load, slope, own_wave, dual, dual_slope = run(
        local_kernel,
        "local",
        [VMEM] * 10 + [SMEM],
        (field_high, field_low, forward, wave, current, conductances)
        + (coupling_high, coupling_low, linear_wide, capacity_wide, place),
        [wide] * 5,
        micros=3,
    )
    if steps == 3:
        (traded,) = run(
            relay_kernel, "relay", [VMEM] * 2, (dual, arrived[-1]), [(packet, F32)]
        )
        arrived[-1:] = [traded, swap(traded, 1)]
    (local_rest,) = run(
        local_rest_kernel,
        "local_rest",
        [VMEM] * 4,
        (local_load, current, coupling_high, coupling_low),
        [((times, half // 2), F32)],
    )
    block = ((length // 2, half), F32)
    packets = (place, *arrived, *others, cut_current)
    packet_specs = [SMEM] + [VMEM] * (len(packets) - 1)
    image, load, own_sums = run(
        functools.partial(first_kernel, steps=steps, apart=len(others)),
        "first",
        packet_specs + [VMEM] * 6,
        (*packets, local_load, local_rest, slope, own_wave, coupling_high, coupling_low),
        [wide, wide, ((8, half), F32)],
        micros=1,
    )
    halo, kept, sent = run(
        functools.partial(spread_kernel, steps=steps, apart=len(others)),
        "spread",
        packet_specs + [VMEM] * 2,
        (*packets, image, back),
        [((times, lanes), F32), block, block],
        micros=1,
    )
    near_image = swap(image, 1)
    bit = 2
    while 2 * bit < parts:
        own_sums = own_sums + swap(own_sums, bit)
        bit *= 2
    far_sums = swap(own_sums, bit) if bit < parts else jnp.zeros_like(own_sums)
    arrived = swap(sent, 1)

    second_load, second_kept, second_sent = run(
        second_kernel,
        "second",
        [SMEM] + [VMEM] * 8,
        (place, halo, near_image, image, back, conductances)
        + (coupling_high, coupling_low, linear_wide),
        [wide, block, block],
        scratch=[pltpu.VMEM((2 * times, nodes), BF16)],
        micros=3,
    )
    answer_parts = hand_out(load, place, kept, arrived)
    (second_sent,) = run(
        relay_kernel,
        "relay",
        [VMEM] * 2,
        (far_sums, second_sent),
        [(second_sent.shape, F32)],
    )
    second_arrived = swap(second_sent, 1)
    gathered = -(-node_groups * parts // LANES) * LANES
    (scalars,) = run(
        functools.partial(products_kernel, length=length),
        "products",
        [SMEM] + [VMEM] * 9,
        (place, own_vector, load, second_load, image, own_wave, dual, dual_slope)
        + (own_sums, far_sums),
        [((16, gathered), F32)],
        micros=1,
    )
    second_parts = hand_out(scalars, place, second_kept, second_arrived)
    scalars = add(cut_halo, exchange(scalars, "nodes", cut_halo))
    answer, slope, skew = run(
        functools.partial(settle_kernel, length=length),
        "settle",
        [SMEM] + [VMEM] * (len(answer_parts) + 2),
        (place, own_vector, capacity, *answer_parts),
        [((rows, nodes), F32), ((rows, nodes), F32), ((8, LANES), F32)],
        micros=1,
    )
    scalars = add(skew, exchange(scalars, "samples", cut_halo))
    field = jax.ShapeDtypeStruct((rows, nodes), F32)
    return tuple(
        pl.pallas_call(
            functools.partial(
                last_kernel, entries=entries, devices=float(node_groups * parts)
            ),
            out_shape=[field, field],
            in_specs=[VMEM] * (5 + len(second_parts)),
            out_specs=[VMEM] * 2,
            compiler_params=pltpu.CompilerParams(vmem_limit_bytes=12 * 2**20),
            name="last",
        )(scalars, own_vector, answer, slope, skew, *second_parts)
    )


def solution(mesh):
    return jax.shard_map(
        shards,
        mesh=mesh,
        in_specs=(
            P("samples", ("copies", "nodes")),
            P("samples", ("copies", "nodes")),
            P(),
            P("nodes"),
            P("nodes"),
            P(None, "nodes"),
            P("nodes"),
            P(None, "nodes"),
            P("nodes"),
            P("nodes"),
        ),
        out_specs=(P("samples", ("copies", "nodes")), P("samples", ("copies", "nodes"))),
        check_vma=False,
    )
```

```python
import functools
import math

import jax
import jax.numpy as jnp
import numpy as np
from jax import lax
from jax.experimental import pallas as pl
from jax.experimental.pallas import tpu as pltpu
from jax.sharding import PartitionSpec as P

CAP = 16
EPSILON = 1e-06
LANES = 128
BF16 = jnp.bfloat16
F32 = jnp.float32
I32 = jnp.int32


def spectral_tables(length):
    indices = np.arange(length)
    frequency = np.where(indices == 1, length // 2, indices // 2)
    angles = (indices[:, None] * frequency[None, :] % length) * (2.0 * math.pi / length)
    cosine_column = (indices % 2 == 0) | (indices == 1)
    synthesis = np.where(cosine_column[None, :], np.cos(angles), np.sin(angles))
    factor = np.where(indices < 2, 1.0 / length, 2.0 / length)
    analysis = synthesis.T * factor[:, None]
    turn = np.zeros((length, length))
    for pair in range(length // 2):
        turn[2 * pair, 2 * pair + 1] = pair / (length // 2)
        turn[2 * pair + 1, 2 * pair] = -pair / (length // 2)
    return synthesis, analysis, turn


def thirds(table):
    parts = []
    for _ in range(3):
        parts.append(table.astype(np.float32).astype(BF16))
        table = table - parts[-1].astype(np.float64)
    return np.stack(parts)


def piece_order(count):
    masks, bit = [0], count // 2
    while bit:
        masks = masks + [mask ^ bit for mask in masks]
        bit //= 2
    return masks


def transform_tables(length, parts):
    synthesis, analysis, turn = spectral_tables(length)
    slope, dual_slope = synthesis @ turn, analysis.T @ turn
    rows = length // parts
    forward, back = [], []
    for place in range(parts):
        times = np.arange(place // 2 * 2 * rows, (place // 2 + 1) * 2 * rows)
        block = lambda owner: np.arange(owner * rows, (owner + 1) * rows)
        coefs = np.concatenate([block(place ^ mask) for mask in piece_order(parts)])
        forward.append(
            np.concatenate(
                [
                    synthesis[np.ix_(times, coefs)],
                    slope[np.ix_(times, coefs)],
                    analysis[np.ix_(coefs, times)].T,
                    dual_slope[np.ix_(times, coefs)],
                ]
            )
        )
        sent = np.concatenate(
            [block(place ^ mask ^ side) for side in (0, 1) for mask in range(0, parts, 2)]
        )
        back.append(analysis[np.ix_(sent, times)])
    return (
        np.moveaxis(thirds(np.stack(forward)), 0, 1),
        np.moveaxis(thirds(np.stack(back)), 0, 1),
    )


def split(values):
    high = values.astype(BF16)
    return high, (values - high.astype(F32)).astype(BF16)


def split_three(values):
    high = values.astype(BF16)
    rest = values - high.astype(F32)
    middle = rest.astype(BF16)
    return high, middle, (rest - middle.astype(F32)).astype(BF16)


def dot(first, second):
    return jnp.dot(first, second, preferred_element_type=F32)


def dot_split(first, second):
    (first_high, first_low), (second_high, second_low) = first, second
    rows = first_high.shape[0]
    both = dot(jnp.concatenate([first_high, first_low], axis=0), second_high)
    return both[:rows] + both[rows:] + dot(first_high, second_low)


def dot_three(first, second):
    rows = first[0].shape[0]
    one = dot(jnp.concatenate(first, axis=0), second[0])
    two = dot(jnp.concatenate(first[:2], axis=0), second[1])
    small = one[2 * rows :] + two[rows:] + dot(first[0], second[2])
    return one[:rows] + ((one[rows : 2 * rows] + two[:rows]) + small)


def lane_sums(values):
    rows, lanes = values.shape
    step = 8 if rows % 8 == 0 else rows
    total = functools.reduce(
        jnp.add,
        [
            values[row : row + step, lane : lane + LANES]
            for row in range(0, rows, step)
            for lane in range(0, lanes, LANES)
        ],
    )
    return jnp.sum(total, axis=0, keepdims=True)


def half_of(side, half):
    return pl.ds(pl.multiple_of(side * half, LANES), half)


def scalar_sum(values):
    return jnp.sum(lane_sums(values), axis=1, keepdims=True)


def pick(values, picked):
    high, _ = split(values)
    middle, low = split(values - high.astype(F32))
    rows = values.shape[0]
    found = dot(jnp.concatenate([high, middle, low], axis=0), picked)
    return found[:rows] + (found[rows : 2 * rows] + found[2 * rows :])


def conductance(operating, table):
    points = table.shape[1]
    spread = jnp.concatenate([table, jnp.zeros((1, LANES - points), F32)], axis=1)
    spread = jnp.broadcast_to(spread, (operating.shape[0], LANES))
    pieces = []
    for block in range(operating.shape[1] // LANES):
        scaled = (operating[:, block * LANES : (block + 1) * LANES] + 4.0) * ((points - 1) / 8.0)
        knot = jnp.clip(jnp.floor(scaled), 0.0, points - 2.0)
        weight = scaled - knot
        place = knot.astype(I32)
        left = jnp.take_along_axis(spread, place, axis=1, mode="promise_in_bounds")
        right = jnp.take_along_axis(spread, place + 1, axis=1, mode="promise_in_bounds")
        pieces.append(left + weight * (right - left))
    return jnp.concatenate(pieces, axis=1)


def fetch_kernel(
    vector_in,
    neighbours_in,
    weights_in,
    degree_in,
    linear_in,
    capacity_in,
    send_list_in,
    boundary_in,
    table_in,
    operating_in,
    forward_in,
    back_in,
    vector,
    picked,
    linear,
    capacity,
    capacity_all,
    table,
    operating,
    forward,
    back,
    entry_rows,
    weight_rows,
    place,
    neighbours,
    weights,
    degree,
    linear_all,
    send_list,
    boundary,
    copied,
):
    place[0], place[1] = lax.axis_index("samples"), lax.axis_index("nodes")
    place[2], place[3] = lax.axis_size("nodes"), lax.axis_size("samples")
    slots, nodes = neighbours.shape
    lanes = picked.shape[1]
    half = linear.shape[1] - lanes
    node_groups = send_list.shape[0] // CAP
    side, part = place[0] % 2, place[1]
    copies = [
        pltpu.make_async_copy(source, target, copied.at[index])
        for index, (source, target) in enumerate(
            [
                (vector_in, vector),
                (send_list_in, send_list),
                (boundary_in, boundary),
                (neighbours_in, neighbours),
                (weights_in, weights),
                (degree_in, degree),
                (linear_in, linear_all),
                (capacity_in, capacity_all),
                (table_in, table),
                (operating_in, operating),
                (forward_in.at[place[0]], forward),
                (back_in.at[place[0]], back),
            ]
        )
    ]
    for copy in copies:
        copy.start()
    for copy in copies[1:3]:
        copy.wait()

    lane = lax.broadcasted_iota(I32, (8, lanes), 1)

    def name(slot, found):
        target = part ^ (slot // CAP + 1)
        node = boundary[send_list[target * CAP + slot % CAP]]
        return jnp.where(lane == slot, node, found)

    cut_nodes = lax.fori_loop(
        0, (node_groups - 1) * CAP, name, jnp.full((8, lanes), -1, I32), unroll=8
    )
    hit = lax.broadcasted_iota(I32, (nodes, lanes), 0) == cut_nodes[:1]
    picked[...] = jnp.where(hit, 1.0, 0.0).astype(BF16)

    for copy in copies[3:8]:
        copy.wait()
    mine = half_of(side, half)
    entry = neighbours[...]
    remote = entry - nodes
    distance = part ^ (remote >> 4)
    entry = jnp.where(remote < 0, entry, nodes + (distance - 1) * CAP + (remote & 15))
    live = lax.broadcasted_iota(I32, (slots, nodes), 0) < degree[...]
    neighbours[...] = entry
    weights[...] = jnp.where(live, weights[...], 0.0)
    columns = jnp.concatenate(
        [
            entry.astype(F32),
            weights[...],
            linear_all[...],
            capacity_all[...],
            jnp.zeros((6, nodes), F32),
        ],
        axis=0,
    )
    at_cut = pick(columns, picked[...])
    linear[:, :half] = linear_all[:, mine]
    linear[:, half:] = at_cut[2 * slots : 2 * slots + 1]
    capacity[:, :half] = capacity_all[:, mine]
    capacity[:, half:] = at_cut[2 * slots + 1 : 2 * slots + 2]
    entry_rows[:, :half] = neighbours[:, mine]
    entry_rows[:, half:] = at_cut[:slots].astype(I32)
    weight_rows[:, :half] = weights[:, mine]
    weight_rows[:, half:] = at_cut[slots : 2 * slots]
    entries = [entry_rows[slot : slot + 1, :] for slot in range(slots)]
    gains = [weight_rows[slot : slot + 1, :] for slot in range(slots)]
    for slot in range(slots):
        for later in range(slot + 1, slots):
            same = entries[slot] == entries[later]
            gains[slot] = gains[slot] + jnp.where(same, gains[later], 0.0)
            entries[later] = jnp.where(same, -1, entries[later])
    for slot in range(slots):
        entry_rows[slot : slot + 1, :] = entries[slot]
        weight_rows[slot : slot + 1, :] = gains[slot]
    copies[0].wait()
    for copy in copies[8:]:
        copy.wait()


def build(entry_rows, weight_rows, coupling_high, coupling_low):
    slots, width = entry_rows.shape
    sources = coupling_high.shape[0]
    blocks = sources // CAP
    unroll = max(count for count in range(1, 35) if blocks % count == 0)
    wide = (CAP, LANES)

    def column_block(block, carry):
        at_lanes = pl.ds(pl.multiple_of(block * LANES, LANES), LANES)
        names = [
            jnp.broadcast_to(entry_rows[slot : slot + 1, at_lanes], wide).astype(jnp.int16)
            for slot in range(slots)
        ]
        parts = [
            split(jnp.broadcast_to(weight_rows[slot : slot + 1, at_lanes], wide))
            for slot in range(slots)
        ]

        def source_rows(step, row):
            for inner in range(unroll):
                high = jnp.zeros(wide, BF16)
                low = jnp.zeros(wide, BF16)
                for slot in range(slots):
                    hit = names[slot] == row + jnp.int16(CAP * inner)
                    high = jnp.where(hit, parts[slot][0], high)
                    low = jnp.where(hit, parts[slot][1], low)
                at = pl.ds(pl.multiple_of((step * unroll + inner) * CAP, CAP), CAP)
                coupling_high[at, at_lanes] = high
                coupling_low[at, at_lanes] = low
            return row + jnp.int16(CAP * unroll)

        lax.fori_loop(
            0,
            blocks // unroll,
            source_rows,
            lax.broadcasted_iota(I32, wide, 0).astype(jnp.int16),
        )
        return carry

    lax.fori_loop(0, width // LANES, column_block, 0)


def prepare_kernel(entry_rows, weight_rows, coupling_high, coupling_low):
    half = coupling_high.shape[1]
    build(entry_rows.at[:, :half], weight_rows.at[:, :half], coupling_high, coupling_low)


def prepare_cut_kernel(after, entry_rows, weight_rows, cut_high, cut_low, cut_halo):
    lanes = cut_high.shape[1]
    half = entry_rows.shape[1] - lanes
    build(entry_rows.at[:, half:], weight_rows.at[:, half:], cut_high, cut_low)
    nodes = cut_high.shape[0] - lanes
    cut_halo[...] = jnp.transpose(cut_high[nodes:].astype(F32) + cut_low[nodes:].astype(F32))


def relay_kernel(*refs):
    count = (len(refs) - 1) // 2
    for source, target in zip(refs[1 : 1 + count], refs[1 + count :]):
        target[...] = source[...]


def conductance_kernel(place, near_operating, operating, table, picked, conductances):
    rows, nodes = operating.shape
    side = place[0] % 2
    for at, values in ((side, operating), (1 - side, near_operating)):
        conductances[pl.ds(pl.multiple_of(at * rows, 8), rows), :nodes] = conductance(
            values[...], table[...]
        )
    conductances[:, nodes:] = pick(conductances[:, :nodes], picked[...])


def coupled(high, stacked, coupling_high, coupling_low, sources, lanes):
    rows = high.shape[0]
    both = dot(stacked, coupling_high[sources, lanes])
    return both[:rows] + both[rows:] + dot(high, coupling_low[sources, lanes])


def packet_layout(steps, times):
    shared = steps * CAP <= LANES
    return shared, times if shared else 0


def packet_steps(steps):
    return [(2,), (1, 3)] if steps == 3 else [(step,) for step in range(1, steps + 1)]


def wave_kernel(*refs, pieces, steps):
    vectors = refs[1 : 1 + pieces]
    (
        forward,
        conductances,
        picked,
        coupling_high,
        coupling_low,
        linear,
        capacity,
        cut_halo,
        field_high,
        field_low,
        wave,
        current,
        cut_current,
    ) = refs[1 + pieces : 1 + pieces + 13]
    *sent, field_last = refs[1 + pieces + 13 :]
    side = refs[0][0] % 2
    rows, nodes = vectors[0].shape
    lanes = picked.shape[1]
    times = wave.shape[0]
    half = linear.shape[1] - lanes
    for index in range(pieces):
        at = slice(index * rows, (index + 1) * rows)
        parts = split_three(vectors[index][...])
        field_high[at, :nodes], field_low[at, :nodes], field_last[at, :nodes] = parts
    field_high[:, nodes:] = dot(field_high[:, :nodes], picked[...]).astype(BF16)
    field_low[:, nodes:] = dot(field_low[:, :nodes], picked[...]).astype(BF16)
    field_last[:, nodes:] = dot(field_last[:, :nodes], picked[...]).astype(BF16)
    wave[...] = dot_three(
        [forward[part, :times] for part in range(3)],
        (field_high[...], field_low[...], field_last[...]),
    )
    slope = dot_split(
        (forward[0, times : 2 * times], forward[1, times : 2 * times]),
        (field_high[:, nodes:], field_low[:, nodes:]),
    )
    high, low = split(conductances[:, :nodes] * wave[:, :nodes])
    current[:times] = high
    current[times:] = low
    at_cut = conductances[:, nodes:] * wave[:, nodes:]
    cut_current[...] = jnp.transpose(at_cut)
    image = (
        linear[:, half:] * wave[:, nodes:]
        + at_cut
        + capacity[:, half:] * slope
        + coupled(
            high, current[...], coupling_high, coupling_low, slice(0, nodes), slice(None)
        )
    )
    image = jnp.transpose(image)
    at_cut = jnp.transpose(conductances[:, nodes:])
    slots = steps * CAP
    shared, start = packet_layout(steps, times)
    for target, wanted in zip(sent, packet_steps(steps)):
        target[...] = jnp.zeros(target.shape, F32)
        if shared:
            target[:slots, :times] = cut_current[:slots]
        for row, values, size in ((0, cut_halo, slots), (1, image, times), (2, at_cut, times)):
            blocks = [values[(step - 1) * CAP : step * CAP, :size] for step in wanted]
            block = blocks[0] if len(blocks) == 1 else jnp.where(side == 0, *blocks)
            target[row * CAP : (row + 1) * CAP, start : start + size] = block


def local_kernel(
    field_high,
    field_low,
    forward,
    wave,
    current,
    conductances,
    coupling_high,
    coupling_low,
    linear,
    capacity,
    place,
    load,
    slope,
    own_wave,
    dual,
    dual_slope,
):
    times, half = load.shape
    sources = slice(0, current.shape[1])
    mine = half_of(place[0] % 2, half)
    others = dot_split(
        (forward[0, times:], forward[1, times:]), (field_high[:, mine], field_low[:, mine])
    )
    slope[...] = capacity[:, :half] * others[:times]
    dual[...] = others[times : 2 * times]
    dual_slope[...] = capacity[:, :half] * others[2 * times :]
    own_wave[...] = wave[:, mine]
    load[...] = own_wave[...] * (linear[:, :half] + conductances[:, mine])
    for lanes in blocks_of(0, half // 2):
        load[:, lanes] += coupled(
            current[:times], current[...], coupling_high, coupling_low, sources, lanes
        )


def local_rest_kernel(load, current, coupling_high, coupling_low, rest):
    times, half = load.shape
    sources = slice(0, current.shape[1])
    for lanes, at in zip(blocks_of(half // 2, half), blocks_of(0, half // 2)):
        rest[:, at] = load[:, lanes] + coupled(
            current[:times], current[...], coupling_high, coupling_low, sources, lanes
        )


def blocks_of(start, stop, step=256):
    return [slice(at, at + step) for at in range(start, stop, step)]


def signed_sums(values):
    rows = values.shape[0]
    folded = functools.reduce(jnp.add, [values[row : row + 8] for row in range(0, rows, 8)])
    even = lax.broadcasted_iota(I32, folded.shape, 0) % 2 == 0
    return (
        jnp.sum(folded, axis=0, keepdims=True),
        jnp.sum(jnp.where(even, folded, -folded), axis=0, keepdims=True),
    )


def analysed(back, load):
    spectrum = dot_three([back[part] for part in range(3)], split_three(load))
    middle = spectrum.shape[0] // 2
    return spectrum[:middle], spectrum[middle:]


def unpack(side, arrived, others, cut_current, lanes):
    steps = len(arrived)
    times = cut_current.shape[1]
    if steps == 3:
        both, own, near = (packet[...] for packet in arrived)
        arrived = [
            jnp.where(side == 0, own, near),
            both,
            jnp.where(side == 0, near, own),
        ]
    slots = steps * CAP
    blank = jnp.zeros((lanes - slots, times), F32)

    def stack(blocks):
        return jnp.transpose(jnp.concatenate([*blocks, blank], axis=0))

    def sender(step, block):
        at = slice((block - 1) * CAP, block * CAP)
        if step == 0:
            return cut_current[at]
        return others[0][step, at] if others else arrived[step - 1][at, :times]

    current = stack([sender(step, step) for step in range(1, steps + 1)])
    return arrived, stack, sender, current


def first_kernel(*refs, steps, apart):
    arrived, others = refs[1 : steps + 1], refs[steps + 1 : steps + 1 + apart]
    (
        cut_current,
        local_load,
        local_rest,
        slope,
        own_wave,
        coupling_high,
        coupling_low,
        image,
        load,
        sums,
    ) = refs[1 + steps + apart :]
    half = load.shape[1]
    lanes = -(-steps * CAP // LANES) * LANES
    nodes = coupling_high.shape[0] - lanes
    current = unpack(refs[0][0] % 2, arrived, others, cut_current, lanes)[-1]
    high, low = split(current)
    share = coupled(
        high,
        jnp.concatenate([high, low], axis=0),
        coupling_high,
        coupling_low,
        slice(nodes, None),
        slice(0, half),
    )
    load[:, : half // 2] = local_load[:, : half // 2] + share[:, : half // 2]
    load[:, half // 2 :] = local_rest[...] + share[:, half // 2 :]
    answer = load[...] + slope[...]
    image[...] = answer
    lines = [*signed_sums(answer), *signed_sums(own_wave[...])]
    sums[...] = jnp.concatenate(lines + [jnp.zeros((4, half), F32)], axis=0)


def spread_kernel(*refs, steps, apart):
    arrived, others = refs[1 : steps + 1], refs[steps + 1 : steps + 1 + apart]
    cut_current, image, back, halo, kept, sent = refs[1 + steps + apart :]
    times = image.shape[0]
    slots = steps * CAP
    start = packet_layout(steps, times)[1]
    arrived, stack, sender, _ = unpack(
        refs[0][0] % 2, arrived, others, cut_current, halo.shape[1]
    )
    kept[...], sent[...] = analysed(back, image[...])
    currents = []
    for step in range(1, steps + 1):
        theirs = jnp.concatenate(
            [sender(step ^ block, block) for block in range(1, steps + 1)], axis=0
        )
        gains = arrived[step - 1][:CAP, start : start + slots]
        image_part = arrived[step - 1][CAP : 2 * CAP, start : start + times]
        there = arrived[step - 1][2 * CAP : 3 * CAP, start : start + times]
        currents.append(there * (image_part + dot_split(split(gains), split(theirs))))
    halo[...] = stack(currents)


def second_kernel(
    place,
    halo,
    near_image,
    image,
    back,
    conductances,
    coupling_high,
    coupling_low,
    linear,
    load,
    kept,
    sent,
    current,
):
    times, half = image.shape
    nodes = current.shape[1]
    side = place[0] % 2
    mine, other = half_of(side, half), half_of(1 - side, half)
    for at, field in ((mine, image), (other, near_image)):
        current[:times, at], current[times:, at] = split(conductances[:, at] * field[...])
    load[...] = image[...] * (linear[:, :half] + conductances[:, mine])
    high, low = split(halo[...])
    halo_stacked = jnp.concatenate([high, low], axis=0)
    for lanes in blocks_of(0, half):
        load[:, lanes] += coupled(
            current[:times], current[...], coupling_high, coupling_low, slice(0, nodes), lanes
        ) + coupled(high, halo_stacked, coupling_high, coupling_low, slice(nodes, None), lanes)
    kept[...], sent[...] = analysed(back, load[...])


def sum_kernel(after, *refs):
    total = refs[0][...]
    for value in refs[1:-1]:
        total = total + value[...]
    refs[-1][...] = total


def turned(field, first_pair, half_order):
    count = field.shape[0]
    row = lax.broadcasted_iota(I32, field.shape, 0)
    scaling = (first_pair + row // 2).astype(F32) * (1.0 / half_order)
    above = pltpu.roll(field, count - 1, 0)
    below = pltpu.roll(field, 1, 0)
    return scaling * jnp.where(row % 2 == 0, above, -below)


def combine_kernel(after, place, kept, arrived, *targets):
    half = kept.shape[1]
    rows = targets[0].shape[0]
    side = place[0] % 2
    for index, target in enumerate(targets):
        at = slice(index * rows, (index + 1) * rows)
        target[:, half_of(side, half)] = kept[at]
        target[:, half_of(1 - side, half)] = arrived[at]


def joined(parts):
    return functools.reduce(jnp.add, [part[...] for part in parts])


def guess(cross, squares):
    ratio = cross / jnp.where(squares > 0.0, squares, 1.0)
    return jnp.clip(jnp.where(squares > 0.0, ratio, 0.0), -40.0, 40.0)


def products_kernel(
    place,
    vector,
    load,
    second_load,
    image,
    wave,
    dual,
    dual_slope,
    own_sums,
    far_sums,
    scalars,
    *,
    length,
):
    start, first = wave[...], load[...]
    field, sums = vector[...], own_sums[...] + far_sums[...]
    coeff = guess(scalar_sum(start * image[...]), scalar_sum(start * start))
    rest = image[...] - coeff * start
    change = second_load[...] - coeff * first
    start_sums = [sums[line + 2 : line + 3] for line in (0, 1)]
    rest_sums = [sums[line : line + 1] - coeff * start_sums[line] for line in (0, 1)]
    start_ends, rest_ends, first_ends, change_ends = (
        signed_sums(values) for values in (start, rest, first, change)
    )

    def mixed(values, value_sums, others, other_ends):
        ends = value_sums[0] * other_ends[0] + value_sums[1] * other_ends[1]
        return lane_sums(values * others) * (2.0 / length) - lane_sums(ends) * (
            1.0 / length / length
        )

    found = [
        lane_sums(field * field),
        lane_sums(dual[...] * rest),
        lane_sums(dual[...] * start),
        mixed(rest, rest_sums, rest, rest_ends),
        mixed(rest, rest_sums, start, start_ends) + mixed(start, start_sums, rest, rest_ends),
        mixed(start, start_sums, start, start_ends),
        lane_sums(dual[...] * change - dual_slope[...] * rest),
        lane_sums(dual[...] * first - dual_slope[...] * start),
        mixed(rest, rest_sums, change, change_ends),
        mixed(rest, rest_sums, first, first_ends) + mixed(start, start_sums, change, change_ends),
        mixed(start, start_sums, first, first_ends),
    ]
    device = place[1] * place[3] + place[0]
    lane = lax.broadcasted_iota(I32, scalars.shape, 1)
    column = jnp.concatenate(found + [jnp.zeros((5, LANES), F32)], axis=0)
    column = jnp.sum(column, axis=1, keepdims=True)
    line = lax.broadcasted_iota(I32, column.shape, 0)
    column = jnp.where(line == len(found), coeff, column)
    scalars[...] = jnp.where(lane == device, column, 0.0)


def settle_kernel(place, vector, capacity, *refs, length):
    *parts, answer, slope, skew = refs
    rows = vector.shape[0]
    first_pair = place[0] * (rows // 2)
    answer[...] = joined(parts)
    field, start = answer[...], vector[...]
    slope[...] = capacity[...] * turned(field, first_pair, length // 2)
    start_slope = capacity[...] * turned(start, first_pair, length // 2)
    products = [
        scalar_sum(field * slope[...]),
        scalar_sum(field * start_slope + start * slope[...]),
        scalar_sum(start * start_slope),
        jnp.zeros((5, 1), F32),
    ]
    skew[...] = jnp.broadcast_to(jnp.concatenate(products, axis=0), skew.shape)


def last_kernel(
    gathered,
    vector,
    answer,
    slope,
    skew,
    *refs,
    entries,
    devices,
):
    *parts, basis_two, next_residue = refs
    own = [gathered[line : line + 1, :] for line in range(12)]
    local = own.pop()

    def everywhere(values):
        return jnp.sum(values, axis=1, keepdims=True) / entries

    scale_square = everywhere(own[0]) + EPSILON
    coeff = everywhere(own[1] + local * own[2]) / scale_square
    near = local - coeff
    rest_square = everywhere(own[3] + near * (own[4] + near * own[5]))
    along_one = everywhere(own[6] + near * own[7])
    along_two = everywhere(own[8] + near * (own[9] + near * own[10]))
    turn = skew[0:1, :1] - coeff * (skew[1:2, :1] - coeff * skew[2:3, :1])
    along_two = along_two + turn * (devices / entries)
    scale = jnp.sqrt(scale_square)
    second_norm = jnp.sqrt(jnp.maximum(rest_square, 0.0) / scale_square + EPSILON)
    inverse = 1.0 / (second_norm * scale)
    along_one = along_one * inverse / scale_square
    along_two = along_two * inverse * inverse
    second = (answer[...] - coeff * vector[...]) * inverse
    basis_two[...] = second
    next_residue[...] = (
        (joined(parts) + slope[...] - coeff * answer[...]) * inverse
        - along_one * vector[...]
        - along_two * second
    )


VMEM = pl.BlockSpec(memory_space=pltpu.VMEM)
SMEM = pl.BlockSpec(memory_space=pltpu.SMEM)


HBM = pl.BlockSpec(memory_space=pltpu.HBM)


def run(kernel, name, specs, operands, outs, scratch=(), micros=1, room=12, spaces=None):
    spaces = spaces or [pltpu.VMEM] * len(outs)
    return pl.pallas_call(
        kernel,
        out_shape=[space(shape, dtype) for space, (shape, dtype) in zip(spaces, outs)],
        in_specs=specs,
        out_specs=[pl.BlockSpec(memory_space=space) for space in spaces],
        scratch_shapes=list(scratch),
        compiler_params=pltpu.CompilerParams(vmem_limit_bytes=room * 2**20),
        cost_estimate=pl.CostEstimate(
            flops=0, bytes_accessed=int(micros * 3e6), transcendentals=0
        ),
        name=name,
    )(*operands)


def swap(value, mask):
    count = lax.axis_size("samples")
    return lax.ppermute(value, "samples", [(at, at ^ mask) for at in range(count)])


def trade(value, masks):
    count, parts = lax.axis_size("nodes"), lax.axis_size("samples")
    pairs = [
        (at * parts + which, (at ^ masks[which % len(masks)]) * parts + which)
        for at in range(count)
        for which in range(parts)
    ]
    return lax.ppermute(value, ("nodes", "samples"), pairs)


def add(after, terms):
    (value,) = run(
        sum_kernel,
        "sum",
        [VMEM] * (len(terms) + 1),
        (after, *terms),
        [(terms[0].shape, F32)],
    )
    return value


def exchange(value, axis, after):
    count, stride, terms = lax.axis_size(axis), 1, [value]
    while stride < count:
        if stride > 1:
            value = add(after, terms)
        radix = 4 if count // stride % 4 == 0 else 2
        terms = [value] + [
            lax.ppermute(value, axis, [(at, at ^ (step * stride)) for at in range(count)])
            for step in range(1, radix)
        ]
        stride *= radix
    return terms


def hand_out(after, place, kept, arrived):
    count = lax.axis_size("samples") // 2
    field = ((kept.shape[0] // count, 2 * kept.shape[1]), F32)
    parts = run(
        combine_kernel,
        "combine",
        [VMEM, SMEM] + [VMEM] * 2,
        (after, place, kept, arrived),
        [field] * count,
    )
    return [parts[0]] + [swap(part, 2 * mask) for mask, part in enumerate(parts) if mask]


def shards(
    vector, operating, table, linear, capacity, weights, degree, neighbours, boundary, send_list
):
    rows, nodes = vector.shape
    parts, node_groups = lax.axis_size("samples"), lax.axis_size("nodes")
    length, half, times = rows * parts, nodes // 2, 2 * rows
    entries = float(length * nodes * node_groups)
    steps = node_groups - 1
    slots = steps * CAP
    lanes = -(-slots // LANES) * LANES
    sources, width = nodes + lanes, half + lanes
    forward, back = (jnp.asarray(table) for table in transform_tables(length, parts))
    linear, capacity, degree, table = (
        value.reshape(1, -1) for value in (linear, capacity, degree, table)
    )

    slot_count = weights.shape[0]
    (
        own_vector,
        picked,
        linear_wide,
        capacity_wide,
        capacity,
        table,
        own_operating,
        forward,
        back,
        entry_rows,
        weight_rows,
        place,
    ) = run(
        fetch_kernel,
        "fetch",
        [HBM] * 12,
        tuple(
            pltpu.with_memory_space_constraint(value, pltpu.HBM)
            for value in (vector, neighbours, weights, degree, linear, capacity, send_list)
            + (boundary, table, operating, forward, back)
        ),
        [
            ((rows, nodes), F32),
            ((nodes, lanes), BF16),
            ((1, width), F32),
            ((1, width), F32),
            ((1, nodes), F32),
            (table.shape, F32),
            ((rows, nodes), F32),
            (forward.shape[1:], BF16),
            (back.shape[1:], BF16),
            ((slot_count, width), I32),
            ((slot_count, width), F32),
            ((4,), I32),
        ],
        scratch=[
            pltpu.VMEM((slot_count, nodes), I32),
            pltpu.VMEM((slot_count, nodes), F32),
            pltpu.VMEM((1, nodes), I32),
            pltpu.VMEM((1, nodes), F32),
            pltpu.SMEM(send_list.shape, I32),
            pltpu.SMEM(boundary.shape, I32),
            pltpu.SemaphoreType.DMA((12,)),
        ],
        micros=2,
        spaces=[pltpu.VMEM] * 11 + [pltpu.SMEM],
    )
    coupling_high, coupling_low = run(
        prepare_kernel,
        "prepare",
        [VMEM] * 2,
        (entry_rows, weight_rows),
        [((sources, half), BF16)] * 2,
        micros=6,
    )
    near_operating = swap(operating, 1)
    vectors, bit = [vector], parts // 2
    while bit > 1:
        vectors = vectors + [swap(piece, bit) for piece in vectors]
        bit //= 2
    far = len(vectors) - 1
    if far:
        vectors[1:] = run(
            relay_kernel,
            "relay",
            [VMEM] * (far + 1),
            (coupling_low, *vectors[1:]),
            [((rows, nodes), F32)] * far,
        )
    vectors = vectors + [swap(piece, 1) for piece in vectors]
    vectors[0] = own_vector
    cut_high, cut_low, cut_halo = run(
        prepare_cut_kernel,
        "prepare_cut",
        [VMEM] * 3,
        (vectors[far], entry_rows, weight_rows),
        [((sources, lanes), BF16), ((sources, lanes), BF16), ((lanes, lanes), F32)],
        micros=1,
    )
    (conductances,) = run(
        conductance_kernel,
        "conductance",
        [SMEM] + [VMEM] * 4,
        (place, near_operating, own_operating, table, picked),
        [((times, sources), F32)],
        micros=1,
    )

    wide = ((times, half), F32)
    shared, start = packet_layout(steps, times)
    packet = (
        max(slots if shared else 0, 3 * CAP),
        -(-(start + max(times, slots)) // LANES) * LANES,
    )
    field_high, field_low, wave, current, cut_current, *sent = run(
        functools.partial(wave_kernel, pieces=parts, steps=steps),
        "wave",
        [SMEM] + [VMEM] * (parts + 8),
        (place, *vectors, forward, conductances, picked, cut_high, cut_low)
        + (linear_wide, capacity_wide, cut_halo),
        [
            ((length, sources), BF16),
            ((length, sources), BF16),
            ((times, sources), F32),
            ((2 * times, nodes), BF16),
            ((lanes, times), F32),
        ]
        + [(packet, F32)] * len(packet_steps(steps)),
        scratch=[pltpu.VMEM((length, sources), BF16)],
        micros=2,
    )
    arrived = [trade(packet, masks) for packet, masks in zip(sent, packet_steps(steps))]
    others = []
    if not shared:
        gathered = lax.all_gather(cut_current, "nodes")
        distance = jnp.arange(node_groups, dtype=I32)
        others = [gathered[lax.axis_index("nodes") ^ distance]]
    local_load, slope, own_wave, dual, dual_slope = run(
        local_kernel,
        "local",
        [VMEM] * 10 + [SMEM],
        (field_high, field_low, forward, wave, current, conductances)
        + (coupling_high, coupling_low, linear_wide, capacity_wide, place),
        [wide] * 5,
        micros=3,
    )
    if steps == 3:
        (traded,) = run(
            relay_kernel, "relay", [VMEM] * 2, (dual, arrived[-1]), [(packet, F32)]
        )
        arrived[-1:] = [traded, swap(traded, 1)]
    (local_rest,) = run(
        local_rest_kernel,
        "local_rest",
        [VMEM] * 4,
        (local_load, current, coupling_high, coupling_low),
        [((times, half // 2), F32)],
    )
    block = ((length // 2, half), F32)
    packets = (place, *arrived, *others, cut_current)
    packet_specs = [SMEM] + [VMEM] * (len(packets) - 1)
    image, load, own_sums = run(
        functools.partial(first_kernel, steps=steps, apart=len(others)),
        "first",
        packet_specs + [VMEM] * 6,
        (*packets, local_load, local_rest, slope, own_wave, coupling_high, coupling_low),
        [wide, wide, ((8, half), F32)],
        micros=1,
    )
    halo, kept, sent = run(
        functools.partial(spread_kernel, steps=steps, apart=len(others)),
        "spread",
        packet_specs + [VMEM] * 2,
        (*packets, image, back),
        [((times, lanes), F32), block, block],
        micros=1,
    )
    near_image = swap(image, 1)
    bit = 2
    while 2 * bit < parts:
        own_sums = own_sums + swap(own_sums, bit)
        bit *= 2
    far_sums = swap(own_sums, bit) if bit < parts else jnp.zeros_like(own_sums)
    arrived = swap(sent, 1)

    second_load, second_kept, second_sent = run(
        second_kernel,
        "second",
        [SMEM] + [VMEM] * 8,
        (place, halo, near_image, image, back, conductances)
        + (coupling_high, coupling_low, linear_wide),
        [wide, block, block],
        scratch=[pltpu.VMEM((2 * times, nodes), BF16)],
        micros=3,
    )
    answer_parts = hand_out(load, place, kept, arrived)
    (second_sent,) = run(
        relay_kernel,
        "relay",
        [VMEM] * 2,
        (far_sums, second_sent),
        [(second_sent.shape, F32)],
    )
    second_arrived = swap(second_sent, 1)
    gathered = -(-node_groups * parts // LANES) * LANES
    (scalars,) = run(
        functools.partial(products_kernel, length=length),
        "products",
        [SMEM] + [VMEM] * 9,
        (place, own_vector, load, second_load, image, own_wave, dual, dual_slope)
        + (own_sums, far_sums),
        [((16, gathered), F32)],
        micros=1,
    )
    second_parts = hand_out(answer_parts[0], place, second_kept, second_arrived)
    scalars = add(cut_halo, exchange(scalars, "nodes", cut_halo))
    answer, slope, skew = run(
        functools.partial(settle_kernel, length=length),
        "settle",
        [SMEM] + [VMEM] * (len(answer_parts) + 2),
        (place, own_vector, capacity, *answer_parts),
        [((rows, nodes), F32), ((rows, nodes), F32), ((8, LANES), F32)],
        micros=1,
    )
    scalars = add(skew, exchange(scalars, "samples", cut_halo))
    field = jax.ShapeDtypeStruct((rows, nodes), F32)
    return tuple(
        pl.pallas_call(
            functools.partial(
                last_kernel, entries=entries, devices=float(node_groups * parts)
            ),
            out_shape=[field, field],
            in_specs=[VMEM] * (5 + len(second_parts)),
            out_specs=[VMEM] * 2,
            compiler_params=pltpu.CompilerParams(vmem_limit_bytes=12 * 2**20),
            name="last",
        )(scalars, own_vector, answer, slope, skew, *second_parts)
    )


def solution(mesh):
    return jax.shard_map(
        shards,
        mesh=mesh,
        in_specs=(
            P("samples", ("copies", "nodes")),
            P("samples", ("copies", "nodes")),
            P(),
            P("nodes"),
            P("nodes"),
            P(None, "nodes"),
            P("nodes"),
            P(None, "nodes"),
            P("nodes"),
            P("nodes"),
        ),
        out_specs=(P("samples", ("copies", "nodes")), P("samples", ("copies", "nodes"))),
        check_vma=False,
    )
```
